32 devices in a mesh: seq: 8 (over z, x), frame: 4 (over y, core).
Axes of the slice: x: 2, y: 2, z: 4, core: 2. Of those that a mesh axis runs over, the one named last changes fastest.
Arguments:
- media: bfloat16 [24, 4, 256, 1536], P('seq', 'frame'), may hold values from -6 to 6
- image_counts: int32 [24], P('seq'), may hold values from 0 to 4, as said below
- time_ids: int32 [24, 4], P('seq', 'frame'), may hold values from 0 to 3
- latents: bfloat16 [64, 1536], P(None, ('seq', 'frame')), may hold values from -6 to 6
- time_table: bfloat16 [4, 1536], P(None, ('seq', 'frame')), may hold values from -4 to 4
- media_gain: bfloat16 [1536], P(('seq', 'frame')), may hold values from 0.5 to 1.5
- latent_gain: bfloat16 [1536], P(('seq', 'frame')), may hold values from 0.5 to 1.5
- feed_gain: bfloat16 [1536], P(('seq', 'frame')), may hold values from 0.5 to 1.5
- query_weight: bfloat16 [1536, 1536], P(None, ('seq', 'frame')), may hold values from -0.15625 to 0.15625
- keyval_weight: bfloat16 [1536, 3072], P(None, ('seq', 'frame')), may hold values from -0.15625 to 0.15625
- output_weight: bfloat16 [1536, 1536], P(('seq', 'frame')), may hold values from -3.5 to 3.5
- up_weight: bfloat16 [1536, 6144], P('seq', 'frame'), may hold values from -0.15625 to 0.15625
- down_weight: bfloat16 [6144, 1536], P('frame', 'seq'), may hold values from -0.078125 to 0.078125
- cotangent: float32 [24, 64, 1536], P('seq', 'frame'), may hold values from -6 to 6
Outputs:
- new_latents: float32 [24, 64, 1536], P('seq', 'frame')
- media_grad: float32 [24, 4, 256, 1536], P('seq', 'frame')
- latents_grad: float32 [64, 1536], P(None, ('seq', 'frame'))
- table_grad: float32 [4, 1536], P(None, ('seq', 'frame'))
- media_gain_grad: float32 [1536], P(('seq', 'frame'))
- latent_gain_grad: float32 [1536], P(('seq', 'frame'))
- feed_gain_grad: float32 [1536], P(('seq', 'frame'))
- query_grad: float32 [1536, 1536], P(None, ('seq', 'frame'))
- keyval_grad: float32 [1536, 3072], P(None, ('seq', 'frame'))
- output_grad: float32 [1536, 1536], P(('seq', 'frame'))
- up_grad: float32 [1536, 6144], P('seq', 'frame')
- down_grad: float32 [6144, 1536], P('frame', 'seq')
The draws below stay inside these ranges and needn't reach their ends.
Inputs may be any that keep to these rules, and one draw needn't show every extreme that they name: `image_counts`: in each aligned block of 3 sequences (those of one index of seq) one sequence has 4 images; a sequence with c images uses slots 0 to c - 1.
All inputs are finite; a program needn't handle non-finite values.
Results may differ from the reference program's by a relative error of at most 0.023.
Values may be sent and summed in bfloat16 or wider, within the bound.
No kernel may reach another device: no remote copies, remote signals or barrier semaphores. Data moves between devices by JAX's collectives and lax.ppermute only.
A program may use at most 320 MiB of HBM per device.

```python
import jax
import jax.numpy as jnp
from jax import lax

HEADS = 16
D = 1536
FF = 6144
LAT = 64
PATCH = 256
SEQ_DEV = 3
SEQS = 24
SLOTS = 4
TIMES = 4
N_FRAME = 4


def draw_image_counts(key, part):
    key = jax.random.fold_in(key, 7)
    count_key, pick_key = jax.random.split(key)
    groups = SEQS // SEQ_DEV
    counts = jax.random.randint(count_key, (groups, SEQ_DEV), 0, SLOTS + 1)
    chosen = jax.random.randint(pick_key, (groups, 1), 0, SEQ_DEV)
    filled = jnp.arange(SEQ_DEV, dtype=jnp.int32)[None, :] == chosen
    return jnp.where(filled, SLOTS, counts).reshape(SEQS).astype(jnp.int32)


def with_ends(result, stream_key, smallest, top_value):
    shape = result.shape
    spot = [jax.random.randint(jax.random.fold_in(stream_key, axis), (), 0, shape[axis]) for axis in range(len(shape))]
    result = result.at[tuple(spot)].set(smallest)
    longest = shape.index(max(shape))
    spot[longest] = (spot[longest] + 1) % shape[longest]
    return result.at[tuple(spot)].set(top_value)


def shard_levels(own_key, dims, cuts, low, largest):
    loudness = 1.0
    for position, shards_of in cuts:
        steps = jax.random.uniform(jax.random.fold_in(jax.random.fold_in(own_key, 6), position), (shards_of,), jnp.float32, low / len(cuts), largest / len(cuts))
        loudness = loudness * jnp.repeat(jnp.exp(steps), dims[position] // shards_of).reshape((-1,) + (1,) * (len(dims) - 1 - position))
    return loudness


def scatter_about(stream_key, dims, spread, limit, pieces=(), held_as=jnp.bfloat16):
    factor_of = shard_levels(stream_key, dims, pieces, -0.22, 0.18) if pieces else 1.0
    result = jax.random.normal(stream_key, dims, jnp.float32) * spread * factor_of
    return jnp.minimum(jnp.maximum(result, -limit), limit).astype(held_as)


def setup_inputs(seed: int = 0) -> dict:
    splits = jax.random.split(jax.random.key(seed), 15)
    return {
        "media": scatter_about(splits[0], (SEQS, SLOTS, PATCH, D), 1.0, 6.0, ((0, 8), (1, 4))),
        "image_counts": draw_image_counts(jax.random.fold_in(splits[14], 71), 0),
        "time_ids": with_ends(jax.random.randint(splits[2], (SEQS, SLOTS), 0, TIMES), jax.random.fold_in(splits[2], 1), 0, TIMES - 1).astype(jnp.int32),
        "latents": scatter_about(splits[3], (LAT, D), 1.0, 6.0, ((1, 32),)),
        "time_table": scatter_about(splits[4], (TIMES, D), 0.5, 4.0, ((1, 32),)),
        "media_gain": jnp.clip(1.0 + 0.1 * jax.random.normal(splits[5], (D,), jnp.float32), 0.5, 1.5).astype(jnp.bfloat16),
        "latent_gain": jnp.clip(1.0 + 0.1 * jax.random.normal(splits[6], (D,), jnp.float32), 0.5, 1.5).astype(jnp.bfloat16),
        "feed_gain": jnp.clip(1.0 + 0.1 * jax.random.normal(splits[7], (D,), jnp.float32), 0.5, 1.5).astype(jnp.bfloat16),
        "query_weight": scatter_about(splits[8], (D, D), D ** -0.5, 0.15625, ((1, 32),)),
        "keyval_weight": scatter_about(splits[9], (D, 2 * D), D ** -0.5, 0.15625, ((1, 32),)),
        "output_weight": scatter_about(splits[10], (D, D), (max(1, D // (PATCH * N_FRAME // 2))) ** -0.5, 3.5, ((0, 32),)),
        "up_weight": scatter_about(splits[11], (D, FF), D ** -0.5, 0.15625, ((0, 8), (1, 4))),
        "down_weight": scatter_about(splits[12], (FF, D), FF ** -0.5, 0.078125, ((0, 4), (1, 8))),
        "cotangent": scatter_about(splits[13], (SEQS, LAT, D), 1.0, 6.0, ((0, 8), (1, 4)), jnp.float32),
    }


EPS = 1e-05
NEGATIVE = -1e+30
HIGHEST = lax.Precision.HIGHEST

@jax.custom_vjp
def low(v):
    return lax.optimization_barrier(v.astype(jnp.bfloat16)).astype(jnp.float32)

@jax.custom_vjp
def low_back(v):
    return v

def low_keep(v):
    return (low(v), None)

def low_pass(kept, grad):
    return (grad,)

def back_keep(v):
    return (v, None)

def back_low(kept, grad):
    return (low(grad),)
low.defvjp(low_keep, low_pass)
low_back.defvjp(back_keep, back_low)

def round_both(values):
    return low_back(low(values))

def layer_norm(values):
    center = values - lax.optimization_barrier(jnp.mean(values, -1, keepdims=True))
    return center * lax.rsqrt(lax.optimization_barrier(jnp.mean(center * center, -1, keepdims=True)) + EPS)

def matmul(first_op, second_op):
    return jnp.dot(first_op, second_op, precision=HIGHEST, preferred_element_type=jnp.float32)

def forward(media_float, params, time_ids, slot_valid):
    lat_param, table, gain_media, gain_latent, gain_feed, query_w, keyval_w, output_w, up_w, down_w = params
    model_width = query_w.shape[0]
    head_dim = model_width // HEADS
    factor = head_dim ** (-0.5)
    hidden_latent = low(layer_norm(lat_param) * gain_latent)
    queries = round_both(matmul(hidden_latent, query_w)).reshape(LAT, HEADS, head_dim)
    latent_kv = round_both(matmul(hidden_latent, keyval_w))

    def one_sequence(seq_item):
        media_seq, seq_times, seq_valid = seq_item
        embedded = media_seq + table[seq_times][:, None, :]
        hidden_media = low(layer_norm(embedded) * gain_media)
        media_kv = round_both(matmul(hidden_media.reshape(-1, model_width), keyval_w))
        keyvals = jnp.concatenate([media_kv, latent_kv], 0)
        key_rows = keyvals[:, :model_width].reshape(-1, HEADS, head_dim)
        value_rows = keyvals[:, model_width:].reshape(-1, HEADS, head_dim)
        key_live = jnp.concatenate([jnp.repeat(seq_valid, PATCH), jnp.ones((LAT,), dtype=bool)])
        scores = low_back(jnp.einsum('lhe,khe->hlk', queries, key_rows, precision=HIGHEST) * factor)
        scores = jnp.where(key_live[None, None, :], scores, NEGATIVE)
        weights = low(jax.nn.softmax(scores, -1))
        context = round_both(jnp.einsum('hlk,khe->lhe', weights, value_rows, precision=HIGHEST).reshape(LAT, model_width))
        mixed = lat_param + low_back(matmul(context, output_w))
        hidden_feed = low(layer_norm(mixed) * gain_feed)
        up_pre = low_back(matmul(hidden_feed, up_w))
        hidden_act = low(jax.nn.gelu(up_pre, approximate=False))
        return mixed + low_back(matmul(hidden_act, down_w))
    checked = jax.checkpoint(one_sequence)

    def scan_step(state_carry, seq_item):
        return (state_carry, checked(seq_item))
    unused, result_out = lax.scan(scan_step, None, (media_float, time_ids, slot_valid))
    return result_out

def reference(media, image_counts, time_ids, latents, time_table, media_gain, latent_gain, feed_gain, query_weight, keyval_weight, output_weight, up_weight, down_weight, cotangent):
    params = tuple((item.astype(jnp.float32) for item in (latents, time_table, media_gain, latent_gain, feed_gain, query_weight, keyval_weight, output_weight, up_weight, down_weight)))
    media_float = media.astype(jnp.float32)
    slot_valid = jnp.arange(SLOTS, dtype=jnp.int32)[None, :] < image_counts[:, None]

    def whole_layer(media_in, params_in):
        return forward(media_in, params_in, time_ids, slot_valid)
    result_out, pullback = jax.vjp(whole_layer, media_float, params)
    media_grad, grads = pullback(cotangent.astype(jnp.float32))
    return (result_out, media_grad, grads[0], grads[1], grads[2], grads[3], grads[4], grads[5], grads[6], grads[7], grads[8], grads[9])
```

```python
import jax
import jax.numpy as jnp
from jax import lax
from jax.sharding import PartitionSpec as P

HEADS = 16
EPS = 1e-05
NEGATIVE = -1e30
HIGHEST = lax.Precision.HIGHEST
BF = jnp.bfloat16
F32 = jnp.float32
BOTH = ("seq", "frame")


def normalize(values):
    center = values - jnp.mean(values, -1, keepdims=True)
    scale_inv = lax.rsqrt(jnp.mean(center * center, -1, keepdims=True) + EPS)
    return (center * scale_inv, scale_inv)


def norm_back(grad_hat, normed, scale_inv):
    return scale_inv * (
        grad_hat
        - jnp.mean(grad_hat, -1, keepdims=True)
        - normed * jnp.mean(grad_hat * normed, -1, keepdims=True)
    )


def mm(a, b):
    return jnp.dot(a, b, preferred_element_type=F32)


def mm_tn(a, b):
    return lax.dot_general(a, b, (((0,), (0,)), ((), ())), preferred_element_type=F32)


def mm_nt(a, b):
    return lax.dot_general(a, b, (((1,), (1,)), ((), ())), preferred_element_type=F32)


def ein(spec, a, b):
    return jnp.einsum(spec, a, b, preferred_element_type=F32)


def exact_gelu(values):
    return jax.nn.gelu(values, approximate=False)


class Grid:
    def __init__(self, seq_count, frame_count):
        self.seq, self.frame = seq_count, frame_count
        self.core = 2
        self.side = frame_count // 2
        self.depth = seq_count // self.side
        self.count = seq_count * frame_count

    def split(self, lin):
        seq, frame = lin // self.frame, lin % self.frame
        return seq // self.side, seq % self.side, frame // 2, frame % 2

    def join(self, z, x, y, c):
        return ((z * self.side + x) * self.side + y) * 2 + c

    def send(self, value, move):
        perm = [(i, self.join(*move(*self.split(i)))) for i in range(self.count)]
        return lax.ppermute(value, BOTH, perm)

    def to_core(self, v):
        return self.send(v, lambda z, x, y, c: (z, x, y, 1 - c))

    def to_z(self, v, k):
        return self.send(v, lambda z, x, y, c: (z ^ k, x, y, c))

    def to_a(self, v, k):
        return self.send(v, lambda z, x, y, c: (z, x, y ^ k, c) if c else (z, x ^ k, y, c))

    def to_b(self, v, k):
        return self.send(v, lambda z, x, y, c: (z, x ^ k, y, c) if c else (z, x, y ^ k, c))

    def to_frame(self, v, k):
        def move(z, x, y, c):
            f = (y * 2 + c) ^ k
            return z, x, f // 2, f % 2

        return self.send(v, move)

    def to_seq(self, v, k):
        def move(z, x, y, c):
            s = (z * self.side + x) ^ k
            return s // self.side, s % self.side, y, c

        return self.send(v, move)

    def own(self):
        return lax.axis_index("seq") * self.frame + lax.axis_index("frame")

    def rel_of_abs(self):
        z, x, y, c = self.split(self.own())
        oz, ox, oy, oc = self.split(jnp.arange(self.count, dtype=jnp.int32))
        rz, rx, ry, rc = oz ^ z, ox ^ x, oy ^ y, oc ^ c
        b = jnp.where(oc == 0, ry, rx)
        a = jnp.where(oc == 0, rx, ry)
        return ((rc * self.side + b) * self.side + a) * self.depth + rz

    def abs_of_rel(self):
        z, x, y, c = self.split(self.own())
        r = jnp.arange(self.count, dtype=jnp.int32)
        rz = r % self.depth
        a = r // self.depth % self.side
        b = r // (self.depth * self.side) % self.side
        oc = (r // (self.depth * self.side * self.side)) ^ c
        rx = jnp.where(oc == 0, a, b)
        ry = jnp.where(oc == 0, b, a)
        return self.join(rz ^ z, rx ^ x, ry ^ y, oc)

    def gather(self, w):
        v = jnp.stack([w] + [self.to_z(w, k) for k in range(1, self.depth)])
        v = jnp.stack([v] + [self.to_a(v, k) for k in range(1, self.side)])
        v = jnp.stack([v] + [self.to_b(v, k) for k in range(1, self.side)])
        v = jnp.stack([v, self.to_core(v)])
        return v.reshape((self.count,) + w.shape)

    def scatter(self, v):
        v = v.reshape((2, self.side, self.side, self.depth) + v.shape[1:])
        t = v[0].astype(F32) + self.to_core(v[1].astype(BF)).astype(F32)
        s = t[0]
        for k in range(1, self.side):
            s = s + self.to_b(t[k].astype(BF), k).astype(F32)
        t = s
        s = t[0]
        for k in range(1, self.side):
            s = s + self.to_a(t[k].astype(BF), k).astype(F32)
        t = s
        s = t[0]
        for k in range(1, self.depth):
            s = s + self.to_z(t[k].astype(BF), k).astype(F32)
        return s


def local(
    grid,
    media,
    image_counts,
    time_ids,
    latents,
    time_table,
    media_gain,
    latent_gain,
    feed_gain,
    query_weight,
    keyval_weight,
    output_weight,
    up_weight,
    down_weight,
    cotangent,
):
    width = output_weight.shape[1]
    head_dim = width // HEADS
    factor = head_dim ** (-0.5)
    lat_rows = latents.shape[0]
    times = time_table.shape[0]
    seq_here, patches = media.shape[0], media.shape[2]
    own_rows = lat_rows // grid.frame
    rows = seq_here * own_rows
    part = width // grid.count
    slot = lax.axis_index("frame")
    seq_pos = lax.axis_index("seq")
    first_row = slot * own_rows
    rel_of_abs = grid.rel_of_abs()
    abs_of_rel = grid.abs_of_rel()

    def gather_sorted(w):
        return jnp.take(grid.gather(w), rel_of_abs, axis=0)

    def scatter_sorted(v):
        return grid.scatter(jnp.take(v, abs_of_rel, axis=0))

    pad = (-(lat_rows + times + 3)) % 8
    packed = jnp.concatenate(
        [latents, time_table, media_gain[None], latent_gain[None], feed_gain[None], jnp.zeros((pad, part), BF)]
    )
    small = gather_sorted(packed.T).reshape(width, -1).T.astype(F32)
    lat_float = small[:lat_rows]
    table_all = small[lat_rows : lat_rows + times]
    media_scale, latent_scale, feed_scale = (small[lat_rows + times + i] for i in range(3))

    keyval_all = gather_sorted(keyval_weight.T).reshape(2, HEADS, head_dim, width)
    key_w, value_w = keyval_all[0], keyval_all[1]
    output_all = gather_sorted(output_weight).reshape(HEADS, head_dim, width)

    hid_f = up_weight.shape[1]
    hid = hid_f // grid.seq
    d_part = up_weight.shape[0]
    up_blocks = up_weight.reshape(d_part, grid.seq, hid).transpose(1, 2, 0)
    down_blocks = down_weight.reshape(grid.seq, hid, d_part)
    both_blocks = jnp.stack([up_blocks, down_blocks], 1)
    seq_ids = jnp.arange(grid.seq, dtype=jnp.int32) ^ seq_pos
    rel_blocks = jnp.take(both_blocks, seq_ids, axis=0)
    got = jnp.stack([rel_blocks[0]] + [grid.to_seq(rel_blocks[k], k) for k in range(1, grid.seq)])
    got = jnp.take(got, seq_ids, axis=0)
    got = got.transpose(1, 2, 0, 3).reshape(2, hid, width)
    up_t, down_w = got[0], got[1]

    is_valid = slot < image_counts
    onehot = (time_ids[:, 0][:, None] == jnp.arange(times, dtype=jnp.int32)[None, :]).astype(F32)
    embedding = jnp.dot(onehot, table_all, precision=HIGHEST)
    embedded = media[:, 0].astype(F32) + embedding[:, None, :]
    normed_media, inv_media = normalize(embedded)
    hidden_media = (normed_media * media_scale).astype(BF)

    normed_lat, inv_lat = normalize(lat_float)
    hidden_lat = (normed_lat * latent_scale).astype(BF)
    hidden_own = lax.dynamic_slice_in_dim(hidden_lat, first_row, own_rows, 0)
    query_own = mm_tn(query_weight, hidden_lat.T).astype(BF)
    query_t = gather_sorted(query_own).reshape(HEADS, head_dim, lat_rows)
    folded = (ein("hel,hed->hld", query_t, key_w) * factor).astype(BF).reshape(HEADS * lat_rows, width)

    media_scores = ein("rd,spd->srp", folded, hidden_media)
    media_scores = jnp.where(is_valid[:, None, None], media_scores, NEGATIVE)
    own_scores = mm_nt(folded, hidden_own)
    top = jnp.maximum(jnp.max(media_scores, -1), jnp.max(own_scores, -1))
    media_exp = jnp.exp(media_scores - top[..., None])
    own_exp = jnp.exp(own_scores - top[..., None])
    total = jnp.sum(media_exp, -1) + jnp.sum(own_exp, -1)
    mix = ein("srp,spd->srd", media_exp.astype(BF), hidden_media) + ein("srk,kd->srd", own_exp.astype(BF), hidden_own)
    mix = (mix / total[..., None]).astype(BF).reshape(seq_here, HEADS, lat_rows, width)
    part_context = ein("shld,hed->shle", mix, value_w).astype(BF)
    pieces = part_context.reshape(seq_here, HEADS, grid.frame, own_rows, head_dim).transpose(2, 0, 1, 3, 4)
    frame_ids = jnp.arange(grid.frame, dtype=jnp.int32) ^ slot
    pieces = jnp.take(pieces, frame_ids, axis=0)
    stats = jnp.stack([top, total]).reshape(2, seq_here, HEADS, lat_rows)
    pieces = [pieces[0]] + [grid.to_frame(pieces[k], k) for k in range(1, grid.frame)]
    all_stats = jnp.stack([stats] + [grid.to_frame(stats, k) for k in range(1, grid.frame)])
    top_all = jnp.max(all_stats[:, 0], 0)
    weights = all_stats[:, 1] * jnp.exp(all_stats[:, 0] - top_all)
    total_all = jnp.sum(weights, 0)
    log_total = top_all + jnp.log(total_all)
    own_weights = lax.dynamic_slice_in_dim(weights / total_all, first_row, own_rows, 3)
    context = sum(p.astype(F32) * own_weights[i][..., None] for i, p in enumerate(pieces))
    context_low = context.astype(BF)

    lat_own = lax.dynamic_slice_in_dim(lat_float, first_row, own_rows, 0)
    mixed = lat_own[None] + ein("shle,hed->sld", context_low, output_all)
    mixed = mixed.reshape(rows, width)
    normed_feed, inv_feed = normalize(mixed)
    hidden_feed = (normed_feed * feed_scale).astype(BF)
    grad_out = cotangent.reshape(rows, width)

    feed_rows = grid.gather(hidden_feed).reshape(-1, width)
    grad_rows = grid.gather(grad_out.astype(BF)).reshape(-1, width)
    up_pre = mm_nt(feed_rows, up_t)
    hidden_act = exact_gelu(up_pre).astype(BF)
    grad_act = mm_nt(grad_rows, down_w)
    _, pullback = jax.vjp(exact_gelu, up_pre)
    grad_up = pullback(grad_act)[0].astype(BF)
    grad_feed = grid.scatter(mm(grad_up, up_t).astype(BF).reshape(grid.count, rows, width))
    down_out = grid.scatter(mm(hidden_act, down_w).astype(BF).reshape(grid.count, rows, width))
    up_part = mm_tn(grad_up, feed_rows).astype(BF)
    down_part = mm_tn(hidden_act, grad_rows).astype(BF)
    new_latents = (mixed + down_out).reshape(seq_here, own_rows, width)
    back_blocks = jnp.stack([up_part, down_part]).reshape(2, hid, grid.seq, d_part).transpose(2, 0, 1, 3)
    back_blocks = jnp.take(back_blocks, seq_ids, axis=0)
    back = jnp.stack([back_blocks[0]] + [grid.to_seq(back_blocks[k], k) for k in range(1, grid.seq)])
    back = jnp.take(back, seq_ids, axis=0).astype(F32)
    up_grad = back[:, 0].reshape(hid_f, d_part).T
    down_grad = back[:, 1].reshape(hid_f, d_part)

    feed_gain_part = jnp.sum(grad_feed * normed_feed, 0)
    grad_mixed = grad_out + norm_back(grad_feed * feed_scale, normed_feed, inv_feed)
    grad_mixed_low = grad_mixed.astype(BF)
    mixed_3 = grad_mixed_low.reshape(seq_here, own_rows, width)
    output_part = ein("shle,sld->hed", context_low, mixed_3).astype(BF)
    output_grad = scatter_sorted(output_part.reshape(grid.count, part, width))
    grad_context = ein("sld,hed->shle", mixed_3, output_all).astype(BF)
    row_own = jnp.sum(grad_context.astype(F32) * context, -1)
    got_grad = jnp.stack([grad_context] + [grid.to_frame(grad_context, k) for k in range(1, grid.frame)])
    got_row = jnp.stack([row_own] + [grid.to_frame(row_own, k) for k in range(1, grid.frame)])
    got_grad = jnp.take(got_grad, frame_ids, axis=0)
    got_row = jnp.take(got_row, frame_ids, axis=0)
    grad_all = got_grad.transpose(1, 2, 0, 3, 4).reshape(seq_here, HEADS, lat_rows, head_dim)
    row_term = got_row.transpose(1, 2, 0, 3).reshape(seq_here, HEADS * lat_rows, 1)

    log_rows = log_total.reshape(seq_here, HEADS * lat_rows, 1)
    grad_folded = ein("shle,hed->shld", grad_all, value_w).astype(BF).reshape(seq_here, HEADS * lat_rows, width)
    media_probs = jnp.exp(media_scores - log_rows)
    own_probs = jnp.exp(own_scores - log_rows)
    media_low, own_low = media_probs.astype(BF), own_probs.astype(BF)
    media_ds = (media_probs * (ein("srd,spd->srp", grad_folded, hidden_media) - row_term)).astype(BF)
    own_ds = (own_probs * (ein("srd,kd->srk", grad_folded, hidden_own) - row_term)).astype(BF)
    key_mix = ein("srp,spd->rd", media_ds, hidden_media) + ein("srk,kd->rd", own_ds, hidden_own)
    key_mix = key_mix.astype(BF).reshape(HEADS, lat_rows, width)
    value_mix = ein("srp,spd->srd", media_low, hidden_media) + ein("srk,kd->srd", own_low, hidden_own)
    value_mix = value_mix.astype(BF).reshape(seq_here, HEADS, lat_rows, width)
    value_part = ein("shle,shld->hed", grad_all, value_mix).astype(BF)
    key_part = (ein("hel,hld->hed", query_t, key_mix) * factor).astype(BF)
    query_part = (ein("hld,hed->hel", key_mix, key_w) * factor).astype(BF)
    keyval_part = jnp.concatenate([key_part, value_part]).reshape(grid.count, 2 * part, width)
    keyval_grad = scatter_sorted(keyval_part).T
    query_sum = scatter_sorted(query_part.reshape(grid.count, part, lat_rows)).T.astype(BF)

    grad_hidden = ein("srp,rd->spd", media_ds, folded) + ein("srp,srd->spd", media_low, grad_folded)
    grad_hidden_own = ein("srk,rd->kd", own_ds, folded) + ein("srk,srd->kd", own_low, grad_folded)
    media_gain_part = jnp.sum(grad_hidden * normed_media, (0, 1))
    grad_embedded = norm_back(grad_hidden * media_scale, normed_media, inv_media)
    table_part = jnp.dot(onehot.T, jnp.sum(grad_embedded, 1), precision=HIGHEST)

    query_grad = mm_tn(hidden_lat, query_sum)
    grad_lat = mm_nt(query_sum, query_weight)
    grad_lat = grad_lat + lax.dynamic_update_slice_in_dim(jnp.zeros_like(grad_lat), grad_hidden_own, first_row, 0)
    latent_gain_part = jnp.sum(grad_lat * normed_lat, 0)
    residual = jnp.sum(grad_mixed.reshape(seq_here, own_rows, width), 0)
    latents_part = norm_back(grad_lat * latent_scale, normed_lat, inv_lat)
    latents_part = latents_part + lax.dynamic_update_slice_in_dim(
        jnp.zeros_like(latents_part), residual, first_row, 0
    )
    smalls = jnp.concatenate(
        [
            latents_part,
            table_part,
            media_gain_part[None],
            latent_gain_part[None],
            feed_gain_part[None],
            jnp.zeros((pad, width), F32),
        ]
    ).astype(BF)
    small_sum = scatter_sorted(smalls.T.reshape(grid.count, part, -1)).T
    latents_grad = small_sum[:lat_rows]
    table_grad = small_sum[lat_rows : lat_rows + times]
    media_gain_grad, latent_gain_grad, feed_gain_grad = (small_sum[lat_rows + times + i] for i in range(3))
    return (
        new_latents,
        grad_embedded[:, None],
        latents_grad,
        table_grad,
        media_gain_grad,
        latent_gain_grad,
        feed_gain_grad,
        query_grad,
        keyval_grad,
        output_grad,
        up_grad,
        down_grad,
    )


def solution(mesh):
    grid = Grid(mesh.shape["seq"], mesh.shape["frame"])

    def run(*args):
        return local(grid, *args)

    return jax.shard_map(
        run,
        mesh=mesh,
        in_specs=(
            P("seq", "frame", None, None),
            P("seq"),
            P("seq", "frame"),
            P(None, BOTH),
            P(None, BOTH),
            P(BOTH),
            P(BOTH),
            P(BOTH),
            P(None, BOTH),
            P(None, BOTH),
            P(BOTH, None),
            P("seq", "frame"),
            P("frame", "seq"),
            P("seq", "frame", None),
        ),
        out_specs=(
            P("seq", "frame", None),
            P("seq", "frame", None, None),
            P(None, BOTH),
            P(None, BOTH),
            P(BOTH),
            P(BOTH),
            P(BOTH),
            P(None, BOTH),
            P(None, BOTH),
            P(BOTH, None),
            P("seq", "frame"),
            P("frame", "seq"),
        ),
        check_vma=False,
    )
```

```python
import functools

import jax
import jax.numpy as jnp
from jax import lax
from jax.experimental import pallas as pl
from jax.experimental.pallas import tpu as pltpu
from jax.sharding import PartitionSpec as P

HEADS = 16
EPS = 1e-05
NEGATIVE = -1e30
HIGHEST = lax.Precision.HIGHEST
BF = jnp.bfloat16
F32 = jnp.float32
BOTH = ("seq", "frame")


def normalize(values):
    center = values - jnp.mean(values, -1, keepdims=True)
    scale_inv = lax.rsqrt(jnp.mean(center * center, -1, keepdims=True) + EPS)
    return (center * scale_inv, scale_inv)


def norm_back(grad_hat, normed, scale_inv):
    return scale_inv * (
        grad_hat
        - jnp.mean(grad_hat, -1, keepdims=True)
        - normed * jnp.mean(grad_hat * normed, -1, keepdims=True)
    )


def mm(a, b):
    return jnp.dot(a, b, preferred_element_type=F32)


def mm_tn(a, b):
    return lax.dot_general(a, b, (((0,), (0,)), ((), ())), preferred_element_type=F32)


def mm_nt(a, b):
    return lax.dot_general(a, b, (((1,), (1,)), ((), ())), preferred_element_type=F32)


def ein(spec, a, b):
    return jnp.einsum(spec, a, b, preferred_element_type=F32)


def exact_gelu(values):
    return jax.nn.gelu(values, approximate=False)


def bits(n):
    return n.bit_length() - 1


class Grid:
    def __init__(self, seq_count, frame_count):
        self.seq, self.frame = seq_count, frame_count
        self.side = frame_count // 2
        self.depth = seq_count // self.side
        self.count = seq_count * frame_count

    def split(self, lin):
        side = bits(self.side)
        return lin >> (2 * side + 1), (lin >> (side + 1)) & (self.side - 1), (lin >> 1) & (self.side - 1), lin & 1

    def join(self, z, x, y, c):
        return ((z * self.side + x) * self.side + y) * 2 + c

    def send(self, value, move):
        perm = [(i, self.join(*move(*self.split(i)))) for i in range(self.count)]
        return lax.ppermute(value, BOTH, perm)

    def to_z(self, v, k):
        return self.send(v, lambda z, x, y, c: (z ^ k, x, y, c))

    def to_a(self, v, k):
        return self.send(v, lambda z, x, y, c: (z, x, y ^ k, c) if c else (z, x ^ k, y, c))

    def to_b(self, v, k):
        return self.send(v, lambda z, x, y, c: (z, x ^ k, y, c) if c else (z, x, y ^ k, c))

    def to_x(self, v, k):
        return self.send(v, lambda z, x, y, c: (z, x ^ k, y, c))

    def to_core(self, v):
        return self.send(v, lambda z, x, y, c: (z, x, y, 1 - c))

    def to_frame(self, v, k):
        def move(z, x, y, c):
            f = (y * 2 + c) ^ k
            return z, x, f // 2, f % 2

        return self.send(v, move)

    def own(self):
        return lax.axis_index("seq") * self.frame + lax.axis_index("frame")

    def scatter_core_last(self, v):
        for send, size in ((self.to_z, self.depth), (self.to_b, self.side), (self.to_a, self.side)):
            for k in reversed(self.strides(size)):
                half = v.shape[0] // 2
                v = v[:half].astype(F32) + send(v[half:].astype(BF), k).astype(F32)
        return v[0] + self.to_core(v[1].astype(BF)).astype(F32)

    def strides(self, size):
        return [1 << t for t in reversed(range(bits(size)))]

    def places(self, steps="zabc"):
        z, x, y, c = self.split(self.own())
        oz, ox, oy, oc = self.split(jnp.arange(self.count, dtype=jnp.int32))
        way = oc if steps[-1] == "c" else c
        rx, ry = ox ^ x, oy ^ y
        fields = {
            "z": (oz ^ z, self.depth),
            "a": (jnp.where(way == 0, rx, ry), self.side),
            "b": (jnp.where(way == 0, ry, rx), self.side),
            "c": (oc ^ c, 2),
        }
        place, bit = 0, 0
        for step in steps:
            value, size = fields[step]
            for k in self.strides(size):
                place = place + ((value & k != 0).astype(jnp.int32) << bit)
                bit += 1
        return place

    def owners(self, steps="zabc"):
        order = jnp.arange(self.count, dtype=jnp.int32)
        return jnp.zeros_like(order).at[self.places(steps)].set(order, unique_indices=True)

    def step(self, v, kind, k):
        send = {"z": self.to_z, "a": self.to_a, "b": self.to_b, "c": lambda p, _: self.to_core(p)}[kind]
        return jnp.concatenate([v, send(v, k)])

    def gather(self, v, steps):
        for kind in steps:
            for k in self.strides({"z": self.depth, "c": 2}.get(kind, self.side)):
                v = self.step(v, kind, k)
        return v

    def gather_ab(self, v, *others):
        v = [v]
        for k in self.strides(self.side):
            v = v + [self.to_a(p, k) for p in v]
        for k in self.strides(self.side):
            own = self.to_b(v[0], k)
            v = v + [own] + [self.to_b(after(p, own, others), k) for p in v[1:]]
        return v

    def gather_core(self, v, *others):
        return v + [self.to_core(p) for p in v[:-1]] + [self.to_core(after(v[-1], others))]


class Scatter:
    def __init__(self, grid, send, *others):
        self.grid = grid
        self.size = send.shape[0]
        half = self.size // 2
        send = after(send, others)
        self.high, self.arrays = [grid.to_core(send[half:])], [grid.to_core(send[:half])]

    def keep(self, keep):
        half = self.size // 2
        self.high.append(keep[half:])
        self.arrays.append(keep)

    def sum(self, lo, hi):
        arrays = self.arrays
        if hi > self.arrays[0].shape[0]:
            arrays, lo, hi = self.high, 0, hi - lo
        return sum(p[lo:hi].astype(F32) for p in arrays)

    def step(self, send, size, *others):
        for k in reversed(self.grid.strides(size)):
            half = self.size // 2
            self.arrays.append(send(after(self.sum(half, self.size).astype(BF), others), k))
            self.size = half

    def to_b(self, *others):
        self.step(self.grid.to_b, self.grid.side, *others)

    def to_a(self, *others):
        self.step(self.grid.to_a, self.grid.side, *others)

    def to_z(self, *others):
        self.step(self.grid.to_z, self.grid.depth, *others)

    def last(self):
        return self.arrays[-1]

    def result(self):
        return self.sum(0, 1)[0]


def after(value, *others):
    return lax.optimization_barrier((value, others))[0]


def load_blocks(order_ref, part_refs, store_ref, sem_ref):
    rows = store_ref.shape[1]
    copies = []
    for part in part_refs:
        for k in range(part.shape[0]):
            n = len(copies)
            block = part.at[k] if part.shape[1] == rows else part.at[k, pl.ds(0, rows)]
            copies.append(pltpu.make_async_copy(block, store_ref.at[order_ref[n]], sem_ref.at[n]))
    return copies


def place_copy(place_ref, block, source_ref, keep_ref, send_ref, sem_ref):
    half = keep_ref.shape[0]
    place = place_ref[block]

    @pl.when(place < half)
    def _():
        pltpu.make_async_copy(source_ref, keep_ref.at[place], sem_ref).start()

    @pl.when(place >= half)
    def _():
        pltpu.make_async_copy(source_ref, send_ref.at[place - half], sem_ref).start()


def dot(a, b):
    return lax.dot_general(a, b, (((1,), (0,)), ((), ())), preferred_element_type=F32)


def pieces_of(value):
    high = value.astype(BF).astype(F32)
    middle = (value - high).astype(BF).astype(F32)
    return high, middle, value - high - middle


def whole(shape):
    return pl.BlockSpec(shape, lambda *_: (0,) * len(shape))


SMEM = pl.BlockSpec(memory_space=pltpu.SMEM)
ANYWHERE = pl.BlockSpec(memory_space=pltpu.HBM)
LANES = 128


def params(mib):
    return pltpu.CompilerParams(vmem_limit_bytes=mib * 1024 * 1024)


def cost(flops, moved):
    return pl.CostEstimate(flops=int(flops), bytes_accessed=int(moved), transcendentals=0)


def attend_kernel(sizes, order_ref, valid_ref, query_ref, media_ref, own_ref, *refs):
    heads, group, seqs, lat, factor, part_count = sizes
    parts = refs[:part_count]
    folded_ref, score_ref, own_score_ref, context_ref, weight_ref, mix_ref, sem_ref = refs[part_count:]
    step = pl.program_id(0)
    head_dim = weight_ref.shape[1]

    @pl.when(step == 0)
    def _():
        copies = load_blocks(order_ref, parts, weight_ref, sem_ref)
        for c in copies:
            c.start()
        for c in copies:
            c.wait()

    for j in range(group):
        h = step * group + j
        folded = mm_tn(query_ref[h], weight_ref[h]) * factor
        folded_ref[j * lat : (j + 1) * lat, :] = folded.astype(BF)
    queries = folded_ref[...]
    own = own_ref[...]
    own_scores = mm_nt(queries, own)
    own_score_ref[...] = own_scores
    own_top = jnp.max(own_scores, -1, keepdims=True)
    lanes = lax.broadcasted_iota(jnp.int32, (group * lat, LANES), 1)
    for s in range(seqs):
        media = media_ref[s]
        scores = mm_nt(queries, media)
        scores = jnp.where(valid_ref[s] > 0, scores, NEGATIVE)
        score_ref[s] = scores
        top = jnp.maximum(jnp.max(scores, -1, keepdims=True), own_top)
        media_exp = jnp.exp(scores - top)
        own_exp = jnp.exp(own_scores - top)
        total = jnp.sum(media_exp, -1, keepdims=True) + jnp.sum(own_exp, -1, keepdims=True)
        mix = dot(media_exp.astype(BF), media) + dot(own_exp.astype(BF), own)
        mix = (mix * (1.0 / total)).astype(BF)
        stats = jnp.zeros(lanes.shape, F32)
        for i, piece in enumerate(pieces_of(top) + pieces_of(total)):
            stats = jnp.where(lanes == head_dim + i, piece, stats)
        for j in range(group):
            mix_ref[j, s * lat : (s + 1) * lat, :] = mix[j * lat : (j + 1) * lat, :]
            context_ref[j, s * lat : (s + 1) * lat, head_dim:] = stats[j * lat : (j + 1) * lat, head_dim:]
    for j in range(group):
        h = step * group + j
        context_ref[j, :, :head_dim] = mm_nt(mix_ref[j], weight_ref[heads + h])


def attend(order, valid, query_t, hidden_media, hidden_own, parts, factor):
    heads, head_dim, lat = query_t.shape
    seqs, patches, width = hidden_media.shape
    group = 4
    own = hidden_own.shape[0]
    rows = group * lat
    return pl.pallas_call(
        functools.partial(attend_kernel, (heads, group, seqs, lat, factor, len(parts))),
        grid=(heads // group,),
        in_specs=[SMEM, SMEM, whole(query_t.shape), whole(hidden_media.shape), whole(hidden_own.shape)]
        + [ANYWHERE] * len(parts),
        out_specs=[
            pl.BlockSpec((rows, width), lambda i: (i, 0)),
            pl.BlockSpec((seqs, rows, patches), lambda i: (0, i, 0)),
            pl.BlockSpec((rows, own), lambda i: (i, 0)),
            pl.BlockSpec((group, seqs * lat, LANES), lambda i: (i, 0, 0)),
        ],
        out_shape=[
            jax.ShapeDtypeStruct((heads * lat, width), BF),
            jax.ShapeDtypeStruct((seqs, heads * lat, patches), F32),
            jax.ShapeDtypeStruct((heads * lat, own), F32),
            jax.ShapeDtypeStruct((heads, seqs * lat, LANES), F32),
        ],
        scratch_shapes=[
            pltpu.VMEM((2 * heads, head_dim, width), BF),
            pltpu.VMEM((group, seqs * lat, width), BF),
            pltpu.SemaphoreType.DMA((2 * heads,)),
        ],
        compiler_params=params(56),
        cost_estimate=cost(15e9, 25e6),
        name="attend",
    )(order, valid, query_t, hidden_media, hidden_own, *parts)


def mixer_kernel(sizes, order_ref, latent_ref, gain_ref, *refs):
    heads, head_dim, seqs, piece_count, part_count = sizes
    pieces = refs[:piece_count]
    parts = refs[piece_count : piece_count + part_count]
    mixed_ref, normed_ref, hidden_ref, context_ref, low_ref, weight_ref, sem_ref = refs[piece_count + part_count :]
    copies = load_blocks(order_ref, parts, weight_ref, sem_ref)
    for c in copies:
        c.start()
    values = [p[...].astype(F32) for p in pieces]
    at = head_dim
    tops = [v[..., at : at + 1] + v[..., at + 1 : at + 2] + v[..., at + 2 : at + 3] for v in values]
    totals = [v[..., at + 3 : at + 4] + v[..., at + 4 : at + 5] + v[..., at + 5 : at + 6] for v in values]
    top = functools.reduce(jnp.maximum, tops)
    shares = [t * jnp.exp(p - top) for t, p in zip(totals, tops)]
    total = functools.reduce(lambda p, q: p + q, shares)
    context = functools.reduce(lambda p, q: p + q, [v * (w / total) for v, w in zip(values, shares)])
    lanes = lax.broadcasted_iota(jnp.int32, context.shape, 2)
    context_ref[...] = jnp.where(lanes == head_dim, top + jnp.log(total), context)
    for h in range(heads):
        low_ref[:, h * head_dim : (h + 1) * head_dim] = context[h, :, :head_dim].astype(BF)
    for c in copies:
        c.wait()
    weight = weight_ref[...].reshape(heads * head_dim, -1)
    mixed = jnp.concatenate([latent_ref[...]] * seqs) + dot(low_ref[...], weight)
    mixed_ref[...] = mixed
    center = mixed - jnp.mean(mixed, -1, keepdims=True)
    normed = center * lax.rsqrt(jnp.mean(center * center, -1, keepdims=True) + EPS)
    normed_ref[...] = normed
    hidden_ref[...] = (normed * gain_ref[...]).astype(BF)


def mixer(order, latent_own, gain, pieces, parts, head_dim):
    heads, rows, _ = pieces[0].shape
    own_rows, width = latent_own.shape
    count = sum(p.shape[0] for p in parts)
    block = heads * head_dim // count
    sizes = (heads, head_dim, rows // own_rows, len(pieces), len(parts))
    return pl.pallas_call(
        functools.partial(mixer_kernel, sizes),
        in_specs=[SMEM, whole(latent_own.shape), whole(gain.shape)]
        + [whole(p.shape) for p in pieces]
        + [ANYWHERE] * len(parts),
        out_specs=[whole((rows, width))] * 3 + [whole((heads, rows, LANES)), whole((rows, heads * head_dim))],
        out_shape=[
            jax.ShapeDtypeStruct((rows, width), F32),
            jax.ShapeDtypeStruct((rows, width), F32),
            jax.ShapeDtypeStruct((rows, width), BF),
            jax.ShapeDtypeStruct((heads, rows, LANES), F32),
            jax.ShapeDtypeStruct((rows, heads * head_dim), BF),
        ],
        scratch_shapes=[pltpu.VMEM((count, block, width), BF), pltpu.SemaphoreType.DMA((count,))],
        compiler_params=params(32),
        cost_estimate=cost(2e9, 8e6),
        name="mixer",
    )(order, latent_own, gain, *pieces, *parts)


def unmix_kernel(sizes, order_ref, grad_feed_ref, grad_out_ref, mixed_ref, normed_ref, gain_ref, context_ref, *refs):
    heads, head_dim, seqs, part_count = sizes
    parts = refs[:part_count]
    message_ref, grad_mixed_ref, low_ref, gain_grad_ref, residual_ref, weight_ref, sem_ref = refs[part_count:]
    copies = load_blocks(order_ref, parts, weight_ref, sem_ref)
    for c in copies:
        c.start()
    mixed = mixed_ref[...]
    center = mixed - jnp.mean(mixed, -1, keepdims=True)
    scale_inv = lax.rsqrt(jnp.mean(center * center, -1, keepdims=True) + EPS)
    normed = normed_ref[...]
    grad_feed = grad_feed_ref[...]
    gain_grad_ref[...] = jnp.sum(grad_feed * normed, 0, keepdims=True)
    grad_mixed = grad_out_ref[...] + norm_back(grad_feed * gain_ref[...], normed, scale_inv)
    grad_mixed_ref[...] = grad_mixed
    own = residual_ref.shape[0]
    residual_ref[...] = sum(grad_mixed[s * own : (s + 1) * own] for s in range(seqs))
    low = grad_mixed.astype(BF)
    low_ref[...] = low
    for c in copies:
        c.wait()
    grads = mm_nt(low, weight_ref[...].reshape(heads * head_dim, -1)).astype(BF)
    lanes = lax.broadcasted_iota(jnp.int32, (low.shape[0], LANES), 1)
    for h in range(heads):
        grad = grads[:, h * head_dim : (h + 1) * head_dim]
        context = context_ref[h]
        row = jnp.sum(grad.astype(F32) * context[:, :head_dim], -1, keepdims=True)
        log_total = context[:, head_dim : head_dim + 1]
        message = jnp.zeros(lanes.shape, F32)
        for i, piece in enumerate(pieces_of(row) + pieces_of(log_total)):
            message = jnp.where(lanes == head_dim + i, piece, message)
        message_ref[h] = message.astype(BF)
        message_ref[h, :, :head_dim] = grad


def unmix(order, grad_feed, grad_out, mixed, normed, gain, context, parts, head_dim, own_rows):
    heads, rows, _ = context.shape
    width = mixed.shape[1]
    count = sum(p.shape[0] for p in parts)
    block = heads * head_dim // count
    sizes = (heads, head_dim, rows // own_rows, len(parts))
    arrays = (grad_feed, grad_out, mixed, normed, gain, context)
    shapes = [((heads, rows, LANES), BF), ((rows, width), F32), ((rows, width), BF), ((1, width), F32), ((own_rows, width), F32)]
    return pl.pallas_call(
        functools.partial(unmix_kernel, sizes),
        in_specs=[SMEM] + [whole(a.shape) for a in arrays] + [ANYWHERE] * len(parts),
        out_specs=[whole(shape) for shape, _ in shapes],
        out_shape=[jax.ShapeDtypeStruct(*item) for item in shapes],
        scratch_shapes=[pltpu.VMEM((count, block, width), BF), pltpu.SemaphoreType.DMA((count,))],
        compiler_params=params(32),
        cost_estimate=cost(2e9, 8e6),
        name="unmix",
    )(order, *arrays, *parts)


def output_part_kernel(groups, place_ref, context_ref, low_ref, *refs):
    keep_ref, send_ref, out_ref, sem_ref = refs[-4:]
    low = low_ref[...]
    per = out_ref.shape[0] // groups
    part = context_ref.shape[1] // groups
    rows = out_ref.shape[1]
    last = pl.ds(keep_ref.shape[1] - rows, rows)
    keep_rows, send_rows = keep_ref.at[:, last], send_ref.at[:, last]
    for g in range(groups):
        value = mm_tn(context_ref[:, g * part : (g + 1) * part], low).astype(BF)
        out_ref[g * per : (g + 1) * per] = value.reshape((per,) + out_ref.shape[1:])
        for i in range(g * per, (g + 1) * per):
            place_copy(place_ref, i, out_ref.at[i], keep_rows, send_rows, sem_ref.at[i])
    for i in range(out_ref.shape[0]):
        pltpu.make_async_copy(out_ref.at[i], keep_rows.at[0], sem_ref.at[i]).wait()


def output_part_of(place, context, low, *halves):
    width = low.shape[1]
    count = place.shape[0]
    block = context.shape[1] // count
    shapes = [h.shape for h in halves] or [(count // 2, block, width)] * 2
    return pl.pallas_call(
        functools.partial(output_part_kernel, 4),
        in_specs=[SMEM, whole(context.shape), whole(low.shape)] + [ANYWHERE] * len(halves),
        out_specs=[ANYWHERE, ANYWHERE],
        out_shape=[jax.ShapeDtypeStruct(shape, BF) for shape in shapes],
        input_output_aliases={3: 0, 4: 1} if halves else {},
        scratch_shapes=[pltpu.VMEM((count, block, width), BF), pltpu.SemaphoreType.DMA((count,))],
        compiler_params=params(32),
        cost_estimate=cost(2e9, 8e6),
        name="output_part",
    )(place, context, low, *halves)


def unpack_feed_kernel(got_ref, up_ref, down_ref):
    part = got_ref.shape[-1] // 2
    for s in range(got_ref.shape[0]):
        up_ref[:, s * part : (s + 1) * part] = got_ref[s, :, :part]
        down_ref[:, s * part : (s + 1) * part] = got_ref[s, :, part:]


def unpack_feed(got):
    count, hid, part = got.shape
    out = (hid, count * part // 2)
    return pl.pallas_call(
        unpack_feed_kernel,
        in_specs=[whole(got.shape)],
        out_specs=[whole(out)] * 2,
        out_shape=[jax.ShapeDtypeStruct(out, BF)] * 2,
        cost_estimate=cost(0, 3e6),
        name="unpack_feed",
    )(got)


def pack_back_kernel(far_up_ref, far_down_ref, near_up_ref, near_down_ref, out_ref):
    part = out_ref.shape[-1] // 2
    for s in range(out_ref.shape[0]):
        at = slice(s * part, (s + 1) * part)
        out_ref[s, :, :part] = (far_up_ref[:, at] + near_up_ref[:, at]).astype(BF)
        out_ref[s, :, part:] = (far_down_ref[:, at] + near_down_ref[:, at]).astype(BF)


def pack_back(count, *grads):
    hid, width = grads[0].shape
    out = (count, hid, 2 * width // count)
    return pl.pallas_call(
        pack_back_kernel,
        in_specs=[whole(g.shape) for g in grads],
        out_specs=whole(out),
        out_shape=jax.ShapeDtypeStruct(out, BF),
        cost_estimate=cost(0, 6e6),
        name="pack_back",
    )(*grads)


def unpack_back_kernel(got_ref, up_ref, down_ref):
    hid, part = got_ref.shape[1], got_ref.shape[2] // 2
    for s in range(got_ref.shape[0]):
        up_ref[s * hid : (s + 1) * hid, :] = got_ref[s, :, :part].astype(F32)
        down_ref[s * hid : (s + 1) * hid, :] = got_ref[s, :, part:].astype(F32)


def unpack_back(got):
    count, hid, part = got.shape
    out = (count * hid, part // 2)
    return pl.pallas_call(
        unpack_back_kernel,
        in_specs=[whole(got.shape)],
        out_specs=[whole(out)] * 2,
        out_shape=[jax.ShapeDtypeStruct(out, F32)] * 2,
        cost_estimate=cost(0, 5e6),
        name="unpack_back",
    )(got)


ROOT_HALF = 0.5**0.5
DENSITY = 1 / (2 * 3.141592653589793) ** 0.5


def loads(parts, rows, store_ref, sem_ref):
    out, n = [], 0
    for part in parts:
        skip = part.shape[1] - rows
        copies = []
        for k in range(part.shape[0]):
            block = part.at[k, pl.ds(skip, rows)] if skip else part.at[k]
            copies.append(pltpu.make_async_copy(block, store_ref.at[n], sem_ref.at[n]))
            n += 1
        out.append(copies)
    return out


def start(copies):
    for c in copies:
        c.start()


def wait(copies):
    for c in copies:
        c.wait()


def feed_kernel(part_count, up_ref, down_ref, *refs):
    feed, grad = refs[:part_count], refs[part_count : 2 * part_count]
    act_ref, grad_up_ref, out_ref, feed_st, grad_st, out_st, feed_sem, grad_sem, out_sem = refs[2 * part_count :]
    n, per, width = feed[0].shape
    chunk = n * per
    feeds, grads = loads(feed, per, feed_st, feed_sem), loads(grad, per, grad_st, grad_sem)
    for i in range(part_count):
        start(feeds[i])
        start(grads[i])
    up, down = up_ref[...], down_ref[...]
    outs = []
    for i in range(part_count):
        at = slice(i * n, (i + 1) * n)
        wait(feeds[i])
        pre = mm_nt(feed_st[at].reshape(chunk, width), up)
        wait(grads[i])
        grad_act = mm_nt(grad_st[at].reshape(chunk, width), down)
        cdf = 0.5 * (1.0 + lax.erf(pre * ROOT_HALF))
        slope = cdf + pre * (jnp.exp(-0.5 * pre * pre) * DENSITY)
        act_ref[i * chunk : (i + 1) * chunk, :] = (pre * cdf).astype(BF)
        grad_up = (grad_act * slope).astype(BF)
        grad_up_ref[i * chunk : (i + 1) * chunk, :] = grad_up
        out_st[at] = dot(grad_up, up).astype(BF).reshape(n, per, width)
        outs.append(pltpu.make_async_copy(out_st.at[pl.ds(i * n, n)], out_ref.at[pl.ds(i * n, n)], out_sem.at[i]))
        outs[i].start()
    wait(outs)


def feed(up, down, feed_parts, grad_parts):
    hid, width = up.shape
    count = len(feed_parts)
    n, per, _ = feed_parts[0].shape
    rows = count * n * per
    store = pltpu.VMEM((count * n, per, width), BF)
    sems = pltpu.SemaphoreType.DMA((count * n,))
    return pl.pallas_call(
        functools.partial(feed_kernel, count),
        in_specs=[whole(up.shape), whole(down.shape)] + [ANYWHERE] * (2 * count),
        out_specs=[whole((rows, hid))] * 2 + [ANYWHERE],
        out_shape=[jax.ShapeDtypeStruct((rows, hid), BF)] * 2 + [jax.ShapeDtypeStruct((count * n, per, width), BF)],
        scratch_shapes=[store] * 3 + [sems] * 3,
        compiler_params=params(48),
        cost_estimate=cost(5e9, 8e6),
        name="feed",
    )(up, down, *feed_parts, *grad_parts)


def feed_rest_kernel(part_count, down_ref, act_ref, grad_up_ref, *refs):
    feed, grad = refs[:part_count], refs[part_count : 2 * part_count]
    up_grad_ref, down_grad_ref, out_ref, feed_st, grad_st, out_st, feed_sem, grad_sem, out_sem = refs[2 * part_count :]
    n, per, width = feed[0].shape
    chunk = n * per
    feeds, grads = loads(feed, per, feed_st, feed_sem), loads(grad, per, grad_st, grad_sem)
    for i in range(part_count):
        start(feeds[i])
        start(grads[i])
    down = down_ref[...]
    first = pl.ds(0, per)
    outs = []
    for i in range(part_count):
        at = slice(i * n, (i + 1) * n)
        act = act_ref[i * chunk : (i + 1) * chunk, :]
        out_st[at] = dot(act, down).astype(BF).reshape(n, per, width)
        outs.append(pltpu.make_async_copy(out_st.at[pl.ds(i * n, n)], out_ref.at[pl.ds(i * n, n), first], out_sem.at[i]))
        outs[i].start()
    for i in range(part_count):
        wait(feeds[i])
        wait(grads[i])
    up_grad_ref[...] = mm_tn(grad_up_ref[...], feed_st[...].reshape(part_count * chunk, width))
    down_grad_ref[...] = mm_tn(act_ref[...], grad_st[...].reshape(part_count * chunk, width))
    wait(outs)


def feed_rest(down, act, grad_up, feed_parts, grad_parts, spare):
    hid, width = down.shape
    count = len(feed_parts)
    n, per, _ = feed_parts[0].shape
    store = pltpu.VMEM((count * n, per, width), BF)
    sems = pltpu.SemaphoreType.DMA((count * n,))
    return pl.pallas_call(
        functools.partial(feed_rest_kernel, count),
        in_specs=[whole(down.shape), whole(act.shape), whole(grad_up.shape)] + [ANYWHERE] * (2 * count),
        out_specs=[whole((hid, width))] * 2 + [ANYWHERE],
        out_shape=[jax.ShapeDtypeStruct((hid, width), F32)] * 2
        + [jax.ShapeDtypeStruct((count * n, per + spare, width), BF)],
        scratch_shapes=[store] * 3 + [sems] * 3,
        compiler_params=params(48),
        cost_estimate=cost(5e9, 8e6),
        name="feed_rest",
    )(down, act, grad_up, *feed_parts, *grad_parts)


def attend_back_kernel(sizes, order_ref, place_ref, slot_ref, query_ref, media_ref, own_ref, *refs):
    heads, group, seqs, lat, factor, piece_count, part_count, first, count = sizes
    pieces = refs[:piece_count]
    folded_ref, score_ref, own_score_ref = refs[piece_count : piece_count + 3]
    parts = refs[piece_count + 3 : piece_count + 3 + part_count]
    refs = refs[piece_count + 3 + part_count :]
    (
        keep_ref,
        send_ref,
        query_part_ref,
        grad_media_ref,
        grad_own_ref,
        weight_ref,
        mix_ref,
        gp_ref,
        grad_ref,
        out_ref,
        key_mix_ref,
        sem_ref,
        out_sem_ref,
    ) = refs[-13:]
    step = pl.program_id(0)
    head_dim = weight_ref.shape[1]
    own_rows = own_ref.shape[0]

    def out_wait():
        for slot in range(2 * group):
            pltpu.make_async_copy(out_ref.at[slot], keep_ref.at[0], out_sem_ref.at[slot]).wait()

    @pl.when(step == 0)
    def _():
        loads_here = []
        for part in parts:
            for k in range(part.shape[0]):
                n = len(loads_here)
                block = order_ref[n]
                head = block & (heads - 1)
                here = (head >= first) & (head < first + count)
                to = jnp.where(here, head - first + jnp.where(block >= heads, count, 0), 0)
                loads_here.append((here, pltpu.make_async_copy(part.at[k], weight_ref.at[to], sem_ref.at[n])))
        for here, c in loads_here:
            pl.when(here)(c.start)
        grad_media_ref[...] = jnp.zeros_like(grad_media_ref)
        grad_own_ref[...] = jnp.zeros_like(grad_own_ref)
        query_part_ref[...] = jnp.zeros_like(query_part_ref)
        for here, c in loads_here:
            pl.when(here)(c.wait)

    columns = []
    for j in range(group):
        h = step * group + j
        for s in range(seqs):
            for k in range(piece_count):
                at = s * lat + k * own_rows
                grad_ref[j, at : at + own_rows, :] = pieces[k][first + h, s * own_rows : (s + 1) * own_rows, :]
        message = grad_ref[j].astype(F32)
        column = [message[:, head_dim + i : head_dim + i + 1] for i in range(6)]
        columns.append((column[0] + column[1] + column[2], column[3] + column[4] + column[5]))
        lifted = dot(grad_ref[j, :, :head_dim], weight_ref[count + h]).astype(BF)
        for s in range(seqs):
            gp_ref[s, j * lat : (j + 1) * lat, :] = lifted[s * lat : (s + 1) * lat, :]
    queries = folded_ref[...]
    own = own_ref[...]
    own_scores = own_score_ref[...]
    key_mix = jnp.zeros(queries.shape, F32)
    for s in range(seqs):
        media = media_ref[s]
        lifted = gp_ref[s]
        row_term, log_total = (
            jnp.concatenate([columns[j][i][s * lat : (s + 1) * lat] for j in range(group)]) for i in range(2)
        )
        probs = jnp.exp(score_ref[s] - log_total)
        own_probs = jnp.exp(own_scores - log_total)
        ds = (probs * (mm_nt(lifted, media) - row_term)).astype(BF)
        own_ds = (own_probs * (mm_nt(lifted, own) - row_term)).astype(BF)
        probs, own_probs = probs.astype(BF), own_probs.astype(BF)
        key_mix = key_mix + dot(ds, media) + dot(own_ds, own)
        mix = (dot(probs, media) + dot(own_probs, own)).astype(BF)
        for j in range(group):
            mix_ref[j, s * lat : (s + 1) * lat, :] = mix[j * lat : (j + 1) * lat, :]
        grad_media_ref[s] += mm_tn(ds, queries) + mm_tn(probs, lifted)
        grad_own_ref[...] += mm_tn(own_ds, queries) + mm_tn(own_probs, lifted)
    key_mix_ref[...] = (key_mix * factor).astype(BF)
    per = query_part_ref.shape[0] // heads
    pl.when(step > 0)(out_wait)
    for j in range(group):
        h = step * group + j
        mixed = key_mix_ref[j * lat : (j + 1) * lat, :]
        sorted_rows = [
            key_mix_ref[pl.ds(pl.multiple_of(j * lat + (k ^ slot_ref[0]) * own_rows, own_rows), own_rows), :]
            for k in range(piece_count)
        ]
        part = mm_nt(weight_ref[h], jnp.concatenate(sorted_rows)).astype(BF)
        for i in range(per):
            rows = head_dim // per
            query_part_ref[place_ref[(first + h) * per + i]] = part[i * rows : (i + 1) * rows]
        out_ref[2 * j] = dot(query_ref[first + h], mixed).astype(BF)
        out_ref[2 * j + 1] = mm_tn(grad_ref[j, :, :head_dim], mix_ref[j]).astype(BF)
        for i in range(2):
            slot = 2 * j + i
            place_copy(place_ref, first + h + i * heads, out_ref.at[slot], keep_ref, send_ref, out_sem_ref.at[slot])
    pl.when(step == pl.num_programs(0) - 1)(out_wait)


def attend_back(order, place, slot, query_t, hidden_media, hidden_own, pieces, folded, scores, own_scores, parts, factor, first, count, *halves):
    heads, head_dim, lat = query_t.shape
    seqs, patches, width = hidden_media.shape
    group = 4
    own = hidden_own.shape[0]
    block = group * lat
    sizes = (heads, group, seqs, lat, factor, len(pieces), len(parts), first, count)
    skip = first // group
    position = 9 + len(pieces) + len(parts)
    return pl.pallas_call(
        functools.partial(attend_back_kernel, sizes),
        grid=(count // group,),
        in_specs=[SMEM, SMEM, SMEM, whole(query_t.shape), whole(hidden_media.shape), whole(hidden_own.shape)]
        + [whole(p.shape) for p in pieces]
        + [
            pl.BlockSpec((block, width), lambda i: (i + skip, 0)),
            pl.BlockSpec((seqs, block, patches), lambda i: (0, i + skip, 0)),
            pl.BlockSpec((block, own), lambda i: (i + skip, 0)),
        ]
        + [ANYWHERE] * (len(parts) + len(halves)),
        out_specs=[
            ANYWHERE,
            ANYWHERE,
            whole((2 * heads, head_dim // 2, lat)),
            whole(hidden_media.shape),
            whole(hidden_own.shape),
        ],
        out_shape=[
            jax.ShapeDtypeStruct((heads, head_dim, width), BF),
            jax.ShapeDtypeStruct((heads, head_dim, width), BF),
            jax.ShapeDtypeStruct((2 * heads, head_dim // 2, lat), BF),
            jax.ShapeDtypeStruct(hidden_media.shape, F32),
            jax.ShapeDtypeStruct(hidden_own.shape, F32),
        ],
        scratch_shapes=[
            pltpu.VMEM((2 * count, head_dim, width), BF),
            pltpu.VMEM((group, seqs * lat, width), BF),
            pltpu.VMEM((seqs, block, width), BF),
            pltpu.VMEM((group, seqs * lat, LANES), BF),
            pltpu.VMEM((2 * group, head_dim, width), BF),
            pltpu.VMEM((block, width), BF),
            pltpu.SemaphoreType.DMA((2 * heads,)),
            pltpu.SemaphoreType.DMA((2 * group,)),
        ],
        input_output_aliases={position: 0, position + 1: 1} if halves else {},
        compiler_params=params(60),
        cost_estimate=cost(12e9, 20e6),
        name="attend_back",
    )(order, place, slot, query_t, hidden_media, hidden_own, *pieces, folded, scores, own_scores, *parts, *halves)


def local(
    grid,
    media,
    image_counts,
    time_ids,
    latents,
    time_table,
    media_gain,
    latent_gain,
    feed_gain,
    query_weight,
    keyval_weight,
    output_weight,
    up_weight,
    down_weight,
    cotangent,
):
    width = output_weight.shape[1]
    head_dim = width // HEADS
    factor = head_dim ** (-0.5)
    lat_rows = latents.shape[0]
    times = time_table.shape[0]
    seq_here, patches = media.shape[0], media.shape[2]
    own_rows = lat_rows // grid.frame
    rows = seq_here * own_rows
    part = width // grid.count
    slot = lax.axis_index("frame")
    first_row = slot * own_rows
    places, owners = grid.places(), grid.owners()
    aligned = grid.count == 2 * HEADS
    if aligned:
        order, place = owners, places
    else:
        order = place = jnp.arange(2 * HEADS, dtype=jnp.int32)

    def scatter_order(keep, send):
        if aligned:
            return keep, send
        v = jnp.concatenate([keep, send]).reshape(grid.count, -1, keep.shape[-1])
        v = v.at[owners].get(mode="promise_in_bounds")
        return v[: grid.count // 2], v[grid.count // 2 :]

    def aligned_parts(parts):
        if aligned:
            return parts
        flat = jnp.concatenate(parts).at[places].get(mode="promise_in_bounds")
        return [flat.reshape(2 * HEADS, -1, width)]

    pad = (-(lat_rows + times + 3)) % 8
    packed = jnp.concatenate(
        [latents, time_table, media_gain[None], latent_gain[None], feed_gain[None], jnp.zeros((pad, part), BF)]
    )
    small = grid.gather(packed.T[None], "z")
    first, *rest = grid.strides(grid.depth)
    keyval_z = grid.step(after(keyval_weight.T, small)[None], "z", first)
    small = after(small, keyval_z)
    for k in rest:
        keyval_z = grid.step(keyval_z, "z", k)
    small = grid.gather(small, "abc").at[places].get(mode="promise_in_bounds")
    small = small.reshape(width, -1).T.astype(F32)
    lat_float = small[:lat_rows]
    table_all = small[lat_rows : lat_rows + times]
    media_scale, latent_scale, feed_scale = (small[lat_rows + times + i][None] for i in range(3))

    grad_out = cotangent.reshape(rows, width)
    hid_f = up_weight.shape[1]
    hid = hid_f // grid.seq
    d_part = up_weight.shape[0]
    blocks = (grid.seq, hid, d_part)
    feed_got = jnp.concatenate([up_weight.T.reshape(blocks), down_weight.reshape(blocks)], -1)
    is_valid = (slot < image_counts).astype(jnp.int32)
    onehot = (time_ids[:, 0][:, None] == jnp.arange(times, dtype=jnp.int32)[None, :]).astype(F32)
    embedding = jnp.dot(onehot, table_all, precision=HIGHEST)
    embedded = media[:, 0].astype(F32) + embedding[:, None, :]
    normed_media, inv_media = normalize(embedded)
    hidden_media = (normed_media * media_scale).astype(BF)

    normed_lat, inv_lat = normalize(lat_float)
    hidden_lat = (normed_lat * latent_scale).astype(BF)
    hidden_own = lax.dynamic_slice_in_dim(hidden_lat, first_row, own_rows, 0)
    lat_own = lax.dynamic_slice_in_dim(lat_float, first_row, own_rows, 0)
    query_own = mm_tn(query_weight, hidden_lat.T).astype(BF)
    frame_ids = jnp.arange(grid.frame, dtype=jnp.int32) ^ slot
    query_t = after(grid.gather(query_own[None], "cab"), keyval_z)
    query_t = grid.gather(query_t, "z")
    first, *rest = grid.strides(grid.depth)
    mixed_first = grid.step(after(jnp.concatenate([output_weight, grad_out.astype(BF)]), query_t)[None], "z", first)
    mixed_z = mixed_first
    for k in rest:
        mixed_z = grid.step(mixed_z, "z", k)
    query_t = query_t.reshape(grid.count, part, grid.frame, own_rows)
    query_places = grid.places("cabz")
    query_t = query_t.at[query_places[:, None], :, frame_ids[None, :]].get(mode="promise_in_bounds")
    query_t = query_t.transpose(0, 2, 1, 3).reshape(HEADS, head_dim, lat_rows)
    keyval_ab = grid.gather_ab(keyval_z, query_t, mixed_first)
    keyval_parts = aligned_parts(grid.gather_core(keyval_ab, mixed_z))
    mixed_z = after(mixed_z, keyval_ab)
    feed_got = lax.all_to_all(after(feed_got, mixed_z), "seq", 0, 0)
    folded, media_scores, own_scores, context_parts = attend(
        order, is_valid, query_t, hidden_media, hidden_own, keyval_parts, factor
    )
    context_parts = context_parts.reshape(HEADS, seq_here, grid.frame, own_rows, LANES)
    pieces = [context_parts[:, :, k].reshape(HEADS, rows, LANES).astype(BF) for k in range(grid.frame)]
    pieces = after(pieces, feed_got)
    pieces = [pieces[0]] + [grid.to_frame(pieces[k], k) for k in range(1, grid.frame)]
    mixed_parts = grid.gather_core(grid.gather_ab(mixed_z, folded))
    if aligned:
        output_parts, grad_parts = mixed_parts, mixed_parts
    else:
        output_parts = aligned_parts([p[:, :part] for p in mixed_parts])
        grad_parts = [p[:, part:] for p in mixed_parts]
    mixed, normed_feed, hidden_feed, context, context_low = mixer(
        order, lat_own, feed_scale, pieces, output_parts, head_dim
    )

    up_t, down_w = unpack_feed(feed_got)
    feed_parts = grid.gather_core(grid.gather_ab(grid.gather(hidden_feed[None], "z"), up_t))
    half = len(feed_parts) // 2
    far, near = (feed_parts[half:], grad_parts[half:]), (feed_parts[:half], grad_parts[:half])
    far_act, far_grad_up, send = feed(up_t, down_w, *far)
    grad_sum = Scatter(grid, send)
    near_act, near_grad_up, keep = feed(up_t, down_w, *after(near, send))
    grad_sum.keep(keep)
    grad_sum.to_b()
    spare = part if aligned else 0
    far_up, far_down, send = feed_rest(down_w, far_act, after(far_grad_up, keep), *far, spare)
    near_up, near_down, keep = feed_rest(down_w, near_act, after(near_grad_up, send), *near, spare)
    grad_sum.to_a(send)
    grad_sum.to_z(keep)
    back = pack_back(grid.seq, far_up, far_down, near_up, near_down)
    grad_feed = after(grad_sum.result(), back)
    message, grad_mixed, grad_mixed_low, feed_gain_part, residual = unmix(
        order, grad_feed, grad_out, mixed, normed_feed, feed_scale, context, output_parts, head_dim, own_rows
    )
    messages = [message] + [grid.to_frame(message, k) for k in range(1, grid.frame)]
    back = lax.all_to_all(after(back, message), "seq", 0, 0)
    if aligned:
        keep, send = output_part_of(place, after(context_low, messages), grad_mixed_low, keep, send)
    else:
        out_keep, out_send = scatter_order(*output_part_of(place, context_low, grad_mixed_low))
        keep, send = jnp.concatenate([keep, out_keep], 1), jnp.concatenate([send, out_send], 1)
    mixed_sum = Scatter(grid, send)
    mixed_sum.keep(keep)
    messages = after(messages, keep)

    def back_half(messages, first, *halves):
        return attend_back(
            order, place, slot.reshape(1), query_t, hidden_media, hidden_own, messages, folded, media_scores, own_scores,
            keyval_parts, factor, first, HEADS // 2, *halves,
        )

    keep, send, query_near, grad_hidden_near, grad_own_near = back_half(messages, 0)
    keep, send = after((keep, send), mixed_sum.arrays[0])
    mixed_sum.to_b(send, back)
    keep, send, query_far, grad_hidden_far, grad_own_far = back_half(messages, HEADS // 2, keep, send)
    keep, send = scatter_order(keep, send)
    keyval_sum = Scatter(grid, send)
    keyval_sum.keep(keep)
    half = grid.count // 2
    query_part = query_near + query_far
    if not aligned:
        query_part = query_part.reshape(grid.count, part, lat_rows).at[owners].get(mode="promise_in_bounds")
    query_part = after(query_part, mixed_sum.last())
    query_sum = Scatter(grid, query_part[half:])
    query_sum.keep(query_part[:half])
    mixed_sum.to_a(send)
    query_sum.to_b()
    query_sum.to_a()
    keyval_sum.to_b(query_sum.last(), mixed_sum.last())
    keyval_b = keyval_sum.last()
    query_sum.to_z(keyval_sum.arrays[0])
    query_sum = query_sum.result().T.astype(BF)
    mixed_sum.to_z(query_sum)
    grad_hidden_near = after(grad_hidden_near, keyval_sum.arrays[0])
    back = after(back, keyval_b)
    grad_hidden = grad_hidden_near + grad_hidden_far
    grad_hidden_own = grad_own_near + grad_own_far

    media_gain_part = jnp.sum(grad_hidden * normed_media, (0, 1))
    grad_embedded = norm_back(grad_hidden * media_scale, normed_media, inv_media)
    table_part = jnp.dot(onehot.T, jnp.sum(grad_embedded, 1), precision=HIGHEST)

    query_grad = mm_tn(hidden_lat, query_sum)
    grad_lat = mm_nt(query_sum, query_weight)
    grad_lat = grad_lat + lax.dynamic_update_slice_in_dim(jnp.zeros_like(grad_lat), grad_hidden_own, first_row, 0)
    latent_gain_part = jnp.sum(grad_lat * normed_lat, 0)
    latents_part = norm_back(grad_lat * latent_scale, normed_lat, inv_lat)
    latents_part = latents_part + lax.dynamic_update_slice_in_dim(
        jnp.zeros_like(latents_part), residual, first_row, 0
    )
    smalls = jnp.concatenate(
        [
            latents_part,
            table_part,
            media_gain_part[None],
            latent_gain_part[None],
            feed_gain_part,
            jnp.zeros((pad, width), F32),
        ]
    ).astype(BF)
    smalls = smalls.T.reshape(grid.count, part, -1).at[grid.owners("cabz")].get(mode="promise_in_bounds")
    small_sum = grid.scatter_core_last(after(smalls, keyval_b)).T
    keyval_sum.to_a()
    keyval_sum.to_z()
    up_grad_t, down_grad = unpack_back(back)
    up_grad = up_grad_t.T
    keyval_grad = keyval_sum.result().T
    mixed_sums = mixed_sum.result()
    new_latents = (mixed + mixed_sums[:rows]).reshape(seq_here, own_rows, width)
    output_grad = mixed_sums[rows:]
    latents_grad = small_sum[:lat_rows]
    table_grad = small_sum[lat_rows : lat_rows + times]
    media_gain_grad, latent_gain_grad, feed_gain_grad = (small_sum[lat_rows + times + i] for i in range(3))
    return (
        new_latents,
        grad_embedded[:, None],
        latents_grad,
        table_grad,
        media_gain_grad,
        latent_gain_grad,
        feed_gain_grad,
        query_grad,
        keyval_grad,
        output_grad,
        up_grad,
        down_grad,
    )


def solution(mesh):
    grid = Grid(mesh.shape["seq"], mesh.shape["frame"])

    def run(*args):
        return local(grid, *args)

    return jax.shard_map(
        run,
        mesh=mesh,
        in_specs=(
            P("seq", "frame", None, None),
            P("seq"),
            P("seq", "frame"),
            P(None, BOTH),
            P(None, BOTH),
            P(BOTH),
            P(BOTH),
            P(BOTH),
            P(None, BOTH),
            P(None, BOTH),
            P(BOTH, None),
            P("seq", "frame"),
            P("frame", "seq"),
            P("seq", "frame", None),
        ),
        out_specs=(
            P("seq", "frame", None),
            P("seq", "frame", None, None),
            P(None, BOTH),
            P(None, BOTH),
            P(BOTH),
            P(BOTH),
            P(BOTH),
            P(None, BOTH),
            P(None, BOTH),
            P(BOTH, None),
            P("seq", "frame"),
            P("frame", "seq"),
        ),
        check_vma=False,
    )
```

```python
import functools

import jax
import jax.numpy as jnp
from jax import lax
from jax.experimental import pallas as pl
from jax.experimental.pallas import tpu as pltpu
from jax.sharding import PartitionSpec as P

HEADS = 16
EPS = 1e-05
NEGATIVE = -1e30
HIGHEST = lax.Precision.HIGHEST
BF = jnp.bfloat16
F32 = jnp.float32
BOTH = ("seq", "frame")


def normalize(values):
    center = values - jnp.mean(values, -1, keepdims=True)
    scale_inv = lax.rsqrt(jnp.mean(center * center, -1, keepdims=True) + EPS)
    return (center * scale_inv, scale_inv)


def norm_back(grad_hat, normed, scale_inv):
    return scale_inv * (
        grad_hat
        - jnp.mean(grad_hat, -1, keepdims=True)
        - normed * jnp.mean(grad_hat * normed, -1, keepdims=True)
    )


def mm(a, b):
    return jnp.dot(a, b, preferred_element_type=F32)


def mm_tn(a, b):
    return lax.dot_general(a, b, (((0,), (0,)), ((), ())), preferred_element_type=F32)


def mm_nt(a, b):
    return lax.dot_general(a, b, (((1,), (1,)), ((), ())), preferred_element_type=F32)


def ein(spec, a, b):
    return jnp.einsum(spec, a, b, preferred_element_type=F32)


def exact_gelu(values):
    return jax.nn.gelu(values, approximate=False)


def bits(n):
    return n.bit_length() - 1


class Grid:
    def __init__(self, seq_count, frame_count):
        self.seq, self.frame = seq_count, frame_count
        self.side = frame_count // 2
        self.depth = seq_count // self.side
        self.count = seq_count * frame_count

    def split(self, lin):
        side = bits(self.side)
        return lin >> (2 * side + 1), (lin >> (side + 1)) & (self.side - 1), (lin >> 1) & (self.side - 1), lin & 1

    def join(self, z, x, y, c):
        return ((z * self.side + x) * self.side + y) * 2 + c

    def send(self, value, move):
        perm = [(i, self.join(*move(*self.split(i)))) for i in range(self.count)]
        return lax.ppermute(value, BOTH, perm)

    def to_z(self, v, k):
        return self.send(v, lambda z, x, y, c: (z ^ k, x, y, c))

    def to_a(self, v, k):
        return self.send(v, lambda z, x, y, c: (z, x, y ^ k, c) if c else (z, x ^ k, y, c))

    def to_b(self, v, k):
        return self.send(v, lambda z, x, y, c: (z, x ^ k, y, c) if c else (z, x, y ^ k, c))

    def to_x(self, v, k):
        return self.send(v, lambda z, x, y, c: (z, x ^ k, y, c))

    def to_core(self, v):
        return self.send(v, lambda z, x, y, c: (z, x, y, 1 - c))

    def to_frame(self, v, k):
        def move(z, x, y, c):
            f = (y * 2 + c) ^ k
            return z, x, f // 2, f % 2

        return self.send(v, move)

    def own(self):
        return lax.axis_index("seq") * self.frame + lax.axis_index("frame")

    def scatter_core_last(self, v):
        for send, size in ((self.to_z, self.depth), (self.to_b, self.side), (self.to_a, self.side)):
            for k in reversed(self.strides(size)):
                half = v.shape[0] // 2
                v = v[:half].astype(F32) + send(v[half:].astype(BF), k).astype(F32)
        return v[0] + self.to_core(v[1].astype(BF)).astype(F32)

    def strides(self, size):
        return [1 << t for t in reversed(range(bits(size)))]

    def places(self, steps="zabc"):
        z, x, y, c = self.split(self.own())
        oz, ox, oy, oc = self.split(jnp.arange(self.count, dtype=jnp.int32))
        way = oc if steps[-1] == "c" else c
        rx, ry = ox ^ x, oy ^ y
        fields = {
            "z": (oz ^ z, self.depth),
            "a": (jnp.where(way == 0, rx, ry), self.side),
            "b": (jnp.where(way == 0, ry, rx), self.side),
            "c": (oc ^ c, 2),
        }
        place, bit = 0, 0
        for step in steps:
            value, size = fields[step]
            for k in self.strides(size):
                place = place + ((value & k != 0).astype(jnp.int32) << bit)
                bit += 1
        return place

    def owners(self, steps="zabc"):
        order = jnp.arange(self.count, dtype=jnp.int32)
        return jnp.zeros_like(order).at[self.places(steps)].set(order, unique_indices=True)

    def step(self, v, kind, k):
        send = {"z": self.to_z, "a": self.to_a, "b": self.to_b, "c": lambda p, _: self.to_core(p)}[kind]
        return jnp.concatenate([v, send(v, k)])

    def gather(self, v, steps):
        for kind in steps:
            for k in self.strides({"z": self.depth, "c": 2}.get(kind, self.side)):
                v = self.step(v, kind, k)
        return v

    def gather_ab(self, v, *others):
        v = [v]
        for k in self.strides(self.side):
            v = v + [self.to_a(p, k) for p in v]
        for k in self.strides(self.side):
            own = self.to_b(v[0], k)
            v = v + [own] + [self.to_b(after(p, own, others), k) for p in v[1:]]
        return v

    def gather_core(self, v, *others):
        return v + [self.to_core(p) for p in v[:-1]] + [self.to_core(after(v[-1], others))]


class Scatter:
    def __init__(self, grid, low, high, *others):
        self.grid = grid
        self.size = 2 * low.shape[0]
        low, high = after((low, high), others)
        self.high, self.arrays = [grid.to_core(high)], [grid.to_core(low)]

    def keep(self, keep):
        half = self.size // 2
        self.high.append(keep[half:])
        self.arrays.append(keep)

    def sum(self, lo, hi):
        arrays = self.arrays
        if hi > self.arrays[0].shape[0]:
            arrays, lo, hi = self.high, 0, hi - lo
        return sum(p[lo:hi].astype(F32) for p in arrays)

    def step(self, send, strides, *others):
        for k in strides:
            half = self.size // 2
            self.arrays.append(send(after(self.sum(half, self.size).astype(BF), others), k))
            self.size = half

    def to_b(self, *others):
        self.step(self.grid.to_b, self.grid.strides(self.grid.side)[::-1], *others)

    def to_a(self, *others):
        self.step(self.grid.to_a, self.grid.strides(self.grid.side)[::-1], *others)

    def to_z(self, *others, first=True, rest=True):
        strides = self.grid.strides(self.grid.depth)[::-1]
        self.step(self.grid.to_z, (strides[:1] if first else []) + (strides[1:] if rest else []), *others)

    def last(self):
        return self.arrays[-1]

    def result(self):
        return self.sum(0, 1)[0]


def after(value, *others):
    return lax.optimization_barrier((value, others))[0]


def load_blocks(order_ref, part_refs, store_ref, sem_ref):
    rows = store_ref.shape[1]
    copies = []
    for part in part_refs:
        for k in range(part.shape[0]):
            n = len(copies)
            block = part.at[k] if part.shape[1] == rows else part.at[k, pl.ds(0, rows)]
            copies.append(pltpu.make_async_copy(block, store_ref.at[order_ref[n]], sem_ref.at[n]))
    return copies


def place_copy(place_ref, block, source_ref, target_refs, sem_ref):
    place = place_ref[block]
    first = 0
    for target in target_refs:
        index, size = place - first, target.shape[0]
        first += size

        @pl.when((index >= 0) & (index < size))
        def _():
            pltpu.make_async_copy(source_ref, target.at[index], sem_ref).start()


def dot(a, b):
    return lax.dot_general(a, b, (((1,), (0,)), ((), ())), preferred_element_type=F32)


def pieces_of(value):
    high = value.astype(BF).astype(F32)
    middle = (value - high).astype(BF).astype(F32)
    return high, middle, value - high - middle


def whole(shape):
    return pl.BlockSpec(shape, lambda *_: (0,) * len(shape))


SMEM = pl.BlockSpec(memory_space=pltpu.SMEM)
ANYWHERE = pl.BlockSpec(memory_space=pltpu.HBM)
LANES = 128


def params(mib):
    return pltpu.CompilerParams(vmem_limit_bytes=mib * 1024 * 1024)


def cost(flops, moved):
    return pl.CostEstimate(flops=int(flops), bytes_accessed=int(moved), transcendentals=0)


def attend_kernel(sizes, order_ref, valid_ref, query_ref, media_ref, own_ref, *refs):
    heads, group, seqs, lat, factor, part_count = sizes
    parts = refs[:part_count]
    folded_ref, score_ref, own_score_ref, context_ref, weight_ref, mix_ref, sem_ref = refs[part_count:]
    step = pl.program_id(0)
    head_dim = weight_ref.shape[1]

    @pl.when(step == 0)
    def _():
        copies = load_blocks(order_ref, parts, weight_ref, sem_ref)
        for c in copies:
            c.start()
        for c in copies:
            c.wait()

    for j in range(group):
        h = step * group + j
        folded = mm_tn(query_ref[h], weight_ref[h]) * factor
        folded_ref[j * lat : (j + 1) * lat, :] = folded.astype(BF)
    queries = folded_ref[...]
    own = own_ref[...]
    own_scores = mm_nt(queries, own)
    own_score_ref[...] = own_scores
    own_top = jnp.max(own_scores, -1, keepdims=True)
    lanes = lax.broadcasted_iota(jnp.int32, (group * lat, LANES), 1)
    for s in range(seqs):
        media = media_ref[s]
        scores = mm_nt(queries, media)
        scores = jnp.where(valid_ref[s] > 0, scores, NEGATIVE)
        score_ref[s] = scores
        top = jnp.maximum(jnp.max(scores, -1, keepdims=True), own_top)
        media_exp = jnp.exp(scores - top)
        own_exp = jnp.exp(own_scores - top)
        total = jnp.sum(media_exp, -1, keepdims=True) + jnp.sum(own_exp, -1, keepdims=True)
        mix = dot(media_exp.astype(BF), media) + dot(own_exp.astype(BF), own)
        mix = (mix * (1.0 / total)).astype(BF)
        stats = jnp.zeros(lanes.shape, F32)
        for i, piece in enumerate(pieces_of(top) + pieces_of(total)):
            stats = jnp.where(lanes == head_dim + i, piece, stats)
        for j in range(group):
            mix_ref[j, s * lat : (s + 1) * lat, :] = mix[j * lat : (j + 1) * lat, :]
            context_ref[j, s * lat : (s + 1) * lat, head_dim:] = stats[j * lat : (j + 1) * lat, head_dim:]
    for j in range(group):
        h = step * group + j
        context_ref[j, :, :head_dim] = mm_nt(mix_ref[j], weight_ref[heads + h])


def attend(order, valid, query_t, hidden_media, hidden_own, parts, factor):
    heads, head_dim, lat = query_t.shape
    seqs, patches, width = hidden_media.shape
    group = 4
    own = hidden_own.shape[0]
    rows = group * lat
    return pl.pallas_call(
        functools.partial(attend_kernel, (heads, group, seqs, lat, factor, len(parts))),
        grid=(heads // group,),
        in_specs=[SMEM, SMEM, whole(query_t.shape), whole(hidden_media.shape), whole(hidden_own.shape)]
        + [ANYWHERE] * len(parts),
        out_specs=[
            pl.BlockSpec((rows, width), lambda i: (i, 0)),
            pl.BlockSpec((seqs, rows, patches), lambda i: (0, i, 0)),
            pl.BlockSpec((rows, own), lambda i: (i, 0)),
            pl.BlockSpec((group, seqs * lat, LANES), lambda i: (i, 0, 0)),
        ],
        out_shape=[
            jax.ShapeDtypeStruct((heads * lat, width), BF),
            jax.ShapeDtypeStruct((seqs, heads * lat, patches), F32),
            jax.ShapeDtypeStruct((heads * lat, own), F32),
            jax.ShapeDtypeStruct((heads, seqs * lat, LANES), F32),
        ],
        scratch_shapes=[
            pltpu.VMEM((2 * heads, head_dim, width), BF),
            pltpu.VMEM((group, seqs * lat, width), BF),
            pltpu.SemaphoreType.DMA((2 * heads,)),
        ],
        compiler_params=params(56),
        cost_estimate=cost(2e9, 2e6),
        name="attend",
    )(order, valid, query_t, hidden_media, hidden_own, *parts)


def mixer_kernel(sizes, order_ref, latent_ref, gain_ref, *refs):
    heads, head_dim, seqs, piece_count, part_count = sizes
    pieces = refs[:piece_count]
    parts = refs[piece_count : piece_count + part_count]
    mixed_ref, normed_ref, hidden_ref, context_ref, low_ref, weight_ref, sem_ref = refs[piece_count + part_count :]
    copies = load_blocks(order_ref, parts, weight_ref, sem_ref)
    for c in copies:
        c.start()
    values = [p[...].astype(F32) for p in pieces]
    at = head_dim
    tops = [v[..., at : at + 1] + v[..., at + 1 : at + 2] + v[..., at + 2 : at + 3] for v in values]
    totals = [v[..., at + 3 : at + 4] + v[..., at + 4 : at + 5] + v[..., at + 5 : at + 6] for v in values]
    top = functools.reduce(jnp.maximum, tops)
    shares = [t * jnp.exp(p - top) for t, p in zip(totals, tops)]
    total = functools.reduce(lambda p, q: p + q, shares)
    context = functools.reduce(lambda p, q: p + q, [v * (w / total) for v, w in zip(values, shares)])
    lanes = lax.broadcasted_iota(jnp.int32, context.shape, 2)
    context_ref[...] = jnp.where(lanes == head_dim, top + jnp.log(total), context)
    for h in range(heads):
        low_ref[:, h * head_dim : (h + 1) * head_dim] = context[h, :, :head_dim].astype(BF)
    for c in copies:
        c.wait()
    weight = weight_ref[...].reshape(heads * head_dim, -1)
    mixed = jnp.concatenate([latent_ref[...]] * seqs) + dot(low_ref[...], weight)
    mixed_ref[...] = mixed
    center = mixed - jnp.mean(mixed, -1, keepdims=True)
    normed = center * lax.rsqrt(jnp.mean(center * center, -1, keepdims=True) + EPS)
    normed_ref[...] = normed
    hidden_ref[...] = (normed * gain_ref[...]).astype(BF)


def mixer(order, latent_own, gain, pieces, parts, head_dim):
    heads, rows, _ = pieces[0].shape
    own_rows, width = latent_own.shape
    count = sum(p.shape[0] for p in parts)
    block = heads * head_dim // count
    sizes = (heads, head_dim, rows // own_rows, len(pieces), len(parts))
    return pl.pallas_call(
        functools.partial(mixer_kernel, sizes),
        in_specs=[SMEM, whole(latent_own.shape), whole(gain.shape)]
        + [whole(p.shape) for p in pieces]
        + [ANYWHERE] * len(parts),
        out_specs=[whole((rows, width))] * 3 + [whole((heads, rows, LANES)), whole((rows, heads * head_dim))],
        out_shape=[
            jax.ShapeDtypeStruct((rows, width), F32),
            jax.ShapeDtypeStruct((rows, width), F32),
            jax.ShapeDtypeStruct((rows, width), BF),
            jax.ShapeDtypeStruct((heads, rows, LANES), F32),
            jax.ShapeDtypeStruct((rows, heads * head_dim), BF),
        ],
        scratch_shapes=[pltpu.VMEM((count, block, width), BF), pltpu.SemaphoreType.DMA((count,))],
        compiler_params=params(32),
        cost_estimate=cost(2e9, 8e6),
        name="mixer",
    )(order, latent_own, gain, *pieces, *parts)


def unmix_kernel(sizes, order_ref, grad_feed_ref, grad_out_ref, mixed_ref, normed_ref, gain_ref, context_ref, *refs):
    heads, head_dim, seqs, part_count = sizes
    parts = refs[:part_count]
    message_ref, grad_mixed_ref, low_ref, gain_grad_ref, residual_ref, weight_ref, sem_ref = refs[part_count:]
    copies = load_blocks(order_ref, parts, weight_ref, sem_ref)
    for c in copies:
        c.start()
    mixed = mixed_ref[...]
    center = mixed - jnp.mean(mixed, -1, keepdims=True)
    scale_inv = lax.rsqrt(jnp.mean(center * center, -1, keepdims=True) + EPS)
    normed = normed_ref[...]
    grad_feed = grad_feed_ref[...]
    gain_grad_ref[...] = jnp.sum(grad_feed * normed, 0, keepdims=True)
    grad_mixed = grad_out_ref[...] + norm_back(grad_feed * gain_ref[...], normed, scale_inv)
    grad_mixed_ref[...] = grad_mixed
    own = residual_ref.shape[0]
    residual_ref[...] = sum(grad_mixed[s * own : (s + 1) * own] for s in range(seqs))
    low = grad_mixed.astype(BF)
    low_ref[...] = low
    for c in copies:
        c.wait()
    grads = mm_nt(low, weight_ref[...].reshape(heads * head_dim, -1)).astype(BF)
    lanes = lax.broadcasted_iota(jnp.int32, (low.shape[0], LANES), 1)
    for h in range(heads):
        grad = grads[:, h * head_dim : (h + 1) * head_dim]
        context = context_ref[h]
        row = jnp.sum(grad.astype(F32) * context[:, :head_dim], -1, keepdims=True)
        log_total = context[:, head_dim : head_dim + 1]
        message = jnp.zeros(lanes.shape, F32)
        for i, piece in enumerate(pieces_of(row) + pieces_of(log_total)):
            message = jnp.where(lanes == head_dim + i, piece, message)
        message_ref[h] = message.astype(BF)
        message_ref[h, :, :head_dim] = grad


def unmix(order, grad_feed, grad_out, mixed, normed, gain, context, parts, head_dim, own_rows):
    heads, rows, _ = context.shape
    width = mixed.shape[1]
    count = sum(p.shape[0] for p in parts)
    block = heads * head_dim // count
    sizes = (heads, head_dim, rows // own_rows, len(parts))
    arrays = (grad_feed, grad_out, mixed, normed, gain, context)
    shapes = [((heads, rows, LANES), BF), ((rows, width), F32), ((rows, width), BF), ((1, width), F32), ((own_rows, width), F32)]
    return pl.pallas_call(
        functools.partial(unmix_kernel, sizes),
        in_specs=[SMEM] + [whole(a.shape) for a in arrays] + [ANYWHERE] * len(parts),
        out_specs=[whole(shape) for shape, _ in shapes],
        out_shape=[jax.ShapeDtypeStruct(*item) for item in shapes],
        scratch_shapes=[pltpu.VMEM((count, block, width), BF), pltpu.SemaphoreType.DMA((count,))],
        compiler_params=params(32),
        cost_estimate=cost(2e9, 8e6),
        name="unmix",
    )(order, *arrays, *parts)


def output_part_kernel(groups, place_ref, context_ref, low_ref, *refs):
    *targets, out_ref, sem_ref = refs[-5:]
    low = low_ref[...]
    per = out_ref.shape[0] // groups
    part = context_ref.shape[1] // groups
    rows = out_ref.shape[1]
    targets = [t.at[:, pl.ds(t.shape[1] - rows, rows)] for t in targets]
    for g in range(groups):
        value = mm_tn(context_ref[:, g * part : (g + 1) * part], low).astype(BF)
        out_ref[g * per : (g + 1) * per] = value.reshape((per,) + out_ref.shape[1:])
        for i in range(g * per, (g + 1) * per):
            place_copy(place_ref, i, out_ref.at[i], targets, sem_ref.at[i])
    for i in range(out_ref.shape[0]):
        pltpu.make_async_copy(out_ref.at[i], targets[0].at[0], sem_ref.at[i]).wait()


def output_part_of(place, context, low, *halves):
    width = low.shape[1]
    count = place.shape[0]
    block = context.shape[1] // count
    shapes = [h.shape for h in halves] or [(n, block, width) for n in (count // 2, count // 4, count // 4)]
    return pl.pallas_call(
        functools.partial(output_part_kernel, 4),
        in_specs=[SMEM, whole(context.shape), whole(low.shape)] + [ANYWHERE] * len(halves),
        out_specs=[ANYWHERE] * 3,
        out_shape=[jax.ShapeDtypeStruct(shape, BF) for shape in shapes],
        input_output_aliases={3: 0, 4: 1, 5: 2} if halves else {},
        scratch_shapes=[pltpu.VMEM((count, block, width), BF), pltpu.SemaphoreType.DMA((count,))],
        compiler_params=params(32),
        cost_estimate=cost(1e9, 2e6),
        name="output_part",
    )(place, context, low, *halves)


def unpack_feed_kernel(got_ref, up_ref, down_ref):
    part = got_ref.shape[-1] // 2
    for s in range(got_ref.shape[0]):
        up_ref[:, s * part : (s + 1) * part] = got_ref[s, :, :part]
        down_ref[:, s * part : (s + 1) * part] = got_ref[s, :, part:]


def unpack_feed(got):
    count, hid, part = got.shape
    out = (hid, count * part // 2)
    return pl.pallas_call(
        unpack_feed_kernel,
        in_specs=[whole(got.shape)],
        out_specs=[whole(out)] * 2,
        out_shape=[jax.ShapeDtypeStruct(out, BF)] * 2,
        cost_estimate=cost(0, 3e6),
        name="unpack_feed",
    )(got)


def pack_back_kernel(far_up_ref, far_down_ref, near_up_ref, near_down_ref, out_ref):
    part = out_ref.shape[-1] // 2
    for s in range(out_ref.shape[0]):
        at = slice(s * part, (s + 1) * part)
        out_ref[s, :, :part] = (far_up_ref[:, at] + near_up_ref[:, at]).astype(BF)
        out_ref[s, :, part:] = (far_down_ref[:, at] + near_down_ref[:, at]).astype(BF)


def pack_back(count, *grads):
    hid, width = grads[0].shape
    out = (count, hid, 2 * width // count)
    return pl.pallas_call(
        pack_back_kernel,
        in_specs=[whole(g.shape) for g in grads],
        out_specs=whole(out),
        out_shape=jax.ShapeDtypeStruct(out, BF),
        cost_estimate=cost(0, 6e6),
        name="pack_back",
    )(*grads)


def unpack_back_kernel(got_ref, up_ref, down_ref):
    hid, part = got_ref.shape[1], got_ref.shape[2] // 2
    for s in range(got_ref.shape[0]):
        up_ref[s * hid : (s + 1) * hid, :] = got_ref[s, :, :part].astype(F32)
        down_ref[s * hid : (s + 1) * hid, :] = got_ref[s, :, part:].astype(F32)


def unpack_back(got):
    count, hid, part = got.shape
    out = (count * hid, part // 2)
    return pl.pallas_call(
        unpack_back_kernel,
        in_specs=[whole(got.shape)],
        out_specs=[whole(out)] * 2,
        out_shape=[jax.ShapeDtypeStruct(out, F32)] * 2,
        cost_estimate=cost(0, 5e6),
        name="unpack_back",
    )(got)


ROOT_HALF = 0.5**0.5
DENSITY = 1 / (2 * 3.141592653589793) ** 0.5


def loads(parts, rows, store_ref, sem_ref):
    out, n = [], 0
    for part in parts:
        skip = part.shape[1] - rows
        copies = []
        for k in range(part.shape[0]):
            block = part.at[k, pl.ds(skip, rows)] if skip else part.at[k]
            copies.append(pltpu.make_async_copy(block, store_ref.at[n], sem_ref.at[n]))
            n += 1
        out.append(copies)
    return out


def start(copies):
    for c in copies:
        c.start()


def wait(copies):
    for c in copies:
        c.wait()


def feed_kernel(part_count, up_ref, down_ref, *refs):
    feed, grad = refs[:part_count], refs[part_count : 2 * part_count]
    act_ref, grad_up_ref, *out_refs = refs[2 * part_count : -6]
    feed_st, grad_st, out_st, feed_sem, grad_sem, out_sem = refs[-6:]
    each = part_count // len(out_refs)
    n, per, width = feed[0].shape
    chunk = n * per
    feeds, grads = loads(feed, per, feed_st, feed_sem), loads(grad, per, grad_st, grad_sem)
    for i in range(part_count):
        start(feeds[i])
        start(grads[i])
    up, down = up_ref[...], down_ref[...]
    outs = []
    each, n, chunk = each // 2, 2 * n, 2 * chunk
    for i in range(part_count // 2):
        at = slice(i * n, (i + 1) * n)
        wait(feeds[2 * i] + feeds[2 * i + 1])
        pre = mm_nt(feed_st[at].reshape(chunk, width), up)
        wait(grads[2 * i] + grads[2 * i + 1])
        grad_act = mm_nt(grad_st[at].reshape(chunk, width), down)
        cdf = 0.5 * (1.0 + lax.erf(pre * ROOT_HALF))
        slope = cdf + pre * (jnp.exp(-0.5 * pre * pre) * DENSITY)
        act_ref[i * chunk : (i + 1) * chunk, :] = (pre * cdf).astype(BF)
        grad_up = (grad_act * slope).astype(BF)
        grad_up_ref[i * chunk : (i + 1) * chunk, :] = grad_up
        out_st[at] = dot(grad_up, up).astype(BF).reshape(n, per, width)
        to = out_refs[i // each].at[pl.ds(i % each * n, n)]
        outs.append(pltpu.make_async_copy(out_st.at[pl.ds(i * n, n)], to, out_sem.at[i]))
        outs[i].start()
    wait(outs)


def feed(up, down, feed_parts, grad_parts, splits):
    hid, width = up.shape
    count = len(feed_parts)
    n, per, _ = feed_parts[0].shape
    rows = count * n * per
    store = pltpu.VMEM((count * n, per, width), BF)
    sems = pltpu.SemaphoreType.DMA((count * n,))
    return pl.pallas_call(
        functools.partial(feed_kernel, count),
        in_specs=[whole(up.shape), whole(down.shape)] + [ANYWHERE] * (2 * count),
        out_specs=[whole((rows, hid))] * 2 + [ANYWHERE] * splits,
        out_shape=[jax.ShapeDtypeStruct((rows, hid), BF)] * 2
        + [jax.ShapeDtypeStruct((count * n // splits, per, width), BF)] * splits,
        scratch_shapes=[store] * 3 + [sems] * 3,
        compiler_params=params(48),
        cost_estimate=cost(5e9, 8e6),
        name="feed",
    )(up, down, *feed_parts, *grad_parts)


def feed_rest_kernel(part_count, down_ref, act_ref, grad_up_ref, *refs):
    feed, grad = refs[:part_count], refs[part_count : 2 * part_count]
    up_grad_ref, down_grad_ref, *out_refs = refs[2 * part_count : -6]
    feed_st, grad_st, out_st, feed_sem, grad_sem, out_sem = refs[-6:]
    each = part_count // len(out_refs)
    n, per, width = feed[0].shape
    chunk = n * per
    feeds, grads = loads(feed, per, feed_st, feed_sem), loads(grad, per, grad_st, grad_sem)
    for i in range(part_count):
        start(feeds[i])
        start(grads[i])
    down = down_ref[...]
    first = pl.ds(0, per)
    outs = []
    for i in range(part_count):
        at = slice(i * n, (i + 1) * n)
        act = act_ref[i * chunk : (i + 1) * chunk, :]
        out_st[at] = dot(act, down).astype(BF).reshape(n, per, width)
        to = out_refs[i // each].at[pl.ds(i % each * n, n), first]
        outs.append(pltpu.make_async_copy(out_st.at[pl.ds(i * n, n)], to, out_sem.at[i]))
        outs[i].start()
    for i in range(part_count):
        wait(feeds[i])
        wait(grads[i])
    up_grad_ref[...] = mm_tn(grad_up_ref[...], feed_st[...].reshape(part_count * chunk, width))
    down_grad_ref[...] = mm_tn(act_ref[...], grad_st[...].reshape(part_count * chunk, width))
    wait(outs)


def feed_rest(down, act, grad_up, feed_parts, grad_parts, spare, splits):
    hid, width = down.shape
    count = len(feed_parts)
    n, per, _ = feed_parts[0].shape
    store = pltpu.VMEM((count * n, per, width), BF)
    sems = pltpu.SemaphoreType.DMA((count * n,))
    return pl.pallas_call(
        functools.partial(feed_rest_kernel, count),
        in_specs=[whole(down.shape), whole(act.shape), whole(grad_up.shape)] + [ANYWHERE] * (2 * count),
        out_specs=[whole((hid, width))] * 2 + [ANYWHERE] * splits,
        out_shape=[jax.ShapeDtypeStruct((hid, width), F32)] * 2
        + [jax.ShapeDtypeStruct((count * n // splits, per + spare, width), BF)] * splits,
        scratch_shapes=[store] * 3 + [sems] * 3,
        compiler_params=params(48),
        cost_estimate=cost(5e9, 8e6),
        name="feed_rest",
    )(down, act, grad_up, *feed_parts, *grad_parts)


def attend_back_kernel(sizes, order_ref, place_ref, slot_ref, query_ref, media_ref, own_ref, *refs):
    heads, group, seqs, lat, factor, piece_count, part_count, first, count = sizes
    pieces = refs[:piece_count]
    folded_ref, score_ref, own_score_ref = refs[piece_count : piece_count + 3]
    parts = refs[piece_count + 3 : piece_count + 3 + part_count]
    refs = refs[piece_count + 3 + part_count :]
    (
        keep_ref,
        low_ref,
        high_ref,
        query_part_ref,
        grad_media_ref,
        grad_own_ref,
        weight_ref,
        mix_ref,
        gp_ref,
        grad_ref,
        out_ref,
        key_mix_ref,
        sem_ref,
        out_sem_ref,
    ) = refs[-14:]
    step = pl.program_id(0)
    head_dim = weight_ref.shape[1]
    own_rows = own_ref.shape[0]

    def out_wait():
        for slot in range(2 * group):
            pltpu.make_async_copy(out_ref.at[slot], keep_ref.at[0], out_sem_ref.at[slot]).wait()

    @pl.when(step == 0)
    def _():
        loads_here = []
        for part in parts:
            for k in range(part.shape[0]):
                n = len(loads_here)
                block = order_ref[n]
                head = block & (heads - 1)
                here = (head >= first) & (head < first + count)
                to = jnp.where(here, head - first + jnp.where(block >= heads, count, 0), 0)
                loads_here.append((here, pltpu.make_async_copy(part.at[k], weight_ref.at[to], sem_ref.at[n])))
        for here, c in loads_here:
            pl.when(here)(c.start)
        grad_media_ref[...] = jnp.zeros_like(grad_media_ref)
        grad_own_ref[...] = jnp.zeros_like(grad_own_ref)
        query_part_ref[...] = jnp.zeros_like(query_part_ref)
        for here, c in loads_here:
            pl.when(here)(c.wait)

    columns = []
    for j in range(group):
        h = step * group + j
        for s in range(seqs):
            for k in range(piece_count):
                at = s * lat + k * own_rows
                grad_ref[j, at : at + own_rows, :] = pieces[k][first + h, s * own_rows : (s + 1) * own_rows, :]
        message = grad_ref[j].astype(F32)
        column = [message[:, head_dim + i : head_dim + i + 1] for i in range(6)]
        columns.append((column[0] + column[1] + column[2], column[3] + column[4] + column[5]))
        lifted = dot(grad_ref[j, :, :head_dim], weight_ref[count + h]).astype(BF)
        for s in range(seqs):
            gp_ref[s, j * lat : (j + 1) * lat, :] = lifted[s * lat : (s + 1) * lat, :]
    queries = folded_ref[...]
    own = own_ref[...]
    own_scores = own_score_ref[...]
    key_mix = jnp.zeros(queries.shape, F32)
    for s in range(seqs):
        media = media_ref[s]
        lifted = gp_ref[s]
        row_term, log_total = (
            jnp.concatenate([columns[j][i][s * lat : (s + 1) * lat] for j in range(group)]) for i in range(2)
        )
        probs = jnp.exp(score_ref[s] - log_total)
        own_probs = jnp.exp(own_scores - log_total)
        ds = (probs * (mm_nt(lifted, media) - row_term)).astype(BF)
        own_ds = (own_probs * (mm_nt(lifted, own) - row_term)).astype(BF)
        probs, own_probs = probs.astype(BF), own_probs.astype(BF)
        key_mix = key_mix + dot(ds, media) + dot(own_ds, own)
        mix = (dot(probs, media) + dot(own_probs, own)).astype(BF)
        for j in range(group):
            mix_ref[j, s * lat : (s + 1) * lat, :] = mix[j * lat : (j + 1) * lat, :]
        grad_media_ref[s] += mm_tn(ds, queries) + mm_tn(probs, lifted)
        grad_own_ref[...] += mm_tn(own_ds, queries) + mm_tn(own_probs, lifted)
    key_mix_ref[...] = (key_mix * factor).astype(BF)
    per = query_part_ref.shape[0] // heads
    pl.when(step > 0)(out_wait)
    for j in range(group):
        h = step * group + j
        mixed = key_mix_ref[j * lat : (j + 1) * lat, :]
        sorted_rows = [
            key_mix_ref[pl.ds(pl.multiple_of(j * lat + (k ^ slot_ref[0]) * own_rows, own_rows), own_rows), :]
            for k in range(piece_count)
        ]
        part = mm_nt(weight_ref[h], jnp.concatenate(sorted_rows)).astype(BF)
        for i in range(per):
            rows = head_dim // per
            query_part_ref[place_ref[(first + h) * per + i]] = part[i * rows : (i + 1) * rows]
        out_ref[2 * j] = dot(query_ref[first + h], mixed).astype(BF)
        out_ref[2 * j + 1] = mm_tn(grad_ref[j, :, :head_dim], mix_ref[j]).astype(BF)
        for i in range(2):
            slot = 2 * j + i
            place_copy(
                place_ref, first + h + i * heads, out_ref.at[slot], (keep_ref, low_ref, high_ref), out_sem_ref.at[slot]
            )
    pl.when(step == pl.num_programs(0) - 1)(out_wait)


def attend_back(order, place, slot, query_t, hidden_media, hidden_own, pieces, folded, scores, own_scores, parts, factor, first, count, work, *halves):
    heads, head_dim, lat = query_t.shape
    seqs, patches, width = hidden_media.shape
    group = 4
    own = hidden_own.shape[0]
    block = group * lat
    sizes = (heads, group, seqs, lat, factor, len(pieces), len(parts), first, count)
    skip = first // group
    position = 9 + len(pieces) + len(parts)
    return pl.pallas_call(
        functools.partial(attend_back_kernel, sizes),
        grid=(count // group,),
        in_specs=[SMEM, SMEM, SMEM, whole(query_t.shape), whole(hidden_media.shape), whole(hidden_own.shape)]
        + [whole(p.shape) for p in pieces]
        + [
            pl.BlockSpec((block, width), lambda i: (i + skip, 0)),
            pl.BlockSpec((seqs, block, patches), lambda i: (0, i + skip, 0)),
            pl.BlockSpec((block, own), lambda i: (i + skip, 0)),
        ]
        + [ANYWHERE] * (len(parts) + len(halves)),
        out_specs=[
            ANYWHERE,
            ANYWHERE,
            ANYWHERE,
            whole((2 * heads, head_dim // 2, lat)),
            whole(hidden_media.shape),
            whole(hidden_own.shape),
        ],
        out_shape=[
            jax.ShapeDtypeStruct((heads, head_dim, width), BF),
            jax.ShapeDtypeStruct((heads // 2, head_dim, width), BF),
            jax.ShapeDtypeStruct((heads // 2, head_dim, width), BF),
            jax.ShapeDtypeStruct((2 * heads, head_dim // 2, lat), BF),
            jax.ShapeDtypeStruct(hidden_media.shape, F32),
            jax.ShapeDtypeStruct(hidden_own.shape, F32),
        ],
        scratch_shapes=[
            pltpu.VMEM((2 * count, head_dim, width), BF),
            pltpu.VMEM((group, seqs * lat, width), BF),
            pltpu.VMEM((seqs, block, width), BF),
            pltpu.VMEM((group, seqs * lat, LANES), BF),
            pltpu.VMEM((2 * group, head_dim, width), BF),
            pltpu.VMEM((block, width), BF),
            pltpu.SemaphoreType.DMA((2 * heads,)),
            pltpu.SemaphoreType.DMA((2 * group,)),
        ],
        input_output_aliases={position: 0, position + 1: 1, position + 2: 2} if halves else {},
        compiler_params=params(60),
        cost_estimate=cost(work, 20e6),
        name="attend_back",
    )(order, place, slot, query_t, hidden_media, hidden_own, *pieces, folded, scores, own_scores, *parts, *halves)


def local(
    grid,
    media,
    image_counts,
    time_ids,
    latents,
    time_table,
    media_gain,
    latent_gain,
    feed_gain,
    query_weight,
    keyval_weight,
    output_weight,
    up_weight,
    down_weight,
    cotangent,
):
    width = output_weight.shape[1]
    head_dim = width // HEADS
    factor = head_dim ** (-0.5)
    lat_rows = latents.shape[0]
    times = time_table.shape[0]
    seq_here, patches = media.shape[0], media.shape[2]
    own_rows = lat_rows // grid.frame
    rows = seq_here * own_rows
    part = width // grid.count
    slot = lax.axis_index("frame")
    first_row = slot * own_rows
    places, owners = grid.places(), grid.owners()
    aligned = grid.count == 2 * HEADS
    if aligned:
        order, place = owners, places
    else:
        order = place = jnp.arange(2 * HEADS, dtype=jnp.int32)

    quarters = (grid.count // 2, grid.count // 2 + grid.count // 4)

    def scatter_order(parts):
        if aligned:
            return parts
        v = jnp.concatenate(parts).reshape(grid.count, -1, parts[0].shape[-1])
        return jnp.split(v.at[owners].get(mode="promise_in_bounds"), quarters)

    def aligned_parts(parts):
        if aligned:
            return parts
        flat = jnp.concatenate(parts).at[places].get(mode="promise_in_bounds")
        return [flat.reshape(2 * HEADS, -1, width)]

    pad = (-(lat_rows + times + 3)) % 8
    packed = jnp.concatenate(
        [latents, time_table, media_gain[None], latent_gain[None], feed_gain[None], jnp.zeros((pad, part), BF)]
    )
    small = grid.gather(packed.T[None], "z")
    first, *rest = grid.strides(grid.depth)
    keyval_z = grid.step(after(keyval_weight.T, small)[None], "z", first)
    small = grid.gather(after(small, keyval_z), "ab")
    for k in rest:
        keyval_z = grid.step(keyval_z, "z", k)
    small = grid.gather(after(small, keyval_z), "c").at[places].get(mode="promise_in_bounds")
    small = small.reshape(width, -1).T.astype(F32)
    lat_float = small[:lat_rows]
    table_all = small[lat_rows : lat_rows + times]
    media_scale, latent_scale, feed_scale = (small[lat_rows + times + i][None] for i in range(3))

    grad_out = cotangent.reshape(rows, width)
    hid_f = up_weight.shape[1]
    hid = hid_f // grid.seq
    d_part = up_weight.shape[0]
    blocks = (grid.seq, hid, d_part)
    feed_got = jnp.concatenate([up_weight.T.reshape(blocks), down_weight.reshape(blocks)], -1)
    is_valid = (slot < image_counts).astype(jnp.int32)
    onehot = (time_ids[:, 0][:, None] == jnp.arange(times, dtype=jnp.int32)[None, :]).astype(F32)
    embedding = jnp.dot(onehot, table_all, precision=HIGHEST)
    embedded = media[:, 0].astype(F32) + embedding[:, None, :]
    normed_media, inv_media = normalize(embedded)
    hidden_media = (normed_media * media_scale).astype(BF)

    normed_lat, inv_lat = normalize(lat_float)
    hidden_lat = (normed_lat * latent_scale).astype(BF)
    hidden_own = lax.dynamic_slice_in_dim(hidden_lat, first_row, own_rows, 0)
    lat_own = lax.dynamic_slice_in_dim(lat_float, first_row, own_rows, 0)
    query_own = mm_tn(query_weight, hidden_lat.T).astype(BF)
    frame_ids = jnp.arange(grid.frame, dtype=jnp.int32) ^ slot
    query_z = grid.gather(query_own[None], "cz")
    first, *rest = grid.strides(grid.depth)
    mixed_first = grid.step(after(jnp.concatenate([output_weight, grad_out.astype(BF)]), query_z)[None], "z", first)
    mixed_z = mixed_first
    for k in rest:
        mixed_z = grid.step(mixed_z, "z", k)
    query_all = grid.gather(query_z, "ab")
    query_t = query_all.reshape(grid.count, part, grid.frame, own_rows)
    query_places = grid.places("czab")
    query_t = query_t.at[query_places[:, None], :, frame_ids[None, :]].get(mode="promise_in_bounds")
    query_t = query_t.transpose(0, 2, 1, 3).reshape(HEADS, head_dim, lat_rows)
    keyval_ab = grid.gather_ab(keyval_z)
    early = (mixed_z, hidden_media, hidden_own, query_t, feed_got)
    keyval_parts = aligned_parts(grid.gather_core(keyval_ab, *early))
    mixed_z = after(mixed_z, keyval_ab)
    folded, media_scores, own_scores, context_parts = attend(
        order, is_valid, query_t, hidden_media, hidden_own, keyval_parts, factor
    )
    context_parts = context_parts.reshape(HEADS, seq_here, grid.frame, own_rows, LANES)
    pieces = [context_parts[:, :, k].reshape(HEADS, rows, LANES).astype(BF) for k in range(grid.frame)]
    pieces = [pieces[0]] + [grid.to_frame(pieces[k], k) for k in range(1, grid.frame)]
    feed_got = lax.all_to_all(after(feed_got, folded), "seq", 0, 0)
    mixed_ab = grid.gather_ab(mixed_z, folded)
    mixed_parts = grid.gather_core(mixed_ab, pieces)
    if aligned:
        output_parts, grad_parts = mixed_parts, mixed_parts
    else:
        output_parts = aligned_parts([p[:, :part] for p in mixed_parts])
        grad_parts = [p[:, part:] for p in mixed_parts]
    pieces[0] = after(pieces[0], feed_got)
    mixed, normed_feed, hidden_feed, context, context_low = mixer(
        order, lat_own, feed_scale, pieces, output_parts, head_dim
    )

    up_t, down_w = unpack_feed(feed_got)
    feed_parts = grid.gather_core(grid.gather_ab(grid.gather(hidden_feed[None], "z"), up_t))
    half = len(feed_parts) // 2
    far, near = (feed_parts[half:], grad_parts[half:]), (feed_parts[:half], grad_parts[:half])
    far_act, far_grad_up, low, high = feed(up_t, down_w, *far, 2)
    grad_sum = Scatter(grid, low, high)
    near_act, near_grad_up, keep = feed(up_t, down_w, *after(near, high), 1)
    grad_sum.keep(keep)
    grad_sum.to_b()
    spare = part if aligned else 0
    far_up, far_down, low, high = feed_rest(down_w, far_act, after(far_grad_up, keep), *far, spare, 2)
    near_up, near_down, keep = feed_rest(down_w, near_act, after(near_grad_up, high), *near, spare, 1)
    grad_sum.to_a(high)
    grad_sum.to_z(keep)
    back = pack_back(grid.seq, far_up, far_down, near_up, near_down)
    grad_feed = after(grad_sum.result(), back)
    message, grad_mixed, grad_mixed_low, feed_gain_part, residual = unmix(
        order, grad_feed, grad_out, mixed, normed_feed, feed_scale, context, output_parts, head_dim, own_rows
    )
    messages = [message] + [grid.to_frame(message, k) for k in range(1, grid.frame)]
    back = lax.all_to_all(after(back, message), "seq", 0, 0)
    output_context = after(context_low, messages)
    if aligned:
        keep, low, high = output_part_of(place, output_context, grad_mixed_low, keep, low, high)
    else:
        pairs = zip((keep, low, high), scatter_order(output_part_of(place, output_context, grad_mixed_low)))
        keep, low, high = (jnp.concatenate(pair, 1) for pair in pairs)
    mixed_sum = Scatter(grid, low, high)
    mixed_sum.keep(keep)
    messages = after(messages, keep)

    def back_heads(first, count, work, *parts):
        *parts, query_part, grad_media, grad_own = attend_back(
            order, place, slot.reshape(1), query_t, hidden_media, hidden_own, messages, folded, media_scores, own_scores,
            keyval_parts, factor, first, count, work, *parts,
        )
        return parts, (query_part, grad_media, grad_own)

    quarter = HEADS // 4
    parts, sums = back_heads(0, quarter, 2e9)
    parts = after(parts, mixed_sum.high, mixed_sum.arrays)
    mixed_sum.to_b(parts, back)
    parts, more = back_heads(quarter, 2 * quarter, 40e9, *parts)
    sums = [sums, more]
    parts = after(parts, mixed_sum.last())
    mixed_sum.to_a(parts)
    parts, more = back_heads(3 * quarter, quarter, 30e9, *parts)
    sums.append(more)
    query_part = sums[0][0] + sums[1][0] + sums[2][0]
    if not aligned:
        query_part = query_part.reshape(grid.count, part, lat_rows).at[owners].get(mode="promise_in_bounds")
    query_keep, low, high = jnp.split(after(query_part, mixed_sum.last()), quarters)
    query_sum = Scatter(grid, low, high)
    query_sum.keep(query_keep)
    keep, low, high = scatter_order(parts)
    keyval_sum = Scatter(grid, low, high, query_sum.high)
    keyval_sum.keep(keep)
    query_sum.to_b()
    keyval_sum.to_b(query_sum.last())
    query_sum.to_a()
    keyval_b = keyval_sum.last()
    query_sum.to_z(keyval_sum.arrays[0])
    query_sum = query_sum.result().T.astype(BF)
    mixed_sum.to_z(keyval_sum.high)
    sums = after(sums, keyval_sum.high)
    grad_hidden, grad_hidden_own = (sums[0][i] + sums[1][i] + sums[2][i] for i in (1, 2))
    back = after(back, keyval_b)

    media_gain_part = jnp.sum(grad_hidden * normed_media, (0, 1))
    grad_embedded = norm_back(grad_hidden * media_scale, normed_media, inv_media)
    table_part = jnp.dot(onehot.T, jnp.sum(grad_embedded, 1), precision=HIGHEST)

    query_grad = mm_tn(hidden_lat, query_sum)
    grad_lat = mm_nt(query_sum, query_weight)
    grad_lat = grad_lat + lax.dynamic_update_slice_in_dim(jnp.zeros_like(grad_lat), grad_hidden_own, first_row, 0)
    latent_gain_part = jnp.sum(grad_lat * normed_lat, 0)
    latents_part = norm_back(grad_lat * latent_scale, normed_lat, inv_lat)
    latents_part = latents_part + lax.dynamic_update_slice_in_dim(
        jnp.zeros_like(latents_part), residual, first_row, 0
    )
    smalls = jnp.concatenate(
        [
            latents_part,
            table_part,
            media_gain_part[None],
            latent_gain_part[None],
            feed_gain_part,
            jnp.zeros((pad, width), F32),
        ]
    ).astype(BF)
    keyval_sum.to_a()
    keyval_sum.to_z()
    smalls = smalls.T.reshape(grid.count, part, -1).at[grid.owners("cabz")].get(mode="promise_in_bounds")
    small_sum = grid.scatter_core_last(after(smalls, keyval_b)).T
    up_grad_t, down_grad = unpack_back(back)
    up_grad = up_grad_t.T
    keyval_grad = keyval_sum.result().T
    mixed_sums = mixed_sum.result()
    new_latents = (mixed + mixed_sums[:rows]).reshape(seq_here, own_rows, width)
    output_grad = mixed_sums[rows:]
    latents_grad = small_sum[:lat_rows]
    table_grad = small_sum[lat_rows : lat_rows + times]
    media_gain_grad, latent_gain_grad, feed_gain_grad = (small_sum[lat_rows + times + i] for i in range(3))
    return (
        new_latents,
        grad_embedded[:, None],
        latents_grad,
        table_grad,
        media_gain_grad,
        latent_gain_grad,
        feed_gain_grad,
        query_grad,
        keyval_grad,
        output_grad,
        up_grad,
        down_grad,
    )


def solution(mesh):
    grid = Grid(mesh.shape["seq"], mesh.shape["frame"])

    def run(*args):
        return local(grid, *args)

    return jax.shard_map(
        run,
        mesh=mesh,
        in_specs=(
            P("seq", "frame", None, None),
            P("seq"),
            P("seq", "frame"),
            P(None, BOTH),
            P(None, BOTH),
            P(BOTH),
            P(BOTH),
            P(BOTH),
            P(None, BOTH),
            P(None, BOTH),
            P(BOTH, None),
            P("seq", "frame"),
            P("frame", "seq"),
            P("seq", "frame", None),
        ),
        out_specs=(
            P("seq", "frame", None),
            P("seq", "frame", None, None),
            P(None, BOTH),
            P(None, BOTH),
            P(BOTH),
            P(BOTH),
            P(BOTH),
            P(None, BOTH),
            P(None, BOTH),
            P(BOTH, None),
            P("seq", "frame"),
            P("frame", "seq"),
        ),
        check_vma=False,
    )
```

```python
import functools

import jax
import jax.numpy as jnp
from jax import lax
from jax.experimental import pallas as pl
from jax.experimental.pallas import tpu as pltpu
from jax.sharding import PartitionSpec as P

HEADS = 16
EPS = 1e-05
NEGATIVE = -1e30
HIGHEST = lax.Precision.HIGHEST
BF = jnp.bfloat16
F32 = jnp.float32
BOTH = ("seq", "frame")


def normalize(values):
    center = values - jnp.mean(values, -1, keepdims=True)
    scale_inv = lax.rsqrt(jnp.mean(center * center, -1, keepdims=True) + EPS)
    return (center * scale_inv, scale_inv)


def norm_back(grad_hat, normed, scale_inv):
    return scale_inv * (
        grad_hat
        - jnp.mean(grad_hat, -1, keepdims=True)
        - normed * jnp.mean(grad_hat * normed, -1, keepdims=True)
    )


def mm(a, b):
    return jnp.dot(a, b, preferred_element_type=F32)


def mm_tn(a, b):
    return lax.dot_general(a, b, (((0,), (0,)), ((), ())), preferred_element_type=F32)


def mm_nt(a, b):
    return lax.dot_general(a, b, (((1,), (1,)), ((), ())), preferred_element_type=F32)


def ein(spec, a, b):
    return jnp.einsum(spec, a, b, preferred_element_type=F32)


def exact_gelu(values):
    return jax.nn.gelu(values, approximate=False)


def bits(n):
    return n.bit_length() - 1


class Grid:
    def __init__(self, seq_count, frame_count):
        self.seq, self.frame = seq_count, frame_count
        self.side = frame_count // 2
        self.depth = seq_count // self.side
        self.count = seq_count * frame_count

    def split(self, lin):
        side = bits(self.side)
        return lin >> (2 * side + 1), (lin >> (side + 1)) & (self.side - 1), (lin >> 1) & (self.side - 1), lin & 1

    def join(self, z, x, y, c):
        return ((z * self.side + x) * self.side + y) * 2 + c

    def send(self, value, move):
        perm = [(i, self.join(*move(*self.split(i)))) for i in range(self.count)]
        return lax.ppermute(value, BOTH, perm)

    def to_z(self, v, k):
        return self.send(v, lambda z, x, y, c: (z ^ k, x, y, c))

    def to_a(self, v, k):
        return self.send(v, lambda z, x, y, c: (z, x, y ^ k, c) if c else (z, x ^ k, y, c))

    def to_b(self, v, k):
        return self.send(v, lambda z, x, y, c: (z, x ^ k, y, c) if c else (z, x, y ^ k, c))

    def to_x(self, v, k):
        return self.send(v, lambda z, x, y, c: (z, x ^ k, y, c))

    def to_core(self, v):
        return self.send(v, lambda z, x, y, c: (z, x, y, 1 - c))

    def to_frame(self, v, k):
        def move(z, x, y, c):
            f = (y * 2 + c) ^ k
            return z, x, f // 2, f % 2

        return self.send(v, move)

    def own(self):
        return lax.axis_index("seq") * self.frame + lax.axis_index("frame")

    def scatter_core_last(self, v):
        for send, size in ((self.to_z, self.depth), (self.to_b, self.side), (self.to_a, self.side)):
            for k in reversed(self.strides(size)):
                half = v.shape[0] // 2
                v = v[:half].astype(F32) + send(v[half:].astype(BF), k).astype(F32)
        return v[0] + self.to_core(v[1].astype(BF)).astype(F32)

    def strides(self, size):
        return [1 << t for t in reversed(range(bits(size)))]

    def places(self, steps="zabc"):
        z, x, y, c = self.split(self.own())
        oz, ox, oy, oc = self.split(jnp.arange(self.count, dtype=jnp.int32))
        way = oc if steps[-1] == "c" else c
        rx, ry = ox ^ x, oy ^ y
        fields = {
            "z": (oz ^ z, self.depth),
            "a": (jnp.where(way == 0, rx, ry), self.side),
            "b": (jnp.where(way == 0, ry, rx), self.side),
            "c": (oc ^ c, 2),
        }
        place, bit = 0, 0
        for step in steps:
            value, size = fields[step]
            for k in self.strides(size):
                place = place + ((value & k != 0).astype(jnp.int32) << bit)
                bit += 1
        return place

    def owners(self, steps="zabc"):
        order = jnp.arange(self.count, dtype=jnp.int32)
        return jnp.zeros_like(order).at[self.places(steps)].set(order, unique_indices=True)

    def step(self, v, kind, k):
        send = {"z": self.to_z, "a": self.to_a, "b": self.to_b, "c": lambda p, _: self.to_core(p)}[kind]
        return jnp.concatenate([v, send(v, k)])

    def gather(self, v, steps):
        for kind in steps:
            for k in self.strides({"z": self.depth, "c": 2}.get(kind, self.side)):
                v = self.step(v, kind, k)
        return v

    def gather_ab(self, v, *others):
        v = [v]
        for k in self.strides(self.side):
            v = v + [self.to_a(p, k) for p in v]
        for k in self.strides(self.side):
            own = self.to_b(v[0], k)
            v = v + [own] + [self.to_b(after(p, own, others), k) for p in v[1:]]
        return v

    def gather_core(self, v, *others):
        return v + [self.to_core(p) for p in v[:-1]] + [self.to_core(after(v[-1], others))]


class Scatter:
    def __init__(self, grid, low, high, *others):
        self.grid = grid
        self.size = 2 * low.shape[0]
        low, high = after((low, high), others)
        self.high, self.arrays = [grid.to_core(high)], [grid.to_core(low)]

    def keep(self, keep):
        half = self.size // 2
        self.high.append(keep[half:])
        self.arrays.append(keep)

    def sum(self, lo, hi):
        arrays = self.arrays
        if hi > self.arrays[0].shape[0]:
            arrays, lo, hi = self.high, 0, hi - lo
        return sum(p[lo:hi].astype(F32) for p in arrays)

    def step(self, send, strides, *others):
        for k in strides:
            half = self.size // 2
            self.arrays.append(send(after(self.sum(half, self.size).astype(BF), others), k))
            self.size = half

    def to_b(self, *others):
        self.step(self.grid.to_b, self.grid.strides(self.grid.side)[::-1], *others)

    def to_a(self, *others):
        self.step(self.grid.to_a, self.grid.strides(self.grid.side)[::-1], *others)

    def to_z(self, *others, first=True, rest=True):
        strides = self.grid.strides(self.grid.depth)[::-1]
        self.step(self.grid.to_z, (strides[:1] if first else []) + (strides[1:] if rest else []), *others)

    def last(self):
        return self.arrays[-1]

    def result(self):
        return self.sum(0, 1)[0]


def after(value, *others):
    return lax.optimization_barrier((value, others))[0]


def load_blocks(order_ref, part_refs, store_ref, sem_ref):
    rows = store_ref.shape[1]
    copies = []
    for part in part_refs:
        for k in range(part.shape[0]):
            n = len(copies)
            block = part.at[k] if part.shape[1] == rows else part.at[k, pl.ds(0, rows)]
            copies.append(pltpu.make_async_copy(block, store_ref.at[order_ref[n]], sem_ref.at[n]))
    return copies


def place_copy(place_ref, block, source_ref, target_refs, sem_ref):
    place = place_ref[block]
    first = 0
    for target in target_refs:
        index, size = place - first, target.shape[0]
        first += size

        @pl.when((index >= 0) & (index < size))
        def _():
            pltpu.make_async_copy(source_ref, target.at[index], sem_ref).start()


def dot(a, b):
    return lax.dot_general(a, b, (((1,), (0,)), ((), ())), preferred_element_type=F32)


def pieces_of(value):
    high = value.astype(BF).astype(F32)
    middle = (value - high).astype(BF).astype(F32)
    return high, middle, value - high - middle


def whole(shape):
    return pl.BlockSpec(shape, lambda *_: (0,) * len(shape))


SMEM = pl.BlockSpec(memory_space=pltpu.SMEM)
ANYWHERE = pl.BlockSpec(memory_space=pltpu.HBM)
LANES = 128


def params(mib):
    return pltpu.CompilerParams(vmem_limit_bytes=mib * 1024 * 1024)


def cost(flops, moved):
    return pl.CostEstimate(flops=int(flops), bytes_accessed=int(moved), transcendentals=0)


def attend_kernel(sizes, order_ref, valid_ref, query_ref, media_ref, own_ref, *refs):
    heads, group, seqs, lat, factor, part_count = sizes
    parts = refs[:part_count]
    folded_ref, score_ref, own_score_ref, context_ref, weight_ref, mix_ref, sem_ref = refs[part_count:]
    step = pl.program_id(0)
    head_dim = weight_ref.shape[1]

    @pl.when(step == 0)
    def _():
        copies = load_blocks(order_ref, parts, weight_ref, sem_ref)
        for c in copies:
            c.start()
        for c in copies:
            c.wait()

    for j in range(group):
        h = step * group + j
        folded = mm_tn(query_ref[h], weight_ref[h]) * factor
        folded_ref[j * lat : (j + 1) * lat, :] = folded.astype(BF)
    queries = folded_ref[...]
    own = own_ref[...]
    own_scores = mm_nt(queries, own)
    own_score_ref[...] = own_scores
    own_top = jnp.max(own_scores, -1, keepdims=True)
    lanes = lax.broadcasted_iota(jnp.int32, (group * lat, LANES), 1)
    for s in range(seqs):
        media = media_ref[s]
        scores = mm_nt(queries, media)
        scores = jnp.where(valid_ref[s] > 0, scores, NEGATIVE)
        score_ref[s] = scores
        top = jnp.maximum(jnp.max(scores, -1, keepdims=True), own_top)
        media_exp = jnp.exp(scores - top)
        own_exp = jnp.exp(own_scores - top)
        total = jnp.sum(media_exp, -1, keepdims=True) + jnp.sum(own_exp, -1, keepdims=True)
        mix = dot(media_exp.astype(BF), media) + dot(own_exp.astype(BF), own)
        mix = (mix * (1.0 / total)).astype(BF)
        stats = jnp.zeros(lanes.shape, F32)
        for i, piece in enumerate(pieces_of(top) + pieces_of(total)):
            stats = jnp.where(lanes == head_dim + i, piece, stats)
        for j in range(group):
            mix_ref[j, s * lat : (s + 1) * lat, :] = mix[j * lat : (j + 1) * lat, :]
            context_ref[j, s * lat : (s + 1) * lat, head_dim:] = stats[j * lat : (j + 1) * lat, head_dim:]
    for j in range(group):
        h = step * group + j
        context_ref[j, :, :head_dim] = mm_nt(mix_ref[j], weight_ref[heads + h])


def attend(order, valid, query_t, hidden_media, hidden_own, parts, factor):
    heads, head_dim, lat = query_t.shape
    seqs, patches, width = hidden_media.shape
    group = 4
    own = hidden_own.shape[0]
    rows = group * lat
    return pl.pallas_call(
        functools.partial(attend_kernel, (heads, group, seqs, lat, factor, len(parts))),
        grid=(heads // group,),
        in_specs=[SMEM, SMEM, whole(query_t.shape), whole(hidden_media.shape), whole(hidden_own.shape)]
        + [ANYWHERE] * len(parts),
        out_specs=[
            pl.BlockSpec((rows, width), lambda i: (i, 0)),
            pl.BlockSpec((seqs, rows, patches), lambda i: (0, i, 0)),
            pl.BlockSpec((rows, own), lambda i: (i, 0)),
            pl.BlockSpec((group, seqs * lat, LANES), lambda i: (i, 0, 0)),
        ],
        out_shape=[
            jax.ShapeDtypeStruct((heads * lat, width), BF),
            jax.ShapeDtypeStruct((seqs, heads * lat, patches), F32),
            jax.ShapeDtypeStruct((heads * lat, own), F32),
            jax.ShapeDtypeStruct((heads, seqs * lat, LANES), F32),
        ],
        scratch_shapes=[
            pltpu.VMEM((2 * heads, head_dim, width), BF),
            pltpu.VMEM((group, seqs * lat, width), BF),
            pltpu.SemaphoreType.DMA((2 * heads,)),
        ],
        compiler_params=params(56),
        cost_estimate=cost(2e9, 2e6),
        name="attend",
    )(order, valid, query_t, hidden_media, hidden_own, *parts)


def mixer_kernel(sizes, order_ref, latent_ref, gain_ref, *refs):
    heads, head_dim, seqs, piece_count, part_count = sizes
    pieces = refs[:piece_count]
    parts = refs[piece_count : piece_count + part_count]
    mixed_ref, normed_ref, hidden_ref, context_ref, low_ref, weight_ref, sem_ref = refs[piece_count + part_count :]
    copies = load_blocks(order_ref, parts, weight_ref, sem_ref)
    for c in copies:
        c.start()
    values = [p[...].astype(F32) for p in pieces]
    at = head_dim
    tops = [v[..., at : at + 1] + v[..., at + 1 : at + 2] + v[..., at + 2 : at + 3] for v in values]
    totals = [v[..., at + 3 : at + 4] + v[..., at + 4 : at + 5] + v[..., at + 5 : at + 6] for v in values]
    top = functools.reduce(jnp.maximum, tops)
    shares = [t * jnp.exp(p - top) for t, p in zip(totals, tops)]
    total = functools.reduce(lambda p, q: p + q, shares)
    context = functools.reduce(lambda p, q: p + q, [v * (w / total) for v, w in zip(values, shares)])
    lanes = lax.broadcasted_iota(jnp.int32, context.shape, 2)
    context_ref[...] = jnp.where(lanes == head_dim, top + jnp.log(total), context)
    for h in range(heads):
        low_ref[:, h * head_dim : (h + 1) * head_dim] = context[h, :, :head_dim].astype(BF)
    for c in copies:
        c.wait()
    weight = weight_ref[...].reshape(heads * head_dim, -1)
    mixed = jnp.concatenate([latent_ref[...]] * seqs) + dot(low_ref[...], weight)
    mixed_ref[...] = mixed
    center = mixed - jnp.mean(mixed, -1, keepdims=True)
    normed = center * lax.rsqrt(jnp.mean(center * center, -1, keepdims=True) + EPS)
    normed_ref[...] = normed
    hidden_ref[...] = (normed * gain_ref[...]).astype(BF)


def mixer(order, latent_own, gain, pieces, parts, head_dim):
    heads, rows, _ = pieces[0].shape
    own_rows, width = latent_own.shape
    count = sum(p.shape[0] for p in parts)
    block = heads * head_dim // count
    sizes = (heads, head_dim, rows // own_rows, len(pieces), len(parts))
    return pl.pallas_call(
        functools.partial(mixer_kernel, sizes),
        in_specs=[SMEM, whole(latent_own.shape), whole(gain.shape)]
        + [whole(p.shape) for p in pieces]
        + [ANYWHERE] * len(parts),
        out_specs=[whole((rows, width))] * 3 + [whole((heads, rows, LANES)), whole((rows, heads * head_dim))],
        out_shape=[
            jax.ShapeDtypeStruct((rows, width), F32),
            jax.ShapeDtypeStruct((rows, width), F32),
            jax.ShapeDtypeStruct((rows, width), BF),
            jax.ShapeDtypeStruct((heads, rows, LANES), F32),
            jax.ShapeDtypeStruct((rows, heads * head_dim), BF),
        ],
        scratch_shapes=[pltpu.VMEM((count, block, width), BF), pltpu.SemaphoreType.DMA((count,))],
        compiler_params=params(60),
        cost_estimate=cost(1e6, 1e6),
        name="mixer",
    )(order, latent_own, gain, *pieces, *parts)


def unmix_kernel(sizes, order_ref, grad_feed_ref, grad_out_ref, mixed_ref, normed_ref, gain_ref, context_ref, *refs):
    heads, head_dim, seqs, part_count = sizes
    parts = refs[:part_count]
    message_ref, grad_mixed_ref, low_ref, gain_grad_ref, residual_ref, weight_ref, sem_ref = refs[part_count:]
    copies = load_blocks(order_ref, parts, weight_ref, sem_ref)
    for c in copies:
        c.start()
    mixed = mixed_ref[...]
    center = mixed - jnp.mean(mixed, -1, keepdims=True)
    scale_inv = lax.rsqrt(jnp.mean(center * center, -1, keepdims=True) + EPS)
    normed = normed_ref[...]
    grad_feed = grad_feed_ref[...]
    gain_grad_ref[...] = jnp.sum(grad_feed * normed, 0, keepdims=True)
    grad_mixed = grad_out_ref[...] + norm_back(grad_feed * gain_ref[...], normed, scale_inv)
    grad_mixed_ref[...] = grad_mixed
    own = residual_ref.shape[0]
    residual_ref[...] = sum(grad_mixed[s * own : (s + 1) * own] for s in range(seqs))
    low = grad_mixed.astype(BF)
    low_ref[...] = low
    for c in copies:
        c.wait()
    grads = mm_nt(low, weight_ref[...].reshape(heads * head_dim, -1)).astype(BF)
    lanes = lax.broadcasted_iota(jnp.int32, (low.shape[0], LANES), 1)
    for h in range(heads):
        grad = grads[:, h * head_dim : (h + 1) * head_dim]
        context = context_ref[h]
        row = jnp.sum(grad.astype(F32) * context[:, :head_dim], -1, keepdims=True)
        log_total = context[:, head_dim : head_dim + 1]
        message = jnp.zeros(lanes.shape, F32)
        for i, piece in enumerate(pieces_of(row) + pieces_of(log_total)):
            message = jnp.where(lanes == head_dim + i, piece, message)
        message_ref[h] = message.astype(BF)
        message_ref[h, :, :head_dim] = grad


def unmix(order, grad_feed, grad_out, mixed, normed, gain, context, parts, head_dim, own_rows):
    heads, rows, _ = context.shape
    width = mixed.shape[1]
    count = sum(p.shape[0] for p in parts)
    block = heads * head_dim // count
    sizes = (heads, head_dim, rows // own_rows, len(parts))
    arrays = (grad_feed, grad_out, mixed, normed, gain, context)
    shapes = [((heads, rows, LANES), BF), ((rows, width), F32), ((rows, width), BF), ((1, width), F32), ((own_rows, width), F32)]
    return pl.pallas_call(
        functools.partial(unmix_kernel, sizes),
        in_specs=[SMEM] + [whole(a.shape) for a in arrays] + [ANYWHERE] * len(parts),
        out_specs=[whole(shape) for shape, _ in shapes],
        out_shape=[jax.ShapeDtypeStruct(*item) for item in shapes],
        scratch_shapes=[pltpu.VMEM((count, block, width), BF), pltpu.SemaphoreType.DMA((count,))],
        compiler_params=params(60),
        cost_estimate=cost(2e9, 8e6),
        name="unmix",
    )(order, *arrays, *parts)


def output_part_kernel(groups, place_ref, context_ref, low_ref, *refs):
    *targets, out_ref, sem_ref = refs[-5:]
    low = low_ref[...]
    per = out_ref.shape[0] // groups
    part = context_ref.shape[1] // groups
    rows = out_ref.shape[1]
    targets = [t.at[:, pl.ds(t.shape[1] - rows, rows)] for t in targets]
    for g in range(groups):
        value = mm_tn(context_ref[:, g * part : (g + 1) * part], low).astype(BF)
        out_ref[g * per : (g + 1) * per] = value.reshape((per,) + out_ref.shape[1:])
        for i in range(g * per, (g + 1) * per):
            place_copy(place_ref, i, out_ref.at[i], targets, sem_ref.at[i])
    for i in range(out_ref.shape[0]):
        pltpu.make_async_copy(out_ref.at[i], targets[0].at[0], sem_ref.at[i]).wait()


def output_part_of(place, context, low, *halves):
    width = low.shape[1]
    count = place.shape[0]
    block = context.shape[1] // count
    shapes = [h.shape for h in halves] or [(n, block, width) for n in (count // 2, count // 4, count // 4)]
    return pl.pallas_call(
        functools.partial(output_part_kernel, 4),
        in_specs=[SMEM, whole(context.shape), whole(low.shape)] + [ANYWHERE] * len(halves),
        out_specs=[ANYWHERE] * 3,
        out_shape=[jax.ShapeDtypeStruct(shape, BF) for shape in shapes],
        input_output_aliases={3: 0, 4: 1, 5: 2} if halves else {},
        scratch_shapes=[pltpu.VMEM((count, block, width), BF), pltpu.SemaphoreType.DMA((count,))],
        compiler_params=params(60),
        cost_estimate=cost(1e9, 2e6),
        name="output_part",
    )(place, context, low, *halves)


def unpack_feed_kernel(got_ref, up_ref, down_ref):
    part = got_ref.shape[-1] // 2
    for s in range(got_ref.shape[0]):
        up_ref[:, s * part : (s + 1) * part] = got_ref[s, :, :part]
        down_ref[:, s * part : (s + 1) * part] = got_ref[s, :, part:]


def unpack_feed(got):
    count, hid, part = got.shape
    out = (hid, count * part // 2)
    return pl.pallas_call(
        unpack_feed_kernel,
        in_specs=[whole(got.shape)],
        out_specs=[whole(out)] * 2,
        out_shape=[jax.ShapeDtypeStruct(out, BF)] * 2,
        cost_estimate=cost(0, 3e6),
        name="unpack_feed",
    )(got)


def pack_back_kernel(far_up_ref, far_down_ref, near_up_ref, near_down_ref, out_ref):
    part = out_ref.shape[-1] // 2
    for s in range(out_ref.shape[0]):
        at = slice(s * part, (s + 1) * part)
        out_ref[s, :, :part] = (far_up_ref[:, at] + near_up_ref[:, at]).astype(BF)
        out_ref[s, :, part:] = (far_down_ref[:, at] + near_down_ref[:, at]).astype(BF)


def pack_back(count, *grads):
    hid, width = grads[0].shape
    out = (count, hid, 2 * width // count)
    return pl.pallas_call(
        pack_back_kernel,
        in_specs=[whole(g.shape) for g in grads],
        out_specs=whole(out),
        out_shape=jax.ShapeDtypeStruct(out, BF),
        cost_estimate=cost(0, 6e6),
        name="pack_back",
    )(*grads)


def unpack_back_kernel(got_ref, up_ref, down_ref):
    hid, part = got_ref.shape[1], got_ref.shape[2] // 2
    for s in range(got_ref.shape[0]):
        up_ref[s * hid : (s + 1) * hid, :] = got_ref[s, :, :part].astype(F32)
        down_ref[s * hid : (s + 1) * hid, :] = got_ref[s, :, part:].astype(F32)


def unpack_back(got):
    count, hid, part = got.shape
    out = (count * hid, part // 2)
    return pl.pallas_call(
        unpack_back_kernel,
        in_specs=[whole(got.shape)],
        out_specs=[whole(out)] * 2,
        out_shape=[jax.ShapeDtypeStruct(out, F32)] * 2,
        cost_estimate=cost(0, 5e6),
        name="unpack_back",
    )(got)


ROOT_HALF = 0.5**0.5
DENSITY = 1 / (2 * 3.141592653589793) ** 0.5


def loads(parts, rows, store_ref, sem_ref):
    out, n = [], 0
    for part in parts:
        skip = part.shape[1] - rows
        copies = []
        for k in range(part.shape[0]):
            block = part.at[k, pl.ds(skip, rows)] if skip else part.at[k]
            copies.append(pltpu.make_async_copy(block, store_ref.at[n], sem_ref.at[n]))
            n += 1
        out.append(copies)
    return out


def start(copies):
    for c in copies:
        c.start()


def wait(copies):
    for c in copies:
        c.wait()


def feed_kernel(part_count, up_ref, down_ref, *refs):
    feed, grad = refs[:part_count], refs[part_count : 2 * part_count]
    act_ref, grad_up_ref, *out_refs = refs[2 * part_count : -6]
    feed_st, grad_st, out_st, feed_sem, grad_sem, out_sem = refs[-6:]
    each = part_count // len(out_refs)
    n, per, width = feed[0].shape
    chunk = n * per
    feeds, grads = loads(feed, per, feed_st, feed_sem), loads(grad, per, grad_st, grad_sem)
    for i in range(part_count):
        start(feeds[i])
        start(grads[i])
    up, down = up_ref[...], down_ref[...]
    outs = []
    each, n, chunk = each // 2, 2 * n, 2 * chunk
    for i in range(part_count // 2):
        at = slice(i * n, (i + 1) * n)
        wait(feeds[2 * i] + feeds[2 * i + 1])
        pre = mm_nt(feed_st[at].reshape(chunk, width), up)
        wait(grads[2 * i] + grads[2 * i + 1])
        grad_act = mm_nt(grad_st[at].reshape(chunk, width), down)
        cdf = 0.5 * (1.0 + lax.erf(pre * ROOT_HALF))
        slope = cdf + pre * (jnp.exp(-0.5 * pre * pre) * DENSITY)
        act_ref[i * chunk : (i + 1) * chunk, :] = (pre * cdf).astype(BF)
        grad_up = (grad_act * slope).astype(BF)
        grad_up_ref[i * chunk : (i + 1) * chunk, :] = grad_up
        out_st[at] = dot(grad_up, up).astype(BF).reshape(n, per, width)
        to = out_refs[i // each].at[pl.ds(i % each * n, n)]
        outs.append(pltpu.make_async_copy(out_st.at[pl.ds(i * n, n)], to, out_sem.at[i]))
        outs[i].start()
    wait(outs)


def feed(up, down, feed_parts, grad_parts, splits):
    hid, width = up.shape
    count = len(feed_parts)
    n, per, _ = feed_parts[0].shape
    rows = count * n * per
    store = pltpu.VMEM((count * n, per, width), BF)
    sems = pltpu.SemaphoreType.DMA((count * n,))
    return pl.pallas_call(
        functools.partial(feed_kernel, count),
        in_specs=[whole(up.shape), whole(down.shape)] + [ANYWHERE] * (2 * count),
        out_specs=[whole((rows, hid))] * 2 + [ANYWHERE] * splits,
        out_shape=[jax.ShapeDtypeStruct((rows, hid), BF)] * 2
        + [jax.ShapeDtypeStruct((count * n // splits, per, width), BF)] * splits,
        scratch_shapes=[store] * 3 + [sems] * 3,
        compiler_params=params(60),
        cost_estimate=cost(5e9, 8e6),
        name="feed",
    )(up, down, *feed_parts, *grad_parts)


def feed_rest_kernel(part_count, down_ref, act_ref, grad_up_ref, *refs):
    feed, grad = refs[:part_count], refs[part_count : 2 * part_count]
    up_grad_ref, down_grad_ref, *out_refs = refs[2 * part_count : -6]
    feed_st, grad_st, out_st, feed_sem, grad_sem, out_sem = refs[-6:]
    each = part_count // len(out_refs)
    n, per, width = feed[0].shape
    chunk = n * per
    feeds, grads = loads(feed, per, feed_st, feed_sem), loads(grad, per, grad_st, grad_sem)
    for i in range(part_count):
        start(grads[i])
        start(feeds[i])
    down = down_ref[...]
    first = pl.ds(0, per)
    outs = []
    for i in range(part_count):
        at = slice(i * n, (i + 1) * n)
        act = act_ref[i * chunk : (i + 1) * chunk, :]
        out_st[at] = dot(act, down).astype(BF).reshape(n, per, width)
        to = out_refs[i // each].at[pl.ds(i % each * n, n), first]
        outs.append(pltpu.make_async_copy(out_st.at[pl.ds(i * n, n)], to, out_sem.at[i]))
        outs[i].start()
    for i in range(part_count):
        wait(feeds[i])
        wait(grads[i])
    up_grad_ref[...] = mm_tn(grad_up_ref[...], feed_st[...].reshape(part_count * chunk, width))
    down_grad_ref[...] = mm_tn(act_ref[...], grad_st[...].reshape(part_count * chunk, width))
    wait(outs)


def feed_rest(down, act, grad_up, feed_parts, grad_parts, spare, splits):
    hid, width = down.shape
    count = len(feed_parts)
    n, per, _ = feed_parts[0].shape
    store = pltpu.VMEM((count * n, per, width), BF)
    sems = pltpu.SemaphoreType.DMA((count * n,))
    return pl.pallas_call(
        functools.partial(feed_rest_kernel, count),
        in_specs=[whole(down.shape), whole(act.shape), whole(grad_up.shape)] + [ANYWHERE] * (2 * count),
        out_specs=[whole((hid, width))] * 2 + [ANYWHERE] * splits,
        out_shape=[jax.ShapeDtypeStruct((hid, width), F32)] * 2
        + [jax.ShapeDtypeStruct((count * n // splits, per + spare, width), BF)] * splits,
        scratch_shapes=[store] * 3 + [sems] * 3,
        compiler_params=params(48),
        cost_estimate=cost(5e9, 8e6),
        name="feed_rest",
    )(down, act, grad_up, *feed_parts, *grad_parts)


def attend_back_kernel(sizes, order_ref, place_ref, slot_ref, query_ref, media_ref, own_ref, *refs):
    heads, group, seqs, lat, factor, piece_count, part_count, first, count = sizes
    pieces = refs[:piece_count]
    folded_ref, score_ref, own_score_ref = refs[piece_count : piece_count + 3]
    parts = refs[piece_count + 3 : piece_count + 3 + part_count]
    refs = refs[piece_count + 3 + part_count :]
    (
        keep_ref,
        low_ref,
        high_ref,
        query_part_ref,
        grad_media_ref,
        grad_own_ref,
        weight_ref,
        mix_ref,
        gp_ref,
        grad_ref,
        out_ref,
        key_mix_ref,
        sem_ref,
        out_sem_ref,
    ) = refs[-14:]
    step = pl.program_id(0)
    head_dim = weight_ref.shape[1]
    own_rows = own_ref.shape[0]

    def out_wait():
        for slot in range(2 * group):
            pltpu.make_async_copy(out_ref.at[slot], keep_ref.at[0], out_sem_ref.at[slot]).wait()

    @pl.when(step == 0)
    def _():
        loads_here = []
        for part in parts:
            for k in range(part.shape[0]):
                n = len(loads_here)
                block = order_ref[n]
                head = block & (heads - 1)
                here = (head >= first) & (head < first + count)
                to = jnp.where(here, head - first + jnp.where(block >= heads, count, 0), 0)
                copy = pltpu.make_async_copy(part.at[k], weight_ref.at[to], sem_ref.at[n])
                loads_here.append((here, copy))
        for here, c in loads_here:
            pl.when(here)(c.start)
        grad_media_ref[...] = jnp.zeros_like(grad_media_ref)
        grad_own_ref[...] = jnp.zeros_like(grad_own_ref)
        query_part_ref[...] = jnp.zeros_like(query_part_ref)
        for here, c in loads_here:
            pl.when(here)(c.wait)

    columns = []
    for j in range(group):
        h = step * group + j
        for s in range(seqs):
            for k in range(piece_count):
                at = s * lat + k * own_rows
                grad_ref[j, at : at + own_rows, :] = pieces[k][first + h, s * own_rows : (s + 1) * own_rows, :]
        message = grad_ref[j].astype(F32)
        column = [message[:, head_dim + i : head_dim + i + 1] for i in range(6)]
        columns.append((column[0] + column[1] + column[2], column[3] + column[4] + column[5]))
        lifted = dot(grad_ref[j, :, :head_dim], weight_ref[count + h]).astype(BF)
        for s in range(seqs):
            gp_ref[s, j * lat : (j + 1) * lat, :] = lifted[s * lat : (s + 1) * lat, :]
    queries = folded_ref[...]
    own = own_ref[...]
    own_scores = own_score_ref[...]
    key_mix = jnp.zeros(queries.shape, F32)
    own_sum = jnp.zeros(own_scores.shape, F32)
    for s in range(seqs):
        media = media_ref[s]
        lifted = gp_ref[s]
        row_term, log_total = (
            jnp.concatenate([columns[j][i][s * lat : (s + 1) * lat] for j in range(group)]) for i in range(2)
        )
        probs = jnp.exp(score_ref[s] - log_total)
        own_probs = jnp.exp(own_scores - log_total)
        ds = (probs * (mm_nt(lifted, media) - row_term)).astype(BF)
        own_ds = (own_probs * (mm_nt(lifted, own) - row_term)).astype(BF)
        probs, own_probs = probs.astype(BF), own_probs.astype(BF)
        key_mix = key_mix + dot(ds, media)
        own_sum = own_sum + own_ds.astype(F32)
        mix = (dot(probs, media) + dot(own_probs, own)).astype(BF)
        for j in range(group):
            mix_ref[j, s * lat : (s + 1) * lat, :] = mix[j * lat : (j + 1) * lat, :]
        pair = jnp.concatenate([queries, lifted])
        grad_media_ref[s] += mm_tn(jnp.concatenate([ds, probs]), pair)
        grad_own_ref[...] += mm_tn(jnp.concatenate([own_ds, own_probs]), pair)
    key_mix = key_mix + dot(own_sum.astype(BF), own)
    key_mix_ref[...] = (key_mix * factor).astype(BF)
    per = query_part_ref.shape[0] // heads
    pl.when(step > 0)(out_wait)
    for j in range(group):
        h = step * group + j
        mixed = key_mix_ref[j * lat : (j + 1) * lat, :]
        sorted_rows = [
            key_mix_ref[pl.ds(pl.multiple_of(j * lat + (k ^ slot_ref[0]) * own_rows, own_rows), own_rows), :]
            for k in range(piece_count)
        ]
        part = mm_nt(weight_ref[h], jnp.concatenate(sorted_rows)).astype(BF)
        for i in range(per):
            rows = head_dim // per
            query_part_ref[place_ref[(first + h) * per + i]] = part[i * rows : (i + 1) * rows]
        out_ref[2 * j] = dot(query_ref[first + h], mixed).astype(BF)
        out_ref[2 * j + 1] = mm_tn(grad_ref[j, :, :head_dim], mix_ref[j]).astype(BF)
        for i in range(2):
            slot = 2 * j + i
            place_copy(
                place_ref, first + h + i * heads, out_ref.at[slot], (keep_ref, low_ref, high_ref), out_sem_ref.at[slot]
            )
    pl.when(step == pl.num_programs(0) - 1)(out_wait)


def attend_back(order, place, slot, query_t, hidden_media, hidden_own, pieces, folded, scores, own_scores, parts, factor, first, count, work, *halves):
    heads, head_dim, lat = query_t.shape
    seqs, patches, width = hidden_media.shape
    group = 4
    own = hidden_own.shape[0]
    block = group * lat
    sizes = (heads, group, seqs, lat, factor, len(pieces), len(parts), first, count)
    skip = first // group
    position = 9 + len(pieces) + len(parts)
    return pl.pallas_call(
        functools.partial(attend_back_kernel, sizes),
        grid=(count // group,),
        in_specs=[SMEM, SMEM, SMEM, whole(query_t.shape), whole(hidden_media.shape), whole(hidden_own.shape)]
        + [whole(p.shape) for p in pieces]
        + [
            pl.BlockSpec((block, width), lambda i: (i + skip, 0)),
            pl.BlockSpec((seqs, block, patches), lambda i: (0, i + skip, 0)),
            pl.BlockSpec((block, own), lambda i: (i + skip, 0)),
        ]
        + [ANYWHERE] * (len(parts) + len(halves)),
        out_specs=[
            ANYWHERE,
            ANYWHERE,
            ANYWHERE,
            whole((2 * heads, head_dim // 2, lat)),
            whole(hidden_media.shape),
            whole(hidden_own.shape),
        ],
        out_shape=[
            jax.ShapeDtypeStruct((heads, head_dim, width), BF),
            jax.ShapeDtypeStruct((heads // 2, head_dim, width), BF),
            jax.ShapeDtypeStruct((heads // 2, head_dim, width), BF),
            jax.ShapeDtypeStruct((2 * heads, head_dim // 2, lat), BF),
            jax.ShapeDtypeStruct(hidden_media.shape, F32),
            jax.ShapeDtypeStruct(hidden_own.shape, F32),
        ],
        scratch_shapes=[
            pltpu.VMEM((2 * count, head_dim, width), BF),
            pltpu.VMEM((group, seqs * lat, width), BF),
            pltpu.VMEM((seqs, block, width), BF),
            pltpu.VMEM((group, seqs * lat, LANES), BF),
            pltpu.VMEM((2 * group, head_dim, width), BF),
            pltpu.VMEM((block, width), BF),
            pltpu.SemaphoreType.DMA((2 * heads,)),
            pltpu.SemaphoreType.DMA((2 * group,)),
        ],
        input_output_aliases={position: 0, position + 1: 1, position + 2: 2} if halves else {},
        compiler_params=params(60),
        cost_estimate=cost(work, 20e6),
        name="attend_back",
    )(order, place, slot, query_t, hidden_media, hidden_own, *pieces, folded, scores, own_scores, *parts, *halves)


def local(
    grid,
    media,
    image_counts,
    time_ids,
    latents,
    time_table,
    media_gain,
    latent_gain,
    feed_gain,
    query_weight,
    keyval_weight,
    output_weight,
    up_weight,
    down_weight,
    cotangent,
):
    width = output_weight.shape[1]
    head_dim = width // HEADS
    factor = head_dim ** (-0.5)
    lat_rows = latents.shape[0]
    times = time_table.shape[0]
    seq_here, patches = media.shape[0], media.shape[2]
    own_rows = lat_rows // grid.frame
    rows = seq_here * own_rows
    part = width // grid.count
    slot = lax.axis_index("frame")
    first_row = slot * own_rows
    places, owners = grid.places(), grid.owners()
    aligned = grid.count == 2 * HEADS
    if aligned:
        order, place = owners, places
    else:
        order = place = jnp.arange(2 * HEADS, dtype=jnp.int32)

    quarters = (grid.count // 2, grid.count // 2 + grid.count // 4)

    def scatter_order(parts):
        if aligned:
            return parts
        v = jnp.concatenate(parts).reshape(grid.count, -1, parts[0].shape[-1])
        return jnp.split(v.at[owners].get(mode="promise_in_bounds"), quarters)

    def aligned_parts(parts):
        if aligned:
            return parts
        flat = jnp.concatenate(parts).at[places].get(mode="promise_in_bounds")
        return [flat.reshape(2 * HEADS, -1, width)]

    pad = (-(lat_rows + times + 3)) % 8
    packed = jnp.concatenate(
        [latents, time_table, media_gain[None], latent_gain[None], feed_gain[None], jnp.zeros((pad, part), BF)]
    )
    small = grid.gather(packed.T[None], "z")
    first, *rest = grid.strides(grid.depth)
    keyval_z = grid.step(after(keyval_weight.T, small)[None], "z", first)
    small = grid.gather(after(small, keyval_z), "ab")
    for k in rest:
        keyval_z = grid.step(keyval_z, "z", k)
    small = grid.gather(after(small, keyval_z), "c").at[places].get(mode="promise_in_bounds")
    small = small.reshape(width, -1).T.astype(F32)
    lat_float = small[:lat_rows]
    table_all = small[lat_rows : lat_rows + times]
    media_scale, latent_scale, feed_scale = (small[lat_rows + times + i][None] for i in range(3))

    grad_out = cotangent.reshape(rows, width)
    hid_f = up_weight.shape[1]
    hid = hid_f // grid.seq
    d_part = up_weight.shape[0]
    blocks = (grid.seq, hid, d_part)
    feed_got = jnp.concatenate([up_weight.T.reshape(blocks), down_weight.reshape(blocks)], -1)
    is_valid = (slot < image_counts).astype(jnp.int32)
    onehot = (time_ids[:, 0][:, None] == jnp.arange(times, dtype=jnp.int32)[None, :]).astype(F32)
    embedding = jnp.dot(onehot, table_all, precision=HIGHEST)
    embedded = media[:, 0].astype(F32) + embedding[:, None, :]
    normed_media, inv_media = normalize(embedded)
    hidden_media = (normed_media * media_scale).astype(BF)

    normed_lat, inv_lat = normalize(lat_float)
    hidden_lat = (normed_lat * latent_scale).astype(BF)
    hidden_own = lax.dynamic_slice_in_dim(hidden_lat, first_row, own_rows, 0)
    lat_own = lax.dynamic_slice_in_dim(lat_float, first_row, own_rows, 0)
    query_own = mm_tn(query_weight, hidden_lat.T).astype(BF)
    frame_ids = jnp.arange(grid.frame, dtype=jnp.int32) ^ slot
    query_z = grid.gather(query_own[None], "cz")
    query_a = grid.gather(query_z, "a")
    first, *rest = grid.strides(grid.depth)
    mixed_first = grid.step(after(jnp.concatenate([output_weight, grad_out.astype(BF)]), query_z)[None], "z", first)
    mixed_z = mixed_first
    for k in rest:
        mixed_z = grid.step(after(mixed_z, query_a), "z", k)
    query_all = grid.gather(query_a, "b")
    query_t = query_all.reshape(grid.count, part, grid.frame, own_rows)
    query_places = grid.places("czab")
    query_t = query_t.at[query_places[:, None], :, frame_ids[None, :]].get(mode="promise_in_bounds")
    query_t = query_t.transpose(0, 2, 1, 3).reshape(HEADS, head_dim, lat_rows)
    keyval_ab = grid.gather_ab(keyval_z)
    early = (mixed_z, hidden_media, hidden_own, query_t, feed_got)
    keyval_parts = aligned_parts(grid.gather_core(keyval_ab, *early))
    mixed_z = after(mixed_z, keyval_ab)
    folded, media_scores, own_scores, context_parts = attend(
        order, is_valid, query_t, hidden_media, hidden_own, keyval_parts, factor
    )
    context_parts = context_parts.reshape(HEADS, seq_here, grid.frame, own_rows, LANES)
    pieces = [context_parts[:, :, k].reshape(HEADS, rows, LANES).astype(BF) for k in range(grid.frame)]
    pieces = [pieces[0]] + [grid.to_frame(pieces[k], k) for k in range(1, grid.frame)]
    feed_got = lax.all_to_all(after(feed_got, folded), "seq", 0, 0)
    mixed_ab = grid.gather_ab(mixed_z, folded)
    mixed_parts = grid.gather_core(mixed_ab, pieces)
    if aligned:
        output_parts, grad_parts = mixed_parts, mixed_parts
    else:
        output_parts = aligned_parts([p[:, :part] for p in mixed_parts])
        grad_parts = [p[:, part:] for p in mixed_parts]
    mixed, normed_feed, hidden_feed, context, context_low = mixer(
        order, lat_own, feed_scale, pieces, output_parts, head_dim
    )

    up_t, down_w = unpack_feed(feed_got)
    feed_parts = grid.gather_core(grid.gather_ab(grid.gather(after(hidden_feed, feed_got)[None], "z"), up_t))
    half = len(feed_parts) // 2
    far, near = (feed_parts[half:], grad_parts[half:]), (feed_parts[:half], grad_parts[:half])
    far_act, far_grad_up, low, high = feed(up_t, down_w, *far, 2)
    grad_sum = Scatter(grid, low, high)
    near_act, near_grad_up, keep = feed(up_t, down_w, *after(near, high), 1)
    grad_sum.keep(keep)
    grad_sum.to_b()
    spare = part if aligned else 0
    far_up, far_down, low, high = feed_rest(down_w, far_act, after(far_grad_up, keep), *far, spare, 2)
    near_up, near_down, keep = feed_rest(down_w, near_act, after(near_grad_up, high), *near, spare, 1)
    grad_sum.to_a(high)
    grad_sum.to_z(keep)
    back = pack_back(grid.seq, far_up, far_down, near_up, near_down)
    grad_feed = after(grad_sum.result(), back)
    message, grad_mixed, grad_mixed_low, feed_gain_part, residual = unmix(
        order, grad_feed, grad_out, mixed, normed_feed, feed_scale, context, output_parts, head_dim, own_rows
    )
    messages = [message] + [grid.to_frame(message, k) for k in range(1, grid.frame)]
    back = lax.all_to_all(after(back, message), "seq", 0, 0)
    output_context = after(context_low, messages)
    if aligned:
        keep, low, high = output_part_of(place, output_context, grad_mixed_low, keep, low, high)
    else:
        pairs = zip((keep, low, high), scatter_order(output_part_of(place, output_context, grad_mixed_low)))
        keep, low, high = (jnp.concatenate(pair, 1) for pair in pairs)
    mixed_sum = Scatter(grid, low, high)
    mixed_sum.keep(keep)
    messages = after(messages, keep)

    def back_heads(first, count, work, *parts):
        *parts, query_part, grad_media, grad_own = attend_back(
            order, place, slot.reshape(1), query_t, hidden_media, hidden_own, messages, folded, media_scores, own_scores,
            keyval_parts, factor, first, count, work, *parts,
        )
        return parts, (query_part, grad_media, grad_own)

    quarter = HEADS // 4
    parts, sums = back_heads(0, quarter, 2e9)
    parts = after(parts, mixed_sum.high, mixed_sum.arrays)
    mixed_sum.to_b(parts, back)
    parts, more = back_heads(quarter, 2 * quarter, 40e9, *parts)
    sums = [sums, more]
    parts = after(parts, mixed_sum.last())
    mixed_sum.to_a(parts)
    parts, more = back_heads(3 * quarter, quarter, 30e9, *parts)
    sums.append(more)
    query_part = sums[0][0] + sums[1][0] + sums[2][0]
    if not aligned:
        query_part = query_part.reshape(grid.count, part, lat_rows).at[owners].get(mode="promise_in_bounds")
    query_keep, low, high = jnp.split(after(query_part, mixed_sum.last()), quarters)
    query_sum = Scatter(grid, low, high)
    query_sum.keep(query_keep)
    keep, low, high = scatter_order(parts)
    keyval_sum = Scatter(grid, low, high, query_sum.high)
    keyval_sum.keep(keep)
    query_sum.to_b()
    keyval_sum.to_b(query_sum.last())
    query_sum.to_a()
    keyval_b = keyval_sum.last()
    query_sum.to_z(keyval_sum.arrays[0])
    query_sum = query_sum.result().T.astype(BF)
    mixed_sum.to_z(keyval_sum.high)
    sums = after(sums, keyval_sum.high)
    grad_hidden, grad_hidden_own = (sums[0][i] + sums[1][i] + sums[2][i] for i in (1, 2))
    back = after(back, keyval_b)

    media_gain_part = jnp.sum(grad_hidden * normed_media, (0, 1))
    grad_embedded = norm_back(grad_hidden * media_scale, normed_media, inv_media)
    table_part = jnp.dot(onehot.T, jnp.sum(grad_embedded, 1), precision=HIGHEST)

    query_grad = mm_tn(hidden_lat, query_sum)
    grad_lat = mm_nt(query_sum, query_weight)
    grad_lat = grad_lat + lax.dynamic_update_slice_in_dim(jnp.zeros_like(grad_lat), grad_hidden_own, first_row, 0)
    latent_gain_part = jnp.sum(grad_lat * normed_lat, 0)
    latents_part = norm_back(grad_lat * latent_scale, normed_lat, inv_lat)
    latents_part = latents_part + lax.dynamic_update_slice_in_dim(
        jnp.zeros_like(latents_part), residual, first_row, 0
    )
    smalls = jnp.concatenate(
        [
            latents_part,
            table_part,
            media_gain_part[None],
            latent_gain_part[None],
            feed_gain_part,
            jnp.zeros((pad, width), F32),
        ]
    ).astype(BF)
    keyval_sum.to_a()
    keyval_sum.to_z()
    smalls = smalls.T.reshape(grid.count, part, -1).at[grid.owners("cabz")].get(mode="promise_in_bounds")
    small_sum = grid.scatter_core_last(after(smalls, keyval_b)).T
    up_grad_t, down_grad = unpack_back(back)
    up_grad = up_grad_t.T
    keyval_grad = keyval_sum.result().T
    mixed_sums = mixed_sum.result()
    new_latents = (mixed + mixed_sums[:rows]).reshape(seq_here, own_rows, width)
    output_grad = mixed_sums[rows:]
    latents_grad = small_sum[:lat_rows]
    table_grad = small_sum[lat_rows : lat_rows + times]
    media_gain_grad, latent_gain_grad, feed_gain_grad = (small_sum[lat_rows + times + i] for i in range(3))
    return (
        new_latents,
        grad_embedded[:, None],
        latents_grad,
        table_grad,
        media_gain_grad,
        latent_gain_grad,
        feed_gain_grad,
        query_grad,
        keyval_grad,
        output_grad,
        up_grad,
        down_grad,
    )


def solution(mesh):
    grid = Grid(mesh.shape["seq"], mesh.shape["frame"])

    def run(*args):
        return local(grid, *args)

    return jax.shard_map(
        run,
        mesh=mesh,
        in_specs=(
            P("seq", "frame", None, None),
            P("seq"),
            P("seq", "frame"),
            P(None, BOTH),
            P(None, BOTH),
            P(BOTH),
            P(BOTH),
            P(BOTH),
            P(None, BOTH),
            P(None, BOTH),
            P(BOTH, None),
            P("seq", "frame"),
            P("frame", "seq"),
            P("seq", "frame", None),
        ),
        out_specs=(
            P("seq", "frame", None),
            P("seq", "frame", None, None),
            P(None, BOTH),
            P(None, BOTH),
            P(BOTH),
            P(BOTH),
            P(BOTH),
            P(None, BOTH),
            P(None, BOTH),
            P(BOTH, None),
            P("seq", "frame"),
            P("frame", "seq"),
        ),
        check_vma=False,
    )
```

```python
import functools

import jax
import jax.numpy as jnp
from jax import lax
from jax.experimental import pallas as pl
from jax.experimental.pallas import tpu as pltpu
from jax.sharding import PartitionSpec as P

HEADS = 16
EPS = 1e-05
NEGATIVE = -1e30
HIGHEST = lax.Precision.HIGHEST
BF = jnp.bfloat16
F32 = jnp.float32
BOTH = ("seq", "frame")


def normalize(values):
    center = values - jnp.mean(values, -1, keepdims=True)
    scale_inv = lax.rsqrt(jnp.mean(center * center, -1, keepdims=True) + EPS)
    return (center * scale_inv, scale_inv)


def norm_back(grad_hat, normed, scale_inv):
    return scale_inv * (
        grad_hat
        - jnp.mean(grad_hat, -1, keepdims=True)
        - normed * jnp.mean(grad_hat * normed, -1, keepdims=True)
    )


def mm(a, b):
    return jnp.dot(a, b, preferred_element_type=F32)


def mm_tn(a, b):
    return lax.dot_general(a, b, (((0,), (0,)), ((), ())), preferred_element_type=F32)


def mm_nt(a, b):
    return lax.dot_general(a, b, (((1,), (1,)), ((), ())), preferred_element_type=F32)


def ein(spec, a, b):
    return jnp.einsum(spec, a, b, preferred_element_type=F32)


def exact_gelu(values):
    return jax.nn.gelu(values, approximate=False)


def bits(n):
    return n.bit_length() - 1


class Grid:
    def __init__(self, seq_count, frame_count):
        self.seq, self.frame = seq_count, frame_count
        self.side = frame_count // 2
        self.depth = seq_count // self.side
        self.count = seq_count * frame_count

    def split(self, lin):
        side = bits(self.side)
        return lin >> (2 * side + 1), (lin >> (side + 1)) & (self.side - 1), (lin >> 1) & (self.side - 1), lin & 1

    def join(self, z, x, y, c):
        return ((z * self.side + x) * self.side + y) * 2 + c

    def send(self, value, move):
        perm = [(i, self.join(*move(*self.split(i)))) for i in range(self.count)]
        return lax.ppermute(value, BOTH, perm)

    def to_z(self, v, k):
        return self.send(v, lambda z, x, y, c: (z ^ k, x, y, c))

    def to_a(self, v, k):
        return self.send(v, lambda z, x, y, c: (z, x, y ^ k, c) if c else (z, x ^ k, y, c))

    def to_b(self, v, k):
        return self.send(v, lambda z, x, y, c: (z, x ^ k, y, c) if c else (z, x, y ^ k, c))

    def to_x(self, v, k):
        return self.send(v, lambda z, x, y, c: (z, x ^ k, y, c))

    def to_core(self, v):
        return self.send(v, lambda z, x, y, c: (z, x, y, 1 - c))

    def to_frame(self, v, k):
        def move(z, x, y, c):
            f = (y * 2 + c) ^ k
            return z, x, f // 2, f % 2

        return self.send(v, move)

    def own(self):
        return lax.axis_index("seq") * self.frame + lax.axis_index("frame")

    def scatter_core_last(self, v):
        for send, size in ((self.to_z, self.depth), (self.to_b, self.side), (self.to_a, self.side)):
            for k in reversed(self.strides(size)):
                half = v.shape[0] // 2
                v = v[:half].astype(F32) + send(v[half:].astype(BF), k).astype(F32)
        return v[0] + self.to_core(v[1].astype(BF)).astype(F32)

    def strides(self, size):
        return [1 << t for t in reversed(range(bits(size)))]

    def places(self, steps="zabc"):
        z, x, y, c = self.split(self.own())
        oz, ox, oy, oc = self.split(jnp.arange(self.count, dtype=jnp.int32))
        way = oc if steps[-1] == "c" else c
        rx, ry = ox ^ x, oy ^ y
        fields = {
            "z": (oz ^ z, self.depth),
            "a": (jnp.where(way == 0, rx, ry), self.side),
            "b": (jnp.where(way == 0, ry, rx), self.side),
            "c": (oc ^ c, 2),
        }
        place, bit = 0, 0
        for step in steps:
            value, size = fields[step]
            for k in self.strides(size):
                place = place + ((value & k != 0).astype(jnp.int32) << bit)
                bit += 1
        return place

    def owners(self, steps="zabc"):
        order = jnp.arange(self.count, dtype=jnp.int32)
        return jnp.zeros_like(order).at[self.places(steps)].set(order, unique_indices=True)

    def step(self, v, kind, k):
        send = {"z": self.to_z, "a": self.to_a, "b": self.to_b, "c": lambda p, _: self.to_core(p)}[kind]
        return jnp.concatenate([v, send(v, k)])

    def gather(self, v, steps):
        for kind in steps:
            for k in self.strides({"z": self.depth, "c": 2}.get(kind, self.side)):
                v = self.step(v, kind, k)
        return v

    def gather_ab(self, v, *others):
        v = [v]
        for k in self.strides(self.side):
            v = v + [self.to_a(p, k) for p in v]
        for k in self.strides(self.side):
            own = self.to_b(v[0], k)
            v = v + [own] + [self.to_b(after(p, own, others), k) for p in v[1:]]
        return v

    def gather_core(self, v, *others):
        return v + [self.to_core(p) for p in v[:-1]] + [self.to_core(after(v[-1], others))]


class Scatter:
    def __init__(self, grid, low, high, *others):
        self.grid = grid
        self.size = 2 * low.shape[0]
        low, high = after((low, high), others)
        self.high, self.arrays = [grid.to_core(high)], [grid.to_core(low)]

    def keep(self, keep):
        half = self.size // 2
        self.high.append(keep[half:])
        self.arrays.append(keep)

    def sum(self, lo, hi):
        arrays = self.arrays
        if hi > self.arrays[0].shape[0]:
            arrays, lo, hi = self.high, 0, hi - lo
        return sum(p[lo:hi].astype(F32) for p in arrays)

    def step(self, send, strides, *others):
        for k in strides:
            half = self.size // 2
            self.arrays.append(send(after(self.sum(half, self.size).astype(BF), others), k))
            self.size = half

    def to_b(self, *others):
        self.step(self.grid.to_b, self.grid.strides(self.grid.side)[::-1], *others)

    def to_a(self, *others):
        self.step(self.grid.to_a, self.grid.strides(self.grid.side)[::-1], *others)

    def to_z(self, *others, first=True, rest=True):
        strides = self.grid.strides(self.grid.depth)[::-1]
        self.step(self.grid.to_z, (strides[:1] if first else []) + (strides[1:] if rest else []), *others)

    def last(self):
        return self.arrays[-1]

    def result(self):
        return self.sum(0, 1)[0]


def after(value, *others):
    return lax.optimization_barrier((value, others))[0]


def load_blocks(order_ref, part_refs, store_ref, sem_ref):
    rows = store_ref.shape[1]
    copies = []
    for part in part_refs:
        for k in range(part.shape[0]):
            n = len(copies)
            block = part.at[k] if part.shape[1] == rows else part.at[k, pl.ds(0, rows)]
            copies.append(pltpu.make_async_copy(block, store_ref.at[order_ref[n]], sem_ref.at[n]))
    return copies


def place_copy(place_ref, block, source_ref, target_refs, sem_ref):
    place = place_ref[block]
    first = 0
    for target in target_refs:
        index, size = place - first, target.shape[0]
        first += size

        @pl.when((index >= 0) & (index < size))
        def _():
            pltpu.make_async_copy(source_ref, target.at[index], sem_ref).start()


def dot(a, b):
    return lax.dot_general(a, b, (((1,), (0,)), ((), ())), preferred_element_type=F32)


def pieces_of(value):
    high = value.astype(BF).astype(F32)
    middle = (value - high).astype(BF).astype(F32)
    return high, middle, value - high - middle


def whole(shape):
    return pl.BlockSpec(shape, lambda *_: (0,) * len(shape))


SMEM = pl.BlockSpec(memory_space=pltpu.SMEM)
ANYWHERE = pl.BlockSpec(memory_space=pltpu.HBM)
LANES = 128


def params(mib):
    return pltpu.CompilerParams(vmem_limit_bytes=mib * 1024 * 1024)


def cost(flops, moved):
    return pl.CostEstimate(flops=int(flops), bytes_accessed=int(moved), transcendentals=0)


def attend_kernel(sizes, order_ref, valid_ref, query_ref, media_ref, own_ref, *refs):
    heads, group, seqs, lat, factor, part_count = sizes
    parts = refs[:part_count]
    folded_ref, score_ref, own_score_ref, context_ref, weight_ref, mix_ref, sem_ref = refs[part_count:]
    step = pl.program_id(0)
    head_dim = weight_ref.shape[1]

    @pl.when(step == 0)
    def _():
        copies = load_blocks(order_ref, parts, weight_ref, sem_ref)
        for c in copies:
            c.start()
        for c in copies:
            c.wait()

    for j in range(group):
        h = step * group + j
        folded = mm_tn(query_ref[h], weight_ref[h]) * factor
        folded_ref[j * lat : (j + 1) * lat, :] = folded.astype(BF)
    queries = folded_ref[...]
    own = own_ref[...]
    own_scores = mm_nt(queries, own)
    own_score_ref[...] = own_scores
    own_top = jnp.max(own_scores, -1, keepdims=True)
    lanes = lax.broadcasted_iota(jnp.int32, (group * lat, LANES), 1)
    for s in range(seqs):
        media = media_ref[s]
        scores = mm_nt(queries, media)
        scores = jnp.where(valid_ref[s] > 0, scores, NEGATIVE)
        score_ref[s] = scores
        top = jnp.maximum(jnp.max(scores, -1, keepdims=True), own_top)
        media_exp = jnp.exp(scores - top)
        own_exp = jnp.exp(own_scores - top)
        total = jnp.sum(media_exp, -1, keepdims=True) + jnp.sum(own_exp, -1, keepdims=True)
        mix = dot(media_exp.astype(BF), media) + dot(own_exp.astype(BF), own)
        mix = (mix * (1.0 / total)).astype(BF)
        stats = jnp.zeros(lanes.shape, F32)
        for i, piece in enumerate(pieces_of(top) + pieces_of(total)):
            stats = jnp.where(lanes == head_dim + i, piece, stats)
        for j in range(group):
            mix_ref[j, s * lat : (s + 1) * lat, :] = mix[j * lat : (j + 1) * lat, :]
            context_ref[j, s * lat : (s + 1) * lat, head_dim:] = stats[j * lat : (j + 1) * lat, head_dim:]
    for j in range(group):
        h = step * group + j
        context_ref[j, :, :head_dim] = mm_nt(mix_ref[j], weight_ref[heads + h])


def attend(order, valid, query_t, hidden_media, hidden_own, parts, factor):
    heads, head_dim, lat = query_t.shape
    seqs, patches, width = hidden_media.shape
    group = 4
    own = hidden_own.shape[0]
    rows = group * lat
    return pl.pallas_call(
        functools.partial(attend_kernel, (heads, group, seqs, lat, factor, len(parts))),
        grid=(heads // group,),
        in_specs=[SMEM, SMEM, whole(query_t.shape), whole(hidden_media.shape), whole(hidden_own.shape)]
        + [ANYWHERE] * len(parts),
        out_specs=[
            pl.BlockSpec((rows, width), lambda i: (i, 0)),
            pl.BlockSpec((seqs, rows, patches), lambda i: (0, i, 0)),
            pl.BlockSpec((rows, own), lambda i: (i, 0)),
            pl.BlockSpec((group, seqs * lat, LANES), lambda i: (i, 0, 0)),
        ],
        out_shape=[
            jax.ShapeDtypeStruct((heads * lat, width), BF),
            jax.ShapeDtypeStruct((seqs, heads * lat, patches), F32),
            jax.ShapeDtypeStruct((heads * lat, own), F32),
            jax.ShapeDtypeStruct((heads, seqs * lat, LANES), F32),
        ],
        scratch_shapes=[
            pltpu.VMEM((2 * heads, head_dim, width), BF),
            pltpu.VMEM((group, seqs * lat, width), BF),
            pltpu.SemaphoreType.DMA((2 * heads,)),
        ],
        compiler_params=params(56),
        cost_estimate=cost(2e9, 2e6),
        name="attend",
    )(order, valid, query_t, hidden_media, hidden_own, *parts)


def mixer_kernel(sizes, order_ref, latent_ref, gain_ref, *refs):
    heads, head_dim, seqs, piece_count, part_count = sizes
    pieces = refs[:piece_count]
    parts = refs[piece_count : piece_count + part_count]
    mixed_ref, normed_ref, hidden_ref, context_ref, low_ref, weight_ref, sem_ref = refs[piece_count + part_count :]
    copies = load_blocks(order_ref, parts, weight_ref, sem_ref)
    for c in copies:
        c.start()
    values = [p[...].astype(F32) for p in pieces]
    at = head_dim
    tops = [v[..., at : at + 1] + v[..., at + 1 : at + 2] + v[..., at + 2 : at + 3] for v in values]
    totals = [v[..., at + 3 : at + 4] + v[..., at + 4 : at + 5] + v[..., at + 5 : at + 6] for v in values]
    top = functools.reduce(jnp.maximum, tops)
    shares = [t * jnp.exp(p - top) for t, p in zip(totals, tops)]
    total = functools.reduce(lambda p, q: p + q, shares)
    context = functools.reduce(lambda p, q: p + q, [v * (w / total) for v, w in zip(values, shares)])
    lanes = lax.broadcasted_iota(jnp.int32, context.shape, 2)
    context_ref[...] = jnp.where(lanes == head_dim, top + jnp.log(total), context)
    for h in range(heads):
        low_ref[:, h * head_dim : (h + 1) * head_dim] = context[h, :, :head_dim].astype(BF)
    for c in copies:
        c.wait()
    weight = weight_ref[...].reshape(heads * head_dim, -1)
    mixed = jnp.concatenate([latent_ref[...]] * seqs) + dot(low_ref[...], weight)
    mixed_ref[...] = mixed
    center = mixed - jnp.mean(mixed, -1, keepdims=True)
    normed = center * lax.rsqrt(jnp.mean(center * center, -1, keepdims=True) + EPS)
    normed_ref[...] = normed
    hidden_ref[...] = (normed * gain_ref[...]).astype(BF)


def mixer(order, latent_own, gain, pieces, parts, head_dim):
    heads, rows, _ = pieces[0].shape
    own_rows, width = latent_own.shape
    count = sum(p.shape[0] for p in parts)
    block = heads * head_dim // count
    sizes = (heads, head_dim, rows // own_rows, len(pieces), len(parts))
    return pl.pallas_call(
        functools.partial(mixer_kernel, sizes),
        in_specs=[SMEM, whole(latent_own.shape), whole(gain.shape)]
        + [whole(p.shape) for p in pieces]
        + [ANYWHERE] * len(parts),
        out_specs=[whole((rows, width))] * 3 + [whole((heads, rows, LANES)), whole((rows, heads * head_dim))],
        out_shape=[
            jax.ShapeDtypeStruct((rows, width), F32),
            jax.ShapeDtypeStruct((rows, width), F32),
            jax.ShapeDtypeStruct((rows, width), BF),
            jax.ShapeDtypeStruct((heads, rows, LANES), F32),
            jax.ShapeDtypeStruct((rows, heads * head_dim), BF),
        ],
        scratch_shapes=[pltpu.VMEM((count, block, width), BF), pltpu.SemaphoreType.DMA((count,))],
        compiler_params=params(60),
        cost_estimate=cost(1e6, 1e6),
        name="mixer",
    )(order, latent_own, gain, *pieces, *parts)


def unmix_kernel(sizes, order_ref, grad_feed_ref, grad_out_ref, mixed_ref, normed_ref, gain_ref, context_ref, *refs):
    heads, head_dim, seqs, part_count = sizes
    parts = refs[:part_count]
    message_ref, grad_mixed_ref, low_ref, gain_grad_ref, residual_ref, weight_ref, sem_ref = refs[part_count:]
    copies = load_blocks(order_ref, parts, weight_ref, sem_ref)
    for c in copies:
        c.start()
    mixed = mixed_ref[...]
    center = mixed - jnp.mean(mixed, -1, keepdims=True)
    scale_inv = lax.rsqrt(jnp.mean(center * center, -1, keepdims=True) + EPS)
    normed = normed_ref[...]
    grad_feed = grad_feed_ref[...]
    gain_grad_ref[...] = jnp.sum(grad_feed * normed, 0, keepdims=True)
    grad_mixed = grad_out_ref[...] + norm_back(grad_feed * gain_ref[...], normed, scale_inv)
    grad_mixed_ref[...] = grad_mixed
    own = residual_ref.shape[0]
    residual_ref[...] = sum(grad_mixed[s * own : (s + 1) * own] for s in range(seqs))
    low = grad_mixed.astype(BF)
    low_ref[...] = low
    for c in copies:
        c.wait()
    grads = mm_nt(low, weight_ref[...].reshape(heads * head_dim, -1)).astype(BF)
    lanes = lax.broadcasted_iota(jnp.int32, (low.shape[0], LANES), 1)
    for h in range(heads):
        grad = grads[:, h * head_dim : (h + 1) * head_dim]
        context = context_ref[h]
        row = jnp.sum(grad.astype(F32) * context[:, :head_dim], -1, keepdims=True)
        log_total = context[:, head_dim : head_dim + 1]
        message = jnp.zeros(lanes.shape, F32)
        for i, piece in enumerate(pieces_of(row) + pieces_of(log_total)):
            message = jnp.where(lanes == head_dim + i, piece, message)
        message_ref[h] = message.astype(BF)
        message_ref[h, :, :head_dim] = grad


def unmix(order, grad_feed, grad_out, mixed, normed, gain, context, parts, head_dim, own_rows):
    heads, rows, _ = context.shape
    width = mixed.shape[1]
    count = sum(p.shape[0] for p in parts)
    block = heads * head_dim // count
    sizes = (heads, head_dim, rows // own_rows, len(parts))
    arrays = (grad_feed, grad_out, mixed, normed, gain, context)
    shapes = [((heads, rows, LANES), BF), ((rows, width), F32), ((rows, width), BF), ((1, width), F32), ((own_rows, width), F32)]
    return pl.pallas_call(
        functools.partial(unmix_kernel, sizes),
        in_specs=[SMEM] + [whole(a.shape) for a in arrays] + [ANYWHERE] * len(parts),
        out_specs=[whole(shape) for shape, _ in shapes],
        out_shape=[jax.ShapeDtypeStruct(*item) for item in shapes],
        scratch_shapes=[pltpu.VMEM((count, block, width), BF), pltpu.SemaphoreType.DMA((count,))],
        compiler_params=params(60),
        cost_estimate=cost(2e9, 8e6),
        name="unmix",
    )(order, *arrays, *parts)


def output_part_kernel(groups, place_ref, context_ref, low_ref, *refs):
    *targets, out_ref, sem_ref = refs[-5:]
    low = low_ref[...]
    per = out_ref.shape[0] // groups
    part = context_ref.shape[1] // groups
    rows = out_ref.shape[1]
    targets = [t.at[:, pl.ds(t.shape[1] - rows, rows)] for t in targets]
    for g in range(groups):
        value = mm_tn(context_ref[:, g * part : (g + 1) * part], low).astype(BF)
        out_ref[g * per : (g + 1) * per] = value.reshape((per,) + out_ref.shape[1:])
        for i in range(g * per, (g + 1) * per):
            place_copy(place_ref, i, out_ref.at[i], targets, sem_ref.at[i])
    for i in range(out_ref.shape[0]):
        pltpu.make_async_copy(out_ref.at[i], targets[0].at[0], sem_ref.at[i]).wait()


def output_part_of(place, context, low, *halves):
    width = low.shape[1]
    count = place.shape[0]
    block = context.shape[1] // count
    shapes = [h.shape for h in halves] or [(n, block, width) for n in (count // 2, count // 4, count // 4)]
    return pl.pallas_call(
        functools.partial(output_part_kernel, 4),
        in_specs=[SMEM, whole(context.shape), whole(low.shape)] + [ANYWHERE] * len(halves),
        out_specs=[ANYWHERE] * 3,
        out_shape=[jax.ShapeDtypeStruct(shape, BF) for shape in shapes],
        input_output_aliases={3: 0, 4: 1, 5: 2} if halves else {},
        scratch_shapes=[pltpu.VMEM((count, block, width), BF), pltpu.SemaphoreType.DMA((count,))],
        compiler_params=params(60),
        cost_estimate=cost(1e9, 2e6),
        name="output_part",
    )(place, context, low, *halves)


def unpack_feed_kernel(got_ref, up_ref, down_ref):
    part = got_ref.shape[-1] // 2
    for s in range(got_ref.shape[0]):
        up_ref[:, s * part : (s + 1) * part] = got_ref[s, :, :part]
        down_ref[:, s * part : (s + 1) * part] = got_ref[s, :, part:]


def unpack_feed(got):
    count, hid, part = got.shape
    out = (hid, count * part // 2)
    return pl.pallas_call(
        unpack_feed_kernel,
        in_specs=[whole(got.shape)],
        out_specs=[whole(out)] * 2,
        out_shape=[jax.ShapeDtypeStruct(out, BF)] * 2,
        cost_estimate=cost(0, 3e6),
        name="unpack_feed",
    )(got)


def pack_back_kernel(far_up_ref, far_down_ref, near_up_ref, near_down_ref, out_ref):
    part = out_ref.shape[-1] // 2
    for s in range(out_ref.shape[0]):
        at = slice(s * part, (s + 1) * part)
        out_ref[s, :, :part] = (far_up_ref[:, at] + near_up_ref[:, at]).astype(BF)
        out_ref[s, :, part:] = (far_down_ref[:, at] + near_down_ref[:, at]).astype(BF)


def pack_back(count, *grads):
    hid, width = grads[0].shape
    out = (count, hid, 2 * width // count)
    return pl.pallas_call(
        pack_back_kernel,
        in_specs=[whole(g.shape) for g in grads],
        out_specs=whole(out),
        out_shape=jax.ShapeDtypeStruct(out, BF),
        cost_estimate=cost(0, 6e6),
        name="pack_back",
    )(*grads)


def unpack_back_kernel(got_ref, up_ref, down_ref):
    hid, part = got_ref.shape[1], got_ref.shape[2] // 2
    for s in range(got_ref.shape[0]):
        up_ref[s * hid : (s + 1) * hid, :] = got_ref[s, :, :part].astype(F32)
        down_ref[s * hid : (s + 1) * hid, :] = got_ref[s, :, part:].astype(F32)


def unpack_back(got):
    count, hid, part = got.shape
    out = (count * hid, part // 2)
    return pl.pallas_call(
        unpack_back_kernel,
        in_specs=[whole(got.shape)],
        out_specs=[whole(out)] * 2,
        out_shape=[jax.ShapeDtypeStruct(out, F32)] * 2,
        cost_estimate=cost(0, 5e6),
        name="unpack_back",
    )(got)


ROOT_HALF = 0.5**0.5
DENSITY = 1 / (2 * 3.141592653589793) ** 0.5


def loads(parts, rows, store_ref, sem_ref):
    out, n = [], 0
    for part in parts:
        skip = part.shape[1] - rows
        copies = []
        for k in range(part.shape[0]):
            block = part.at[k, pl.ds(skip, rows)] if skip else part.at[k]
            copies.append(pltpu.make_async_copy(block, store_ref.at[n], sem_ref.at[n]))
            n += 1
        out.append(copies)
    return out


def start(copies):
    for c in copies:
        c.start()


def wait(copies):
    for c in copies:
        c.wait()


def feed_kernel(part_count, up_ref, down_ref, *refs):
    feed, grad = refs[:part_count], refs[part_count : 2 * part_count]
    act_ref, grad_up_ref, *out_refs = refs[2 * part_count : -6]
    feed_st, grad_st, out_st, feed_sem, grad_sem, out_sem = refs[-6:]
    each = part_count // len(out_refs)
    n, per, width = feed[0].shape
    chunk = n * per
    feeds, grads = loads(feed, per, feed_st, feed_sem), loads(grad, per, grad_st, grad_sem)
    for i in range(part_count):
        start(feeds[i])
        start(grads[i])
    up, down = up_ref[...], down_ref[...]
    outs = []
    each, n, chunk = each // 2, 2 * n, 2 * chunk
    for i in range(part_count // 2):
        at = slice(i * n, (i + 1) * n)
        wait(feeds[2 * i] + feeds[2 * i + 1])
        pre = mm_nt(feed_st[at].reshape(chunk, width), up)
        wait(grads[2 * i] + grads[2 * i + 1])
        grad_act = mm_nt(grad_st[at].reshape(chunk, width), down)
        cdf = 0.5 * (1.0 + lax.erf(pre * ROOT_HALF))
        slope = cdf + pre * (jnp.exp(-0.5 * pre * pre) * DENSITY)
        act_ref[i * chunk : (i + 1) * chunk, :] = (pre * cdf).astype(BF)
        grad_up = (grad_act * slope).astype(BF)
        grad_up_ref[i * chunk : (i + 1) * chunk, :] = grad_up
        out_st[at] = dot(grad_up, up).astype(BF).reshape(n, per, width)
        to = out_refs[i // each].at[pl.ds(i % each * n, n)]
        outs.append(pltpu.make_async_copy(out_st.at[pl.ds(i * n, n)], to, out_sem.at[i]))
        outs[i].start()
    wait(outs)


def feed(up, down, feed_parts, grad_parts, splits):
    hid, width = up.shape
    count = len(feed_parts)
    n, per, _ = feed_parts[0].shape
    rows = count * n * per
    store = pltpu.VMEM((count * n, per, width), BF)
    sems = pltpu.SemaphoreType.DMA((count * n,))
    return pl.pallas_call(
        functools.partial(feed_kernel, count),
        in_specs=[whole(up.shape), whole(down.shape)] + [ANYWHERE] * (2 * count),
        out_specs=[whole((rows, hid))] * 2 + [ANYWHERE] * splits,
        out_shape=[jax.ShapeDtypeStruct((rows, hid), BF)] * 2
        + [jax.ShapeDtypeStruct((count * n // splits, per, width), BF)] * splits,
        scratch_shapes=[store] * 3 + [sems] * 3,
        compiler_params=params(60),
        cost_estimate=cost(5e9, 8e6),
        name="feed",
    )(up, down, *feed_parts, *grad_parts)


def feed_rest_kernel(part_count, down_ref, act_ref, grad_up_ref, *refs):
    feed, grad = refs[:part_count], refs[part_count : 2 * part_count]
    up_grad_ref, down_grad_ref, *out_refs = refs[2 * part_count : -6]
    feed_st, grad_st, out_st, feed_sem, grad_sem, out_sem = refs[-6:]
    each = part_count // len(out_refs)
    n, per, width = feed[0].shape
    chunk = n * per
    feeds, grads = loads(feed, per, feed_st, feed_sem), loads(grad, per, grad_st, grad_sem)
    for i in range(part_count):
        start(grads[i])
        start(feeds[i])
    down = down_ref[...]
    first = pl.ds(0, per)
    outs = []
    for i in range(part_count):
        at = slice(i * n, (i + 1) * n)
        act = act_ref[i * chunk : (i + 1) * chunk, :]
        out_st[at] = dot(act, down).astype(BF).reshape(n, per, width)
        to = out_refs[i // each].at[pl.ds(i % each * n, n), first]
        outs.append(pltpu.make_async_copy(out_st.at[pl.ds(i * n, n)], to, out_sem.at[i]))
        outs[i].start()
    for i in range(part_count):
        wait(feeds[i])
        wait(grads[i])
    up_grad_ref[...] = mm_tn(grad_up_ref[...], feed_st[...].reshape(part_count * chunk, width))
    down_grad_ref[...] = mm_tn(act_ref[...], grad_st[...].reshape(part_count * chunk, width))
    wait(outs)


def feed_rest(down, act, grad_up, feed_parts, grad_parts, spare, splits):
    hid, width = down.shape
    count = len(feed_parts)
    n, per, _ = feed_parts[0].shape
    store = pltpu.VMEM((count * n, per, width), BF)
    sems = pltpu.SemaphoreType.DMA((count * n,))
    return pl.pallas_call(
        functools.partial(feed_rest_kernel, count),
        in_specs=[whole(down.shape), whole(act.shape), whole(grad_up.shape)] + [ANYWHERE] * (2 * count),
        out_specs=[whole((hid, width))] * 2 + [ANYWHERE] * splits,
        out_shape=[jax.ShapeDtypeStruct((hid, width), F32)] * 2
        + [jax.ShapeDtypeStruct((count * n // splits, per + spare, width), BF)] * splits,
        scratch_shapes=[store] * 3 + [sems] * 3,
        compiler_params=params(48),
        cost_estimate=cost(5e9, 8e6),
        name="feed_rest",
    )(down, act, grad_up, *feed_parts, *grad_parts)


def attend_back_kernel(sizes, order_ref, place_ref, slot_ref, query_ref, media_ref, own_ref, *refs):
    heads, group, seqs, lat, factor, piece_count, part_count, first, count = sizes
    pieces = refs[:piece_count]
    folded_ref, score_ref, own_score_ref = refs[piece_count : piece_count + 3]
    parts = refs[piece_count + 3 : piece_count + 3 + part_count]
    refs = refs[piece_count + 3 + part_count :]
    (
        keep_ref,
        low_ref,
        high_ref,
        query_part_ref,
        grad_media_ref,
        grad_own_ref,
        weight_ref,
        mix_ref,
        gp_ref,
        grad_ref,
        out_ref,
        key_mix_ref,
        sem_ref,
        out_sem_ref,
    ) = refs[-14:]
    step = pl.program_id(0)
    head_dim = weight_ref.shape[1]
    own_rows = own_ref.shape[0]

    def weight_loads():
        loads_here = []
        for part in parts:
            for k in range(part.shape[0]):
                n = len(loads_here)
                block = order_ref[n]
                head = block & (heads - 1)
                here = (head >= first) & (head < first + count)
                to = jnp.where(here, head - first + jnp.where(block >= heads, count, 0), 0)
                copy = pltpu.make_async_copy(part.at[k], weight_ref.at[to], sem_ref.at[n])
                loads_here.append((here, block >= heads, copy))
        return loads_here

    def out_wait():
        for slot in range(2 * group):
            pltpu.make_async_copy(out_ref.at[slot], keep_ref.at[0], out_sem_ref.at[slot]).wait()

    @pl.when(step == 0)
    def _():
        loads_here = weight_loads()
        for here, value, c in loads_here:
            pl.when(here & value)(c.start)
        for here, value, c in loads_here:
            pl.when(here & ~value)(c.start)
        grad_media_ref[...] = jnp.zeros_like(grad_media_ref)
        grad_own_ref[...] = jnp.zeros_like(grad_own_ref)
        query_part_ref[...] = jnp.zeros_like(query_part_ref)
        for here, value, c in loads_here:
            pl.when(here & value)(c.wait)

    columns = []
    for j in range(group):
        h = step * group + j
        for s in range(seqs):
            for k in range(piece_count):
                at = s * lat + k * own_rows
                grad_ref[j, at : at + own_rows, :] = pieces[k][first + h, s * own_rows : (s + 1) * own_rows, :]
        message = grad_ref[j].astype(F32)
        column = [message[:, head_dim + i : head_dim + i + 1] for i in range(6)]
        columns.append((column[0] + column[1] + column[2], column[3] + column[4] + column[5]))
        lifted = dot(grad_ref[j, :, :head_dim], weight_ref[count + h]).astype(BF)
        for s in range(seqs):
            gp_ref[s, j * lat : (j + 1) * lat, :] = lifted[s * lat : (s + 1) * lat, :]
    queries = folded_ref[...]
    own = own_ref[...]
    own_scores = own_score_ref[...]
    key_mix = jnp.zeros(queries.shape, F32)
    own_sum = jnp.zeros(own_scores.shape, F32)
    for s in range(seqs):
        media = media_ref[s]
        lifted = gp_ref[s]
        row_term, log_total = (
            jnp.concatenate([columns[j][i][s * lat : (s + 1) * lat] for j in range(group)]) for i in range(2)
        )
        probs = jnp.exp(score_ref[s] - log_total)
        own_probs = jnp.exp(own_scores - log_total)
        ds = (probs * (mm_nt(lifted, media) - row_term)).astype(BF)
        own_ds = (own_probs * (mm_nt(lifted, own) - row_term)).astype(BF)
        probs, own_probs = probs.astype(BF), own_probs.astype(BF)
        key_mix = key_mix + dot(ds, media)
        own_sum = own_sum + own_ds.astype(F32)
        mix = (dot(probs, media) + dot(own_probs, own)).astype(BF)
        for j in range(group):
            mix_ref[j, s * lat : (s + 1) * lat, :] = mix[j * lat : (j + 1) * lat, :]
        pair = jnp.concatenate([queries, lifted])
        grad_media_ref[s] += mm_tn(jnp.concatenate([ds, probs]), pair)
        grad_own_ref[...] += mm_tn(jnp.concatenate([own_ds, own_probs]), pair)
    key_mix = key_mix + dot(own_sum.astype(BF), own)
    key_mix_ref[...] = (key_mix * factor).astype(BF)
    per = query_part_ref.shape[0] // heads
    pl.when(step > 0)(out_wait)

    @pl.when(step == 0)
    def _():
        for here, value, c in weight_loads():
            pl.when(here & ~value)(c.wait)

    for j in range(group):
        h = step * group + j
        mixed = key_mix_ref[j * lat : (j + 1) * lat, :]
        sorted_rows = [
            key_mix_ref[pl.ds(pl.multiple_of(j * lat + (k ^ slot_ref[0]) * own_rows, own_rows), own_rows), :]
            for k in range(piece_count)
        ]
        part = mm_nt(weight_ref[h], jnp.concatenate(sorted_rows)).astype(BF)
        for i in range(per):
            rows = head_dim // per
            query_part_ref[place_ref[(first + h) * per + i]] = part[i * rows : (i + 1) * rows]
        out_ref[2 * j] = dot(query_ref[first + h], mixed).astype(BF)
        out_ref[2 * j + 1] = mm_tn(grad_ref[j, :, :head_dim], mix_ref[j]).astype(BF)
        for i in range(2):
            slot = 2 * j + i
            place_copy(
                place_ref, first + h + i * heads, out_ref.at[slot], (keep_ref, low_ref, high_ref), out_sem_ref.at[slot]
            )
    pl.when(step == pl.num_programs(0) - 1)(out_wait)


def attend_back(order, place, slot, query_t, hidden_media, hidden_own, pieces, folded, scores, own_scores, parts, factor, first, count, work, *halves):
    heads, head_dim, lat = query_t.shape
    seqs, patches, width = hidden_media.shape
    group = 4
    own = hidden_own.shape[0]
    block = group * lat
    sizes = (heads, group, seqs, lat, factor, len(pieces), len(parts), first, count)
    skip = first // group
    position = 9 + len(pieces) + len(parts)
    return pl.pallas_call(
        functools.partial(attend_back_kernel, sizes),
        grid=(count // group,),
        in_specs=[SMEM, SMEM, SMEM, whole(query_t.shape), whole(hidden_media.shape), whole(hidden_own.shape)]
        + [whole(p.shape) for p in pieces]
        + [
            pl.BlockSpec((block, width), lambda i: (i + skip, 0)),
            pl.BlockSpec((seqs, block, patches), lambda i: (0, i + skip, 0)),
            pl.BlockSpec((block, own), lambda i: (i + skip, 0)),
        ]
        + [ANYWHERE] * (len(parts) + len(halves)),
        out_specs=[
            ANYWHERE,
            ANYWHERE,
            ANYWHERE,
            whole((2 * heads, head_dim // 2, lat)),
            whole(hidden_media.shape),
            whole(hidden_own.shape),
        ],
        out_shape=[
            jax.ShapeDtypeStruct((heads, head_dim, width), BF),
            jax.ShapeDtypeStruct((heads // 2, head_dim, width), BF),
            jax.ShapeDtypeStruct((heads // 2, head_dim, width), BF),
            jax.ShapeDtypeStruct((2 * heads, head_dim // 2, lat), BF),
            jax.ShapeDtypeStruct(hidden_media.shape, F32),
            jax.ShapeDtypeStruct(hidden_own.shape, F32),
        ],
        scratch_shapes=[
            pltpu.VMEM((2 * count, head_dim, width), BF),
            pltpu.VMEM((group, seqs * lat, width), BF),
            pltpu.VMEM((seqs, block, width), BF),
            pltpu.VMEM((group, seqs * lat, LANES), BF),
            pltpu.VMEM((2 * group, head_dim, width), BF),
            pltpu.VMEM((block, width), BF),
            pltpu.SemaphoreType.DMA((2 * heads,)),
            pltpu.SemaphoreType.DMA((2 * group,)),
        ],
        input_output_aliases={position: 0, position + 1: 1, position + 2: 2} if halves else {},
        compiler_params=params(60),
        cost_estimate=cost(work, 20e6),
        name="attend_back",
    )(order, place, slot, query_t, hidden_media, hidden_own, *pieces, folded, scores, own_scores, *parts, *halves)


def local(
    grid,
    media,
    image_counts,
    time_ids,
    latents,
    time_table,
    media_gain,
    latent_gain,
    feed_gain,
    query_weight,
    keyval_weight,
    output_weight,
    up_weight,
    down_weight,
    cotangent,
):
    width = output_weight.shape[1]
    head_dim = width // HEADS
    factor = head_dim ** (-0.5)
    lat_rows = latents.shape[0]
    times = time_table.shape[0]
    seq_here, patches = media.shape[0], media.shape[2]
    own_rows = lat_rows // grid.frame
    rows = seq_here * own_rows
    part = width // grid.count
    slot = lax.axis_index("frame")
    first_row = slot * own_rows
    places, owners = grid.places(), grid.owners()
    aligned = grid.count == 2 * HEADS
    if aligned:
        order, place = owners, places
    else:
        order = place = jnp.arange(2 * HEADS, dtype=jnp.int32)

    quarters = (grid.count // 2, grid.count // 2 + grid.count // 4)

    def scatter_order(parts):
        if aligned:
            return parts
        v = jnp.concatenate(parts).reshape(grid.count, -1, parts[0].shape[-1])
        return jnp.split(v.at[owners].get(mode="promise_in_bounds"), quarters)

    def aligned_parts(parts):
        if aligned:
            return parts
        flat = jnp.concatenate(parts).at[places].get(mode="promise_in_bounds")
        return [flat.reshape(2 * HEADS, -1, width)]

    pad = (-(lat_rows + times + 3)) % 8
    packed = jnp.concatenate(
        [latents, time_table, media_gain[None], latent_gain[None], feed_gain[None], jnp.zeros((pad, part), BF)]
    )
    small = grid.gather(packed.T[None], "z")
    first, *rest = grid.strides(grid.depth)
    keyval_z = grid.step(after(keyval_weight.T, small)[None], "z", first)
    small = grid.gather(after(small, keyval_z), "ab")
    for k in rest:
        keyval_z = grid.step(keyval_z, "z", k)
    small = grid.gather(after(small, keyval_z), "c").at[places].get(mode="promise_in_bounds")
    small = small.reshape(width, -1).T.astype(F32)
    lat_float = small[:lat_rows]
    table_all = small[lat_rows : lat_rows + times]
    media_scale, latent_scale, feed_scale = (small[lat_rows + times + i][None] for i in range(3))

    grad_out = cotangent.reshape(rows, width)
    hid_f = up_weight.shape[1]
    hid = hid_f // grid.seq
    d_part = up_weight.shape[0]
    blocks = (grid.seq, hid, d_part)
    feed_got = jnp.concatenate([up_weight.T.reshape(blocks), down_weight.reshape(blocks)], -1)
    is_valid = (slot < image_counts).astype(jnp.int32)
    onehot = (time_ids[:, 0][:, None] == jnp.arange(times, dtype=jnp.int32)[None, :]).astype(F32)
    embedding = jnp.dot(onehot, table_all, precision=HIGHEST)
    embedded = media[:, 0].astype(F32) + embedding[:, None, :]
    normed_media, inv_media = normalize(embedded)
    hidden_media = (normed_media * media_scale).astype(BF)

    normed_lat, inv_lat = normalize(lat_float)
    hidden_lat = (normed_lat * latent_scale).astype(BF)
    hidden_own = lax.dynamic_slice_in_dim(hidden_lat, first_row, own_rows, 0)
    lat_own = lax.dynamic_slice_in_dim(lat_float, first_row, own_rows, 0)
    query_own = mm_tn(query_weight, hidden_lat.T).astype(BF)
    frame_ids = jnp.arange(grid.frame, dtype=jnp.int32) ^ slot
    query_z = grid.gather(query_own[None], "cz")
    query_a = grid.gather(query_z, "a")
    first, *rest = grid.strides(grid.depth)
    mixed_first = grid.step(after(jnp.concatenate([output_weight, grad_out.astype(BF)]), query_z)[None], "z", first)
    mixed_z = mixed_first
    for k in rest:
        mixed_z = grid.step(after(mixed_z, query_a), "z", k)
    query_all = grid.gather(query_a, "b")
    query_t = query_all.reshape(grid.count, part, grid.frame, own_rows)
    query_places = grid.places("czab")
    query_t = query_t.at[query_places[:, None], :, frame_ids[None, :]].get(mode="promise_in_bounds")
    query_t = query_t.transpose(0, 2, 1, 3).reshape(HEADS, head_dim, lat_rows)
    keyval_ab = grid.gather_ab(keyval_z)
    early = (mixed_z, hidden_media, hidden_own, query_t, feed_got)
    keyval_parts = aligned_parts(grid.gather_core(keyval_ab, *early))
    mixed_z = after(mixed_z, keyval_ab)
    folded, media_scores, own_scores, context_parts = attend(
        order, is_valid, query_t, hidden_media, hidden_own, keyval_parts, factor
    )
    context_parts = context_parts.reshape(HEADS, seq_here, grid.frame, own_rows, LANES)
    pieces = [context_parts[:, :, k].reshape(HEADS, rows, LANES).astype(BF) for k in range(grid.frame)]
    pieces = [pieces[0]] + [grid.to_frame(pieces[k], k) for k in range(1, grid.frame)]
    feed_got = lax.all_to_all(after(feed_got, folded), "seq", 0, 0)
    mixed_ab = grid.gather_ab(mixed_z, folded)
    mixed_parts = grid.gather_core(mixed_ab, pieces)
    if aligned:
        output_parts, grad_parts = mixed_parts, mixed_parts
    else:
        output_parts = aligned_parts([p[:, :part] for p in mixed_parts])
        grad_parts = [p[:, part:] for p in mixed_parts]
    mixed, normed_feed, hidden_feed, context, context_low = mixer(
        order, lat_own, feed_scale, pieces, output_parts, head_dim
    )

    up_t, down_w = unpack_feed(feed_got)
    feed_parts = grid.gather_core(grid.gather_ab(grid.gather(after(hidden_feed, feed_got)[None], "z"), up_t))
    half = len(feed_parts) // 2
    far, near = (feed_parts[half:], grad_parts[half:]), (feed_parts[:half], grad_parts[:half])
    far_act, far_grad_up, low, high = feed(up_t, down_w, *far, 2)
    grad_sum = Scatter(grid, low, high)
    near_act, near_grad_up, keep = feed(up_t, down_w, *after(near, high), 1)
    grad_sum.keep(keep)
    grad_sum.to_b()
    spare = part if aligned else 0
    far_up, far_down, low, high = feed_rest(down_w, far_act, after(far_grad_up, keep), *far, spare, 2)
    near_up, near_down, keep = feed_rest(down_w, near_act, after(near_grad_up, high), *near, spare, 1)
    grad_sum.to_a(high)
    grad_sum.to_z(keep)
    back = pack_back(grid.seq, far_up, far_down, near_up, near_down)
    grad_feed = after(grad_sum.result(), back)
    message, grad_mixed, grad_mixed_low, feed_gain_part, residual = unmix(
        order, grad_feed, grad_out, mixed, normed_feed, feed_scale, context, output_parts, head_dim, own_rows
    )
    messages = [message] + [grid.to_frame(message, k) for k in range(1, grid.frame)]
    back = lax.all_to_all(after(back, message), "seq", 0, 0)
    output_context = after(context_low, messages)
    if aligned:
        keep, low, high = output_part_of(place, output_context, grad_mixed_low, keep, low, high)
    else:
        pairs = zip((keep, low, high), scatter_order(output_part_of(place, output_context, grad_mixed_low)))
        keep, low, high = (jnp.concatenate(pair, 1) for pair in pairs)
    mixed_sum = Scatter(grid, low, high)
    mixed_sum.keep(keep)
    messages = after(messages, keep)

    def back_heads(first, count, work, *parts):
        *parts, query_part, grad_media, grad_own = attend_back(
            order, place, slot.reshape(1), query_t, hidden_media, hidden_own, messages, folded, media_scores, own_scores,
            keyval_parts, factor, first, count, work, *parts,
        )
        return parts, (query_part, grad_media, grad_own)

    quarter = HEADS // 4
    parts, sums = back_heads(0, quarter, 2e9)
    parts = after(parts, mixed_sum.high, mixed_sum.arrays)
    mixed_sum.to_b(parts, back)
    parts, more = back_heads(quarter, 2 * quarter, 40e9, *parts)
    sums = [sums, more]
    parts = after(parts, mixed_sum.last())
    mixed_sum.to_a(parts)
    parts, more = back_heads(3 * quarter, quarter, 30e9, *parts)
    sums.append(more)
    query_part = sums[0][0] + sums[1][0] + sums[2][0]
    if not aligned:
        query_part = query_part.reshape(grid.count, part, lat_rows).at[owners].get(mode="promise_in_bounds")
    query_keep, low, high = jnp.split(after(query_part, mixed_sum.last()), quarters)
    query_sum = Scatter(grid, low, high)
    query_sum.keep(query_keep)
    keep, low, high = scatter_order(parts)
    keyval_sum = Scatter(grid, low, high, query_sum.high)
    keyval_sum.keep(keep)
    query_sum.to_b()
    keyval_sum.to_b(query_sum.last())
    query_sum.to_a()
    keyval_b = keyval_sum.last()
    query_sum.to_z(keyval_sum.arrays[0])
    query_sum = query_sum.result().T.astype(BF)
    mixed_sum.to_z(keyval_sum.high)
    sums = after(sums, keyval_sum.high)
    grad_hidden, grad_hidden_own = (sums[0][i] + sums[1][i] + sums[2][i] for i in (1, 2))
    back = after(back, keyval_b)

    media_gain_part = jnp.sum(grad_hidden * normed_media, (0, 1))
    grad_embedded = norm_back(grad_hidden * media_scale, normed_media, inv_media)
    table_part = jnp.dot(onehot.T, jnp.sum(grad_embedded, 1), precision=HIGHEST)

    query_grad = mm_tn(hidden_lat, query_sum)
    grad_lat = mm_nt(query_sum, query_weight)
    grad_lat = grad_lat + lax.dynamic_update_slice_in_dim(jnp.zeros_like(grad_lat), grad_hidden_own, first_row, 0)
    latent_gain_part = jnp.sum(grad_lat * normed_lat, 0)
    latents_part = norm_back(grad_lat * latent_scale, normed_lat, inv_lat)
    latents_part = latents_part + lax.dynamic_update_slice_in_dim(
        jnp.zeros_like(latents_part), residual, first_row, 0
    )
    smalls = jnp.concatenate(
        [
            latents_part,
            table_part,
            media_gain_part[None],
            latent_gain_part[None],
            feed_gain_part,
            jnp.zeros((pad, width), F32),
        ]
    ).astype(BF)
    keyval_sum.to_a()
    keyval_sum.to_z()
    smalls = smalls.T.reshape(grid.count, part, -1).at[grid.owners("cabz")].get(mode="promise_in_bounds")
    small_sum = grid.scatter_core_last(after(smalls, keyval_b)).T
    up_grad_t, down_grad = unpack_back(back)
    up_grad = up_grad_t.T
    keyval_grad = keyval_sum.result().T
    mixed_sums = mixed_sum.result()
    new_latents = (mixed + mixed_sums[:rows]).reshape(seq_here, own_rows, width)
    output_grad = mixed_sums[rows:]
    latents_grad = small_sum[:lat_rows]
    table_grad = small_sum[lat_rows : lat_rows + times]
    media_gain_grad, latent_gain_grad, feed_gain_grad = (small_sum[lat_rows + times + i] for i in range(3))
    return (
        new_latents,
        grad_embedded[:, None],
        latents_grad,
        table_grad,
        media_gain_grad,
        latent_gain_grad,
        feed_gain_grad,
        query_grad,
        keyval_grad,
        output_grad,
        up_grad,
        down_grad,
    )


def solution(mesh):
    grid = Grid(mesh.shape["seq"], mesh.shape["frame"])

    def run(*args):
        return local(grid, *args)

    return jax.shard_map(
        run,
        mesh=mesh,
        in_specs=(
            P("seq", "frame", None, None),
            P("seq"),
            P("seq", "frame"),
            P(None, BOTH),
            P(None, BOTH),
            P(BOTH),
            P(BOTH),
            P(BOTH),
            P(None, BOTH),
            P(None, BOTH),
            P(BOTH, None),
            P("seq", "frame"),
            P("frame", "seq"),
            P("seq", "frame", None),
        ),
        out_specs=(
            P("seq", "frame", None),
            P("seq", "frame", None, None),
            P(None, BOTH),
            P(None, BOTH),
            P(BOTH),
            P(BOTH),
            P(BOTH),
            P(None, BOTH),
            P(None, BOTH),
            P(BOTH, None),
            P("seq", "frame"),
            P("frame", "seq"),
        ),
        check_vma=False,
    )
```
